32 devices in a mesh: section: 2 (over x), dp: 16 (over z, y, core).
Axes of the slice: x: 2, y: 2, z: 4, core: 2. Of those that a mesh axis runs over, the one named last changes fastest.
Arguments:
- hidden_in: bfloat16 [2, 16, 512, 768], P(None, 'dp'), may hold values from -6 to 6
- seg_ids: int32 [2, 16, 512], P(None, 'dp'), may hold values from 0 to 3, never falling along the last dimension, each value on 1 to 256 neighbouring positions
- pair_ids: int32 [2, 64], P(None, 'dp'), may hold values from 0 to 63, as said below
- w_qkv: bfloat16 [2, 768, 2304], P('section'), may hold values from -0.21875 to 0.21875
- b_query: bfloat16 [2, 768], P('section'), may hold values from -3 to 3
- b_value: bfloat16 [2, 768], P('section'), may hold values from -3 to 3
- w_attn_out: bfloat16 [2, 768, 768], P('section'), may hold values from -0.875 to 0.875
- b_attn_out: bfloat16 [2, 768], P('section'), may hold values from -1.75 to 1.75
- ln1_gain: bfloat16 [2, 768], P('section'), may hold values from 0.5 to 1.5
- ln1_bias: bfloat16 [2, 768], P('section'), may hold values from -1.75 to 1.75
- w_in: bfloat16 [2, 768, 3072], P('section'), may hold values from -0.21875 to 0.21875
- b_in: bfloat16 [2, 3072], P('section'), may hold values from -3 to 3
- w_out: bfloat16 [2, 3072, 768], P('section'), may hold values from -0.109375 to 0.109375
- b_out: bfloat16 [2, 768], P('section'), may hold values from -1.75 to 1.75
- ln2_gain: bfloat16 [2, 768], P('section'), may hold values from 0.5 to 1.5
- ln2_bias: bfloat16 [2, 768], P('section'), may hold values from -0.625 to 0.625
Outputs:
- pooled: float32 [2, 64, 768], P(None, 'dp', 'section')
- seg_loss: float32 [2, 64], P(None, 'dp')
- grad_input: float32 [2, 16, 512, 768], P(None, 'dp', None, 'section')
- grad_w_qkv: float32 [2, 768, 2304], P('section', 'dp')
- grad_b_query: float32 [2, 768], P('section', 'dp')
- grad_b_value: float32 [2, 768], P('section', 'dp')
- grad_w_attn_out: float32 [2, 768, 768], P('section', 'dp')
- grad_b_attn_out: float32 [2, 768], P('section', 'dp')
- grad_ln1_gain: float32 [2, 768], P('section', 'dp')
- grad_ln1_bias: float32 [2, 768], P('section', 'dp')
- grad_w_in: float32 [2, 768, 3072], P('section', 'dp')
- grad_b_in: float32 [2, 3072], P('section', 'dp')
- grad_w_out: float32 [2, 3072, 768], P('section', 'dp')
- grad_b_out: float32 [2, 768], P('section', 'dp')
- grad_ln2_gain: float32 [2, 768], P('section', 'dp')
- grad_ln2_bias: float32 [2, 768], P('section', 'dp')
The draws below stay inside these ranges and needn't reach their ends.
Inputs may be any that keep to these rules, and one draw needn't show every extreme that they name: `seg_ids`: in each row the document numbers never fall and all 4 of them occur. In each micro-batch pair_ids is a permutation of the 64 documents forming one cycle; no document is its own partner.
All inputs are finite; a program needn't handle non-finite values.
Results may differ from the reference program's by a relative error of at most 0.02.
Values may be sent and summed in bfloat16 or wider, within the bound.
A program may use at most 256 MiB of HBM per device.

```python
import math
import jax
import jax.numpy as jnp
import numpy as np
from jax import lax

D = 768
HEADS = 12
HEAD_DIM = 64
FF = 3072
SEQ = 512
SEGS = 4
MICRO = 2
BATCH = 16
SEG_ALL = 64
N_SECTION = 2


def draw_pair_ids(key, part):
    key = jax.random.fold_in(key, 11)

    def one_cycle(sub_key):
        ordering = jax.random.permutation(sub_key, SEG_ALL).astype(jnp.int32)
        return jnp.zeros((SEG_ALL,), jnp.int32).at[ordering].set(jnp.roll(ordering, -1))
    return jax.vmap(one_cycle)(jax.random.split(key, MICRO))


def spiked(entries, rng, source, target, parts, factor):
    owner, partner = [(jnp.arange(entries.shape[axis_at]) // (entries.shape[axis_at] // parts)).reshape([-1 if axis == axis_at else 1 for axis in range(entries.ndim)]) for axis_at in (source, target)]
    chosen = jax.random.permutation(rng, parts)[partner]
    strong = (owner == chosen) | (owner == (partner + parts // 2) % parts)
    return jnp.where(strong, factor * entries, entries)


def shard_levels(own_key, extent, cuts, smallest, high):
    factor_of = 1.0
    for position, blocks in cuts:
        heights = jax.random.uniform(jax.random.fold_in(jax.random.fold_in(own_key, 6), position), (blocks,), jnp.float32, smallest / len(cuts), high / len(cuts))
        factor_of = factor_of * jnp.repeat(jnp.exp(heights), extent[position] // blocks).reshape((-1,) + (1,) * (len(extent) - 1 - position))
    return factor_of


def profile(amount, total, most, skew):
    weights = [(1 << 20) // math.isqrt(rank ** skew) + 1 for rank in range(2, amount + 1)]
    rest, given = total - most - (amount - 1), [1] * (amount - 1)
    while rest > 0:
        candidates = [i for i in range(amount - 1) if given[i] < most]
        whole, budget = sum([weights[i] for i in candidates]), rest
        for i in candidates:
            addition = min(most - given[i], max(1, budget * weights[i] // whole), rest)
            given[i] = given[i] + addition
            rest = rest - addition
    return np.array([most] + given)


def uneven(key, number_of, total, most, slope):
    if number_of == 2:
        one = jax.random.randint(key, (), max(1, total - most), min(most, total - 1) + 1)
        return jnp.stack([one, total - one])
    sizes = jnp.asarray(profile(number_of, total, most, slope), jnp.int32)
    couples = (number_of - 1) // 2
    source_of, receiver = sizes[1:1 + 2 * couples:2], sizes[2:2 + 2 * couples:2]
    margin = jnp.minimum(source_of - 1, most - receiver)
    passed = jax.random.randint(jax.random.fold_in(key, 1), (couples,), 0, 1 << 20) % (margin + 1)
    sizes = sizes.at[1:1 + 2 * couples:2].set(source_of - passed).at[2:2 + 2 * couples:2].set(receiver + passed)
    return sizes[jax.random.permutation(jax.random.fold_in(key, 2), number_of)]


def centred(key, shape, deviation, reach, cuts=(), held_as=jnp.bfloat16):
    level = shard_levels(key, shape, cuts, -0.22, 0.18) if cuts else 1.0
    array = jax.random.normal(key, shape, jnp.float32) * deviation * level
    return jnp.minimum(jnp.maximum(array, -reach), reach).astype(held_as)


def heavy_noise(stream_key, extent, width, reach, pieces, heavy, held_as=jnp.bfloat16):
    entries = width * jax.random.normal(stream_key, extent, jnp.float32)
    if pieces:
        entries = entries * shard_levels(stream_key, extent, pieces, -0.22, 0.18)
    return jnp.clip(spiked(entries, jax.random.fold_in(stream_key, 3), *heavy), -reach, reach).astype(held_as)


def setup_inputs(seed: int = 0) -> dict:
    splits = jax.random.split(jax.random.key(seed), 17)
    return {
        "hidden_in": heavy_noise(splits[0], (MICRO, BATCH, SEQ, D), 1.0, 6.0, ((1, 16),), (1, 3, 16, 2.0)),
        "seg_ids": jax.vmap(lambda own: jnp.searchsorted(jnp.cumsum(uneven(own, SEGS, SEQ, SEQ // 2, 1)), jnp.arange(SEQ), side="right"))(jax.random.split(splits[1], MICRO * BATCH)).reshape((MICRO, BATCH, SEQ)).astype(jnp.int32),
        "pair_ids": draw_pair_ids(jax.random.fold_in(splits[16], 71), 0),
        "w_qkv": centred(splits[3], (N_SECTION, D, 3 * D), D ** -0.5, 0.21875, ((0, 2),)),
        "b_query": centred(splits[4], (N_SECTION, D), 0.5, 3.0, ((0, 2),)),
        "b_value": centred(splits[5], (N_SECTION, D), 0.5, 3.0, ((0, 2),)),
        "w_attn_out": centred(splits[6], (N_SECTION, D, D), (D // 16) ** -0.5, 0.875, ((0, 2),)),
        "b_attn_out": centred(splits[7], (N_SECTION, D), 0.3, 1.75, ((0, 2),)),
        "ln1_gain": jnp.clip(1.0 + 0.1 * jax.random.normal(splits[8], (N_SECTION, D), jnp.float32), 0.5, 1.5).astype(jnp.bfloat16),
        "ln1_bias": centred(splits[9], (N_SECTION, D), 0.3, 1.75, ((0, 2),)),
        "w_in": centred(splits[10], (N_SECTION, D, FF), D ** -0.5, 0.21875, ((0, 2),)),
        "b_in": centred(splits[11], (N_SECTION, FF), 0.5, 3.0, ((0, 2),)),
        "w_out": centred(splits[12], (N_SECTION, FF, D), FF ** -0.5, 0.109375, ((0, 2),)),
        "b_out": centred(splits[13], (N_SECTION, D), 0.3, 1.75, ((0, 2),)),
        "ln2_gain": jnp.clip(1.0 + 0.1 * jax.random.normal(splits[14], (N_SECTION, D), jnp.float32), 0.5, 1.5).astype(jnp.bfloat16),
        "ln2_bias": centred(splits[15], (N_SECTION, D), 0.1, 0.625, ((0, 2),)),
    }


@jax.custom_vjp
def low(v):
    return lax.optimization_barrier(v.astype(jnp.bfloat16)).astype(jnp.float32)

@jax.custom_vjp
def low_back(v):
    return v

def low_keep(v):
    return (low(v), None)

def low_pass(kept, grad):
    return (grad,)

def back_keep(v):
    return (v, None)

def back_low(kept, grad):
    return (low(grad),)
low.defvjp(low_keep, low_pass)
low_back.defvjp(back_keep, back_low)
MASK_FILL = 1000000000.0
NORM_EPS = 1e-12
UNIT_EPS = 1e-06
TEMPER = 20.0
HIGHEST = lax.Precision.HIGHEST

def matmul(left, right):
    return jnp.dot(left, right, precision=HIGHEST, preferred_element_type=jnp.float32)

def layer_norm(row_values, gain, shift):
    centre = row_values - lax.optimization_barrier(jnp.mean(row_values, axis=-1, keepdims=True))
    scaling = lax.rsqrt(lax.optimization_barrier(jnp.mean(centre * centre, axis=-1, keepdims=True)) + NORM_EPS)
    return centre * scaling * gain + shift

def attend_row(row_items):
    queries, key_rows, values, segments = row_items
    head_shape = (SEQ, HEADS, HEAD_DIM)
    raw_scores = jnp.einsum('qhd,khd->hqk', queries.reshape(head_shape), key_rows.reshape(head_shape), precision=HIGHEST, preferred_element_type=jnp.float32) * HEAD_DIM ** (-0.5)
    scores = low_back(raw_scores)
    same_segment = segments[:, None] == segments[None, :]
    scores = jnp.where(same_segment[None], scores, -MASK_FILL)
    exponent = jnp.exp(scores - lax.optimization_barrier(jnp.max(scores, axis=-1, keepdims=True)))
    weights_low = low(exponent / lax.optimization_barrier(jnp.sum(exponent, axis=-1, keepdims=True)))
    context = jnp.einsum('hqk,khd->qhd', weights_low, values.reshape(head_shape), precision=HIGHEST, preferred_element_type=jnp.float32)
    return context.reshape(SEQ, D)

def encoder_layer(inputs, segments, weight_set):
    w_qkv, b_query, b_value, w_attn_out, b_attn_out, ln1_gain, ln1_bias, w_in, b_in, w_out, b_out, ln2_gain, ln2_bias = weight_set
    projected = matmul(inputs, w_qkv)
    queries = low(low_back(projected[:, :D] + b_query))
    key_rows = low(low_back(projected[:, D:2 * D]))
    values = low(low_back(projected[:, 2 * D:] + b_value))
    context = lax.map(jax.checkpoint(attend_row), (queries.reshape(-1, SEQ, D), key_rows.reshape(-1, SEQ, D), values.reshape(-1, SEQ, D), segments))
    context = low(low_back(context.reshape(-1, D)))
    hidden = layer_norm(inputs + low_back(matmul(context, w_attn_out) + b_attn_out), ln1_gain, ln1_bias)
    pre_act = low_back(matmul(low(hidden), w_in) + b_in)
    active = low(jax.nn.gelu(pre_act, approximate=False))
    return layer_norm(hidden + low_back(matmul(active, w_out) + b_out), ln2_gain, ln2_bias)

def contrast(outputs, segments, pairs):
    member_mask = (segments[:, :, None] == jnp.arange(SEGS)[None, None, :]).astype(jnp.float32)
    seg_sums = jnp.einsum('bsj,bsd->bjd', member_mask, outputs, precision=HIGHEST, preferred_element_type=jnp.float32)
    counts = lax.optimization_barrier(jnp.sum(member_mask, axis=1))
    pooled = (seg_sums / counts[:, :, None]).reshape(SEG_ALL, D)
    unit_rows = low(pooled * lax.rsqrt(lax.optimization_barrier(jnp.sum(pooled * pooled, axis=-1, keepdims=True)) + UNIT_EPS))
    logits = low_back(TEMPER * matmul(unit_rows, unit_rows.T))
    columns = jnp.arange(SEG_ALL)
    logits = jnp.where(columns[:, None] == columns[None, :], -MASK_FILL, logits)
    peak_value = lax.optimization_barrier(jnp.max(logits, axis=-1, keepdims=True))
    log_totals = peak_value[:, 0] + jnp.log(lax.optimization_barrier(jnp.sum(jnp.exp(logits - peak_value), axis=-1)))
    chosen = lax.optimization_barrier(jnp.sum(jnp.where(columns[None, :] == pairs[:, None], logits, 0.0), axis=-1))
    return (pooled, log_totals - chosen)

def reference(hidden_in, seg_ids, pair_ids, w_qkv, b_query, b_value, w_attn_out, b_attn_out, ln1_gain, ln1_bias, w_in, b_in, w_out, b_out, ln2_gain, ln2_bias):
    weights = tuple((weight_arg.astype(jnp.float32) for weight_arg in (w_qkv, b_query, b_value, w_attn_out, b_attn_out, ln1_gain, ln1_bias, w_in, b_in, w_out, b_out, ln2_gain, ln2_bias)))

    def forward(inputs, weight_sets):
        activations = inputs.reshape(-1, D)
        segments = seg_ids.reshape(-1, SEQ)
        for layer_index in range(N_SECTION):
            activations = encoder_layer(activations, segments, tuple((weight_set[layer_index] for weight_set in weight_sets)))
            if layer_index + 1 < N_SECTION:
                activations = low_back(low(activations))
        activations = activations.reshape(MICRO, BATCH, SEQ, D)
        pooled_list = []
        loss_list = []
        for micro_index in range(MICRO):
            pooled, seg_losses = contrast(activations[micro_index], seg_ids[micro_index], pair_ids[micro_index])
            pooled_list.append(pooled)
            loss_list.append(seg_losses)
        seg_loss = jnp.stack(loss_list)
        return (jnp.sum(seg_loss), (jnp.stack(pooled_list), seg_loss))
    total_loss, pull_back, extras = jax.vjp(forward, hidden_in.astype(jnp.float32), weights, has_aux=True)
    grad_input, weight_grads = pull_back(jnp.ones_like(total_loss))
    return (extras[0], extras[1], grad_input, weight_grads[0], weight_grads[1], weight_grads[2], weight_grads[3], weight_grads[4], weight_grads[5], weight_grads[6], weight_grads[7], weight_grads[8], weight_grads[9], weight_grads[10], weight_grads[11], weight_grads[12])
```

```python
import functools
import jax, jax.numpy as jnp
from jax import lax
from jax.experimental import pallas as pl
from jax.experimental.pallas import tpu as pltpu
from jax.sharding import PartitionSpec as P

HEADS = 12
HEAD_DIM = 64
SEGS = 4
UNIT_EPS = 1e-06
TEMPER = 20.0
MASK_FILL = 1000000000.0
NORM_EPS = 1e-12
BF = jnp.bfloat16
F32 = jnp.float32
VMEM_LIMIT = 60 * 2**20
MESH = pl.DeviceIdType.MESH
ANY = pl.BlockSpec(memory_space=pl.ANY)
VM = pl.BlockSpec(memory_space=pltpu.VMEM)


def dot(a, b):
    return jnp.dot(a, b, preferred_element_type=F32)


def dot_nt(a, b):
    return lax.dot_general(a, b, (((1,), (1,)), ((), ())), preferred_element_type=F32)


def dot_tn(a, b):
    return lax.dot_general(a, b, (((0,), (0,)), ((), ())), preferred_element_type=F32)


def split3(v):
    hi = v.astype(BF)
    rest = v - hi.astype(F32)
    mid = rest.astype(BF)
    low = (rest - mid.astype(F32)).astype(BF)
    return hi, mid, low


def members(seg_row):
    rows = lax.broadcasted_iota(jnp.int32, (16, seg_row.shape[1]), 0)
    return jnp.where(rows == seg_row, 1.0, 0.0).astype(BF)


def normed_rows(rows):
    centre = rows - jnp.mean(rows, axis=-1, keepdims=True)
    scale = lax.rsqrt(jnp.mean(centre * centre, axis=-1, keepdims=True) + NORM_EPS)
    return centre * scale, scale


def gelu_pair(u):
    mag = jnp.abs(u)
    t = 1.0 / (1.0 + (0.3275911 * 0.7071067811865476) * mag)
    e = jnp.exp(-0.5 * (u * u))
    poly = t * (0.127414796 + t * (-0.142248368 + t * (0.7107068705 + t * (-0.7265760135 + t * 0.5307027145))))
    tail = poly * e
    cdf = jnp.where(u >= 0.0, 1.0 - tail, tail)
    return u * cdf, cdf + (u * 0.3989422804014327) * e


def fwd_kernel(tb, fc, qb,
    x_h, seg, wqkv_h, bq, bv, wat_h, bat, g1, b1, win_h, bin_, wout_h, bout, g2, b2,
    pool_o, x_o, qkv_h, lse_o, c_h, z1_h, s1_o, hb_h, gp_h, act_h, z2_h, s2_o,
    x_s, wqkv, wat, win, wout, qkv, bias, c_s, h_s, hb_s, z1_s, gp_s, act_s, z2_s, y_s, lse_s, yf,
    insem, wsem, outsem, send_sem, recv_sem):
    sec = lax.axis_index("section")
    other = {"section": 1 - sec}
    M, T, D = x_s.shape
    FF = win.shape[1]
    nb = T // tb

    ws = [pltpu.make_async_copy(a, b, wsem.at[i]) for i, (a, b) in enumerate(
        ((wqkv_h, wqkv), (wat_h, wat), (win_h, win), (wout_h, wout)))]
    ws[0].start()
    barrier = pltpu.get_barrier_semaphore()
    pl.semaphore_signal(barrier, inc=1, device_id=other, device_id_type=MESH)

    @pl.when(sec == 0)
    def _():
        for m in range(M):
            pltpu.make_async_copy(x_h.at[m], x_s.at[m], insem.at[m]).start()
    for w in ws[1:]:
        w.start()
    pl.semaphore_wait(barrier, 1)

    lane = lax.broadcasted_iota(jnp.int32, (1, 128), 1)
    low_half = lane < HEAD_DIM

    def out_copies(m):
        pairs = [(x_s, x_o), (qkv, qkv_h), (c_s, c_h), (hb_s, hb_h), (z1_s, z1_h), (act_s, act_h), (gp_s, gp_h), (z2_s, z2_h)]
        return [pltpu.make_async_copy(a.at[m], b.at[m], outsem.at[m, i]) for i, (a, b) in enumerate(pairs)]

    def handoff(m, i):
        r = pl.ds(i * tb if isinstance(i, int) else pl.multiple_of(i * tb, tb), tb)
        return pltpu.make_async_remote_copy(src_ref=y_s.at[m, r], dst_ref=x_s.at[m, r], send_sem=send_sem.at[m, i],
            recv_sem=recv_sem.at[m, i], device_id=other, device_id_type=MESH)

    def micro_step(m, _):
        outs = out_copies(m)
        mem = members(seg[pl.ds(m, 1), :])
        bias[...] = (dot_tn(mem, mem) - 1.0) * MASK_FILL

        @pl.when(sec == 0)
        def _():
            pltpu.make_async_copy(x_h.at[m], x_s.at[m], insem.at[m]).wait()

        @pl.when(sec != 0)
        def _():
            for i in range(nb):
                handoff(m, i).wait_recv()
        outs[0].start()

        @pl.when(m == 0)
        def _():
            ws[0].wait()

        def qkv_step(i, _):
            r = pl.ds(pl.multiple_of(i * tb, tb), tb)
            xi = x_s[m, r, :]
            for j, b in ((0, bq), (1, None), (2, bv)):
                cols = slice(j * D, (j + 1) * D)
                v = dot(xi, wqkv[:, cols])
                if b is not None:
                    v = v + b[...].astype(F32)
                qkv[m, r, cols] = v.astype(BF)
            return 0
        lax.fori_loop(0, nb, qkv_step, 0)
        outs[1].start()
        lse_s[...] = jnp.zeros_like(lse_s)

        def att_step(p, _):
            cols = pl.ds(pl.multiple_of(p * 128, 128), 128)
            kcols = pl.ds(pl.multiple_of(p * 128 + D, 128), 128)
            vcols = pl.ds(pl.multiple_of(p * 128 + 2 * D, 128), 128)
            k2 = qkv[m, :, kcols]
            v2 = jnp.concatenate([qkv[m, :, vcols], jnp.ones((T, 128), BF)], axis=1)
            for i in range(T // qb):
                rows = slice(i * qb, (i + 1) * qb)
                q2 = qkv[m, rows, cols] * (HEAD_DIM ** -0.5)
                halves = []
                for h in range(2):
                    pick = low_half if h == 0 else jnp.logical_not(low_half)
                    s = dot_nt(jnp.where(pick, q2, 0), k2) + bias[rows, :]
                    mx = jnp.max(s, axis=-1, keepdims=True)
                    e = jnp.exp(s - mx).astype(BF)
                    c = dot(e, v2)
                    l = c[:, 128:]
                    halves.append(c[:, :128] / l)
                    lse_s[rows, :] = jnp.where(lane == 2 * p + h, mx + jnp.log(l), lse_s[rows, :])
                c_s[m, rows, cols] = jnp.where(low_half, halves[0], halves[1]).astype(BF)
            return 0
        lax.fori_loop(0, HEADS // 2, att_step, 0)
        outs[2].start()
        lse_o[m] = jnp.transpose(lse_s[...])[:16, :]

        @pl.when(m == 0)
        def _():
            ws[1].wait()

        def proj_step(i, _):
            r = pl.ds(pl.multiple_of(i * tb, tb), tb)
            r1 = x_s[m, r, :].astype(F32) + dot(c_s[m, r, :], wat[...]) + bat[...].astype(F32)
            z, scale = normed_rows(r1)
            h = z * g1[...].astype(F32) + b1[...].astype(F32)
            h_s[r, :] = h
            hb_s[m, r, :] = h.astype(BF)
            z1_s[m, r, :] = z.astype(BF)
            s1_o[m, r, :] = scale
            return 0
        lax.fori_loop(0, nb, proj_step, 0)
        outs[3].start()
        outs[4].start()

        @pl.when(m == 0)
        def _():
            ws[2].wait()
            ws[3].wait()

        def ffn_step(i, _):
            r = pl.ds(pl.multiple_of(i * tb, tb), tb)
            hi = hb_s[m, r, :]
            acc = h_s[r, :] + bout[...].astype(F32)
            nj = FF // fc
            us = [dot(hi, win[:, :fc])]
            for j in range(nj):
                cols = slice(j * fc, (j + 1) * fc)
                if j + 1 < nj:
                    us.append(dot(hi, win[:, (j + 1) * fc:(j + 2) * fc]))
                f, gp = gelu_pair(us[j] + bin_[:, cols].astype(F32))
                f = f.astype(BF)
                act_s[m, r, cols] = f
                gp_s[m, r, cols] = gp.astype(BF)
                acc = acc + dot(f, wout[cols, :])
            z, scale = normed_rows(acc)
            y = z * g2[...].astype(F32) + b2[...].astype(F32)
            z2_s[m, r, :] = z.astype(BF)
            s2_o[m, r, :] = scale
            y_s[m, r, :] = y.astype(BF)
            yf[r, :] = y

            @pl.when(sec == 0)
            def _():
                handoff(m, i).start()
            return 0
        lax.fori_loop(0, nb, ffn_step, 0)
        for o in outs[5:]:
            o.start()
        hi, mid, low = split3(yf[...])
        pool_o[m] = (dot(mem, hi) + dot(mem, mid)) + dot(mem, low)
        return 0
    lax.fori_loop(0, M, micro_step, 0)
    for m in range(M):
        for o in out_copies(m):
            o.wait()

    @pl.when(sec == 0)
    def _():
        for m in range(M):
            for i in range(nb):
                handoff(m, i).wait_send()


def stack_fwd(x, seg, weights, tb=256, fc=768, qb=256):
    M, T, D = x.shape
    FF = weights[7].shape[1]
    sds = jax.ShapeDtypeStruct
    out_shape = (sds((M, 16, D), F32), sds((M, T, D), BF), sds((M, T, 3 * D), BF), sds((M, 16, T), F32), sds((M, T, D), BF),
        sds((M, T, D), BF), sds((M, T, 1), F32), sds((M, T, D), BF), sds((M, T, FF), BF), sds((M, T, FF), BF), sds((M, T, D), BF), sds((M, T, 1), F32))
    out_specs = (VM, ANY, ANY, VM, ANY, ANY, VM, ANY, ANY, ANY, ANY, VM)
    V = pltpu.VMEM
    S = pltpu.SemaphoreType.DMA
    nb = T // tb
    scratch = [V((M, T, D), BF), V((D, 3 * D), BF), V((D, D), BF), V((D, FF), BF), V((FF, D), BF), V((M, T, 3 * D), BF), V((T, T), F32),
        V((M, T, D), BF), V((T, D), F32), V((M, T, D), BF), V((M, T, D), BF), V((M, T, FF), BF), V((M, T, FF), BF), V((M, T, D), BF), V((M, T, D), BF),
        V((T, 128), F32), V((T, D), F32), S((M,)), S((4,)), S((M, 8)), S((M, nb)), S((M, nb))]
    in_specs = (ANY, VM, ANY, VM, VM, ANY, VM, VM, VM, ANY, VM, ANY, VM, VM, VM)
    return pl.pallas_call(functools.partial(fwd_kernel, tb, fc, qb), out_shape=out_shape, in_specs=in_specs, out_specs=out_specs,
        scratch_shapes=scratch, compiler_params=pltpu.CompilerParams(vmem_limit_bytes=VMEM_LIMIT, collective_id=0, has_side_effects=True),
        name="stack_fwd")(x, seg, *weights)


def rowsum8(v):
    return jnp.sum(v.reshape(v.shape[0] // 8, 8, v.shape[1]), axis=0)


def bwd_kernel(tb, fc, kb,
    seg, dp, lse, s1, s2, qkv_h, c_h, z1_h, gp_h, z2_h, wqkv_h, wat_h, g1, win_h, wout_h, g2,
    vec_o, dx_h, db2_h, du_h, db1_h, dqkv_h,
    dyr, wqkv, wat, win, wout, qkv, c_s, z1, gp, z2, bias, dy_s, dr1, dc, delta, du, db2, db1, dqkv, dx, dxb, vacc, bacc,
    insem, wsem, outsem, send_sem, recv_sem):
    sec = lax.axis_index("section")
    other = {"section": 1 - sec}
    M, T, D = c_s.shape
    FF = win.shape[1]
    nb = T // tb

    ws = [pltpu.make_async_copy(a, b, wsem.at[i]) for i, (a, b) in enumerate(
        ((wout_h, wout), (win_h, win), (wat_h, wat), (wqkv_h, wqkv)))]

    def in_copies(m):
        pairs = [(z2_h, z2), (gp_h, gp), (z1_h, z1), (c_h, c_s), (qkv_h, qkv)]
        return [pltpu.make_async_copy(a.at[m], b.at[m], insem.at[m, i]) for i, (a, b) in enumerate(pairs)]
    first = in_copies(0)
    first[0].start()
    ws[0].start()
    barrier = pltpu.get_barrier_semaphore()
    pl.semaphore_signal(barrier, inc=1, device_id=other, device_id_type=MESH)
    for a, b in zip(first[1:], ws[1:]):
        a.start()
        b.start()
    first[4].start()
    for m in range(1, M):
        for a in in_copies(m):
            a.start()
    vacc[...] = jnp.zeros_like(vacc)
    bacc[...] = jnp.zeros_like(bacc)
    pl.semaphore_wait(barrier, 1)

    lane = lax.broadcasted_iota(jnp.int32, (1, 128), 1)
    low_half = lane < HEAD_DIM
    indicator = jnp.where(lax.broadcasted_iota(jnp.int32, (16, D), 1) // HEAD_DIM == lax.broadcasted_iota(jnp.int32, (16, D), 0), 1.0, 0.0).astype(BF)

    def out_copies(m):
        pairs = [(db2, db2_h), (du, du_h), (db1, db1_h), (dqkv, dqkv_h), (dx, dx_h)]
        return [pltpu.make_async_copy(a.at[m], b.at[m], outsem.at[m, i]) for i, (a, b) in enumerate(pairs)]

    def handoff(m, i):
        r = pl.ds(i * tb if isinstance(i, int) else pl.multiple_of(i * tb, tb), tb)
        return pltpu.make_async_remote_copy(src_ref=dxb.at[m, r], dst_ref=dyr.at[m, r], send_sem=send_sem.at[m, i],
            recv_sem=recv_sem.at[m, i], device_id=other, device_id_type=MESH)

    def norm_pull(z, scale, gain, dy):
        g = dy * gain
        return scale * (g - jnp.mean(g, axis=-1, keepdims=True) - z * jnp.mean(g * z, axis=-1, keepdims=True))

    def micro_step(m, _):
        ins = in_copies(m)
        outs = out_copies(m)
        mem = members(seg[pl.ds(m, 1), :])
        bias[...] = (dot_tn(mem, mem) - 1.0) * MASK_FILL
        dp3 = jnp.concatenate(split3(dp[m]), axis=0)

        @pl.when(sec == 0)
        def _():
            for i in range(nb):
                handoff(m, i).wait_recv()

        @pl.when(m == 0)
        def _():
            ws[0].wait()
            ws[1].wait()
            ws[2].wait()
        for a in ins[:4]:
            a.wait()

        def tok_step(i, _):
            r = pl.ds(pl.multiple_of(i * tb, tb), tb)

            @pl.when(sec == 0)
            def _():
                dy_s[...] = dyr[m, r, :].astype(F32)

            @pl.when(sec != 0)
            def _():
                blk = members(seg[pl.ds(m, 1), r])
                dy_s[...] = dot_tn(jnp.concatenate([blk, blk, blk], axis=0), dp3)
            dy = dy_s[...]
            z = z2[m, r, :].astype(F32)
            dr2 = norm_pull(z, s2[m, r, :], g2[...].astype(F32), dy)
            vacc[0] += rowsum8(dy * z)
            vacc[1] += rowsum8(dy)
            d2 = dr2.astype(BF)
            db2[m, r, :] = d2
            vacc[2] += rowsum8(d2.astype(F32))
            dh = dr2
            nj = FF // fc
            dfs = [dot_nt(d2, wout[:fc, :])]
            for j in range(nj):
                cols = slice(j * fc, (j + 1) * fc)
                if j + 1 < nj:
                    dfs.append(dot_nt(d2, wout[(j + 1) * fc:(j + 2) * fc, :]))
                dub = (dfs[j] * gp[m, r, cols].astype(F32)).astype(BF)
                du[m, r, cols] = dub
                bacc[:, cols] += rowsum8(dub.astype(F32))
                dh = dh + dot_nt(dub, win[:, cols])
            z = z1[m, r, :].astype(F32)
            d1 = norm_pull(z, s1[m, r, :], g1[...].astype(F32), dh)
            vacc[3] += rowsum8(dh * z)
            vacc[4] += rowsum8(dh)
            dr1[r, :] = d1
            d1 = d1.astype(BF)
            db1[m, r, :] = d1
            vacc[5] += rowsum8(d1.astype(F32))
            dcb = dot_nt(d1, wat[...]).astype(BF)
            dc[r, :] = dcb
            prod = dcb.astype(F32) * c_s[m, r, :].astype(F32)
            hi = prod.astype(BF)
            low = (prod - hi.astype(F32)).astype(BF)
            delta[:, r] = dot_nt(indicator, hi) + dot_nt(indicator, low)
            return 0
        lax.fori_loop(0, nb, tok_step, 0)
        for o in outs[:3]:
            o.start()
        ins[4].wait()

        def att_step(p, _):
            cols = pl.ds(pl.multiple_of(p * 128, 128), 128)
            kcols = pl.ds(pl.multiple_of(p * 128 + D, 128), 128)
            vcols = pl.ds(pl.multiple_of(p * 128 + 2 * D, 128), 128)
            q2 = qkv[m, :, cols] * (HEAD_DIM ** -0.5)
            dc2 = dc[:, cols]
            dqt = jnp.zeros((128, T), F32)
            for i in range(T // kb):
                rows = slice(i * kb, (i + 1) * kb)
                k2 = qkv[m, rows, kcols]
                v2 = qkv[m, rows, vcols]
                dks, dvs = [], []
                for h in range(2):
                    pick = low_half if h == 0 else jnp.logical_not(low_half)
                    kh = jnp.where(pick, k2, 0)
                    vh = jnp.where(pick, v2, 0)
                    st = dot_nt(kh, q2) + bias[rows, :]
                    pt = jnp.exp(st - lse[m, pl.ds(2 * p + h, 1), :])
                    dpt = dot_nt(vh, dc2)
                    da = (pt * (dpt - delta[pl.ds(2 * p + h, 1), :])).astype(BF)
                    dvs.append(dot(pt.astype(BF), dc2))
                    dks.append(dot(da, q2))
                    dqt = dqt + dot_tn(kh, da)
                dqkv[m, rows, kcols] = jnp.where(low_half, dks[0], dks[1]).astype(BF)
                dqkv[m, rows, vcols] = jnp.where(low_half, dvs[0], dvs[1]).astype(BF)
            dqkv[m, :, cols] = (jnp.transpose(dqt) * (HEAD_DIM ** -0.5)).astype(BF)
            return 0
        lax.fori_loop(0, HEADS // 2, att_step, 0)
        outs[3].start()

        @pl.when(m == 0)
        def _():
            ws[3].wait()

        def dx_step(i, _):
            r = pl.ds(pl.multiple_of(i * tb, tb), tb)
            v = dr1[r, :] + dot_nt(dqkv[m, r, :], wqkv[...])
            dx[m, r, :] = v
            dxb[m, r, :] = v.astype(BF)
            vacc[6] += rowsum8(dqkv[m, r, :D].astype(F32))
            vacc[7] += rowsum8(dqkv[m, r, 2 * D:].astype(F32))

            @pl.when(sec != 0)
            def _():
                handoff(m, i).start()
            return 0
        lax.fori_loop(0, nb, dx_step, 0)
        outs[4].start()
        return 0
    lax.fori_loop(0, M, micro_step, 0)
    vec_o[...] = jnp.concatenate([jnp.sum(vacc[...], axis=1)]
        + [jnp.sum(bacc[:, j * D:(j + 1) * D], axis=0, keepdims=True) for j in range(FF // D)] + [jnp.zeros((4, D), F32)], axis=0)
    for m in range(M):
        for o in out_copies(m):
            o.wait()

    @pl.when(sec != 0)
    def _():
        for m in range(M):
            for i in range(nb):
                handoff(m, i).wait_send()


def stack_bwd(seg, dp, stash, weights, tb=256, fc=768, kb=256):
    qkv, lse, c, z1, s1, gp, z2, s2 = stash
    wqkv, bq, bv, wat, bat, g1, b1, win, bin_, wout, bout, g2, b2 = weights
    M, T, D = c.shape
    FF = win.shape[1]
    sds = jax.ShapeDtypeStruct
    out_shape = (sds((16, D), F32), sds((M, T, D), F32), sds((M, T, D), BF), sds((M, T, FF), BF), sds((M, T, D), BF), sds((M, T, 3 * D), BF))
    out_specs = (VM, ANY, ANY, ANY, ANY, ANY)
    V = pltpu.VMEM
    S = pltpu.SemaphoreType.DMA
    nb = T // tb
    scratch = [V((M, T, D), BF), V((D, 3 * D), BF), V((D, D), BF), V((D, FF), BF), V((FF, D), BF),
        V((M, T, 3 * D), BF), V((M, T, D), BF), V((M, T, D), BF), V((M, T, FF), BF), V((M, T, D), BF),
        V((T, T), F32), V((tb, D), F32), V((T, D), F32), V((T, D), BF), V((16, T), F32),
        V((M, T, FF), BF), V((M, T, D), BF), V((M, T, D), BF), V((M, T, 3 * D), BF), V((M, T, D), F32), V((M, T, D), BF),
        V((8, 8, D), F32), V((8, FF), F32), S((M, 5)), S((4,)), S((M, 5)), S((M, nb)), S((M, nb))]
    in_specs = (VM, VM, VM, VM, VM, ANY, ANY, ANY, ANY, ANY, ANY, ANY, VM, ANY, ANY, VM)
    return pl.pallas_call(functools.partial(bwd_kernel, tb, fc, kb), out_shape=out_shape, in_specs=in_specs, out_specs=out_specs,
        scratch_shapes=scratch, compiler_params=pltpu.CompilerParams(vmem_limit_bytes=VMEM_LIMIT, collective_id=1, has_side_effects=True),
        name="stack_bwd")(seg, dp, lse, s1, s2, qkv, c, z1, gp, z2, wqkv, wat, g1, win, wout, g2)


def contrast_head(pool, seg, pairs, all_pairs):
    M, S = pairs.shape
    D = pool.shape[-1]
    counts = jnp.sum((seg[:, :, None] == jnp.arange(SEGS)).astype(F32), axis=1)[:, :, None]
    pooled = pool[:, :SEGS] / counts
    radius = lax.rsqrt(jnp.sum(pooled * pooled, axis=-1, keepdims=True) + UNIT_EPS)
    unit = (pooled * radius).astype(BF)
    every = lax.all_gather(unit, "dp", axis=1, tiled=True)
    total = every.shape[1]
    start = lax.axis_index("dp") * S
    logits = TEMPER * jnp.einsum("mgd,mkd->mgk", every, every, preferred_element_type=F32)
    cols = jnp.arange(total)
    logits = jnp.where(cols[:, None] == cols[None, :], -MASK_FILL, logits)
    peak = jnp.max(logits, axis=-1, keepdims=True)
    exponent = jnp.exp(logits - peak)
    denom = jnp.sum(exponent, axis=-1, keepdims=True)
    target = cols[None, None, :] == all_pairs[:, :, None]
    loss = peak[..., 0] + jnp.log(denom[..., 0]) - jnp.sum(jnp.where(target, logits, 0.0), axis=-1)
    dl = (exponent / denom - target.astype(F32)).astype(BF)
    rows = lax.dynamic_slice_in_dim(dl, start, S, 1)
    columns = lax.dynamic_slice_in_dim(dl, start, S, 2)
    dn = TEMPER * (jnp.einsum("mgk,mkd->mgd", rows, every, preferred_element_type=F32)
        + jnp.einsum("mkg,mkd->mgd", columns, every, preferred_element_type=F32))
    dp = radius * dn - radius * radius * radius * jnp.sum(pooled * dn, axis=-1, keepdims=True) * pooled
    loss = lax.dynamic_slice_in_dim(loss, start, S, 1)
    return pooled, loss, jnp.pad(dp / counts, ((0, 0), (0, 16 - SEGS), (0, 0)))


def scattered(grads):
    count = lax.axis_size("dp")
    packed = jnp.concatenate([g.reshape(count, -1) for g in grads], axis=1)
    part = lax.psum_scatter(packed, "dp", scatter_dimension=0, tiled=True)[0].astype(F32)
    outs, at = [], 0
    for g in grads:
        size = g.size // count
        outs.append(part[at:at + size].reshape((1, g.shape[0] // count) + g.shape[1:]))
        at += size
    return outs


def swapped(value):
    return lax.ppermute(value, "section", [(0, 1), (1, 0)])


def local(hidden_in, seg_ids, pair_ids, w_qkv, b_query, b_value, w_attn_out, b_attn_out, ln1_gain, ln1_bias, w_in, b_in, w_out, b_out, ln2_gain, ln2_bias):
    M, _, T, D = hidden_in.shape
    sec = lax.axis_index("section")
    first = sec == 0
    seg = seg_ids[:, 0]
    weights = (w_qkv[0], b_query, b_value, w_attn_out[0], b_attn_out, ln1_gain, ln1_bias, w_in[0], b_in, w_out[0], b_out, ln2_gain, ln2_bias)
    all_pairs = lax.all_gather(pair_ids, "dp", axis=1, tiled=True)
    pool, x, qkv, lse, c, z1, s1, hb, gp, act, z2, s2 = stack_fwd(hidden_in[:, 0], seg, weights)
    pooled, loss, dp = contrast_head(pool, seg, pair_ids, all_pairs)
    vec, dx, db2, du, db1, dqkv = stack_bwd(seg, dp, (qkv, lse, c, z1, s1, gp, z2, s2), weights)
    big = [jnp.einsum("mta,mtb->ab", a, b, preferred_element_type=F32).astype(BF) for a, b in ((x, dqkv), (c, db1), (hb, du), (act, db2))]
    g_qkv, g_at, g_in, g_out = scattered(big)
    small = scattered([vec[i] for i in range(8)] + [vec[8:8 + w_in.shape[2] // D].reshape(-1)])
    gg2, gb2, gbo, gg1, gb1, gba, gbq, gbv, gbi = small
    half = D // 2
    kept = lax.dynamic_slice_in_dim(dx, sec * half, half, 2)
    sent = lax.dynamic_slice_in_dim(dx, (1 - sec) * half, half, 2).astype(BF)
    grad_input = jnp.where(first, kept, swapped(sent).astype(F32))[:, None]
    pooled_kept = lax.dynamic_slice_in_dim(pooled, sec * half, half, 2)
    pooled_sent = lax.dynamic_slice_in_dim(pooled, (1 - sec) * half, half, 2).astype(BF)
    pooled_out = jnp.where(first, swapped(pooled_sent).astype(F32), pooled_kept)
    loss_out = jnp.where(first, swapped(loss.astype(BF)).astype(F32), loss)
    return (pooled_out, loss_out, grad_input, g_qkv, gbq, gbv, g_at, gba, gg1, gb1, g_in, gbi, g_out, gbo, gg2, gb2)


def solution(mesh):
    in_specs = (
        P(None, "dp", None, None),
        P(None, "dp", None),
        P(None, "dp"),
        P("section", None, None),
        P("section", None),
        P("section", None),
        P("section", None, None),
        P("section", None),
        P("section", None),
        P("section", None),
        P("section", None, None),
        P("section", None),
        P("section", None, None),
        P("section", None),
        P("section", None),
        P("section", None),
    )
    out_specs = (
        P(None, "dp", "section"),
        P(None, "dp"),
        P(None, "dp", None, "section"),
        P("section", "dp", None),
        P("section", "dp"),
        P("section", "dp"),
        P("section", "dp", None),
        P("section", "dp"),
        P("section", "dp"),
        P("section", "dp"),
        P("section", "dp", None),
        P("section", "dp"),
        P("section", "dp", None),
        P("section", "dp"),
        P("section", "dp"),
        P("section", "dp"),
    )
    return jax.shard_map(local, mesh=mesh, in_specs=in_specs, out_specs=out_specs, check_vma=False)
```

```python
import functools
import jax, jax.numpy as jnp
from jax import lax
from jax.experimental import pallas as pl
from jax.experimental.pallas import tpu as pltpu
from jax.sharding import PartitionSpec as P

HEADS = 12
HEAD_DIM = 64
SEGS = 4
UNIT_EPS = 1e-06
TEMPER = 20.0
MASK_FILL = 1000000000.0
NORM_EPS = 1e-12
BF = jnp.bfloat16
F32 = jnp.float32
VMEM_LIMIT = 60 * 2**20
MESH = pl.DeviceIdType.MESH
ANY = pl.BlockSpec(memory_space=pl.ANY)
VM = pl.BlockSpec(memory_space=pltpu.VMEM)


def dot(a, b):
    return jnp.dot(a, b, preferred_element_type=F32)


def dot_nt(a, b):
    return lax.dot_general(a, b, (((1,), (1,)), ((), ())), preferred_element_type=F32)


def dot_tn(a, b):
    return lax.dot_general(a, b, (((0,), (0,)), ((), ())), preferred_element_type=F32)


def split3(v):
    hi = v.astype(BF)
    rest = v - hi.astype(F32)
    mid = rest.astype(BF)
    low = (rest - mid.astype(F32)).astype(BF)
    return hi, mid, low


def members(seg_row):
    rows = lax.broadcasted_iota(jnp.int32, (16, seg_row.shape[1]), 0)
    return jnp.where(rows == seg_row, 1.0, 0.0).astype(BF)


def normed_rows(rows):
    centre = rows - jnp.mean(rows, axis=-1, keepdims=True)
    scale = lax.rsqrt(jnp.mean(centre * centre, axis=-1, keepdims=True) + NORM_EPS)
    return centre * scale, scale


def gelu_pair(u):
    mag = jnp.abs(u)
    t = 1.0 / (1.0 + (0.3275911 * 0.7071067811865476) * mag)
    e = jnp.exp(-0.5 * (u * u))
    poly = t * (0.127414796 + t * (-0.142248368 + t * (0.7107068705 + t * (-0.7265760135 + t * 0.5307027145))))
    tail = poly * e
    cdf = jnp.where(u >= 0.0, 1.0 - tail, tail)
    return u * cdf, cdf + (u * 0.3989422804014327) * e


def fwd_kernel(tb, fc, qb,
    x_h, seg, wqkv_h, bq, bv, wat_h, bat, g1, b1, win_h, bin_, wout_h, bout, g2, b2,
    pool_o, x_o, qkv_h, lse_o, c_h, z1_h, s1_o, hb_h, gp_h, act_h, z2_h, s2_o,
    x_s, wqkv, wat, win, wout, qkv, bias, c_s, h_s, hb_s, z1_s, gp_s, act_s, z2_s, y_s, lse_s, yf,
    insem, wsem, outsem, send_sem, recv_sem):
    sec = lax.axis_index("section")
    other = {"section": 1 - sec}
    M, T, D = x_s.shape
    FF = win.shape[1]
    nb = T // tb

    ws = [pltpu.make_async_copy(a, b, wsem.at[i]) for i, (a, b) in enumerate(
        ((wqkv_h, wqkv), (wat_h, wat), (win_h, win), (wout_h, wout)))]
    ws[0].start()
    barrier = pltpu.get_barrier_semaphore()
    pl.semaphore_signal(barrier, inc=1, device_id=other, device_id_type=MESH)

    @pl.when(sec == 0)
    def _():
        for m in range(M):
            pltpu.make_async_copy(x_h.at[m], x_s.at[m], insem.at[m]).start()
    for w in ws[1:]:
        w.start()
    pl.semaphore_wait(barrier, 1)

    lane = lax.broadcasted_iota(jnp.int32, (1, 128), 1)
    low_half = lane < HEAD_DIM

    def out_copies(m):
        pairs = [(x_s, x_o), (qkv, qkv_h), (c_s, c_h), (hb_s, hb_h), (z1_s, z1_h), (gp_s, gp_h), (z2_s, z2_h)]
        copies = [pltpu.make_async_copy(a.at[m], b.at[m], outsem.at[m, i]) for i, (a, b) in enumerate(pairs)]
        span = pl.ds(m * T if isinstance(m, int) else pl.multiple_of(m * T, T), T)
        return copies + [pltpu.make_async_copy(act_s.at[m, :, j * D:(j + 1) * D], act_h.at[j, span], outsem.at[m, 7 + j]) for j in range(FF // D)]

    def handoff(m, i):
        r = pl.ds(i * tb if isinstance(i, int) else pl.multiple_of(i * tb, tb), tb)
        return pltpu.make_async_remote_copy(src_ref=y_s.at[m, r], dst_ref=x_s.at[m, r], send_sem=send_sem.at[m, i],
            recv_sem=recv_sem.at[m, i], device_id=other, device_id_type=MESH)

    def micro_step(m, _):
        outs = out_copies(m)
        mem = members(seg[pl.ds(m, 1), :])
        bias[...] = (dot_tn(mem, mem) - 1.0) * MASK_FILL

        @pl.when(sec == 0)
        def _():
            pltpu.make_async_copy(x_h.at[m], x_s.at[m], insem.at[m]).wait()

        @pl.when(sec != 0)
        def _():
            for i in range(nb):
                handoff(m, i).wait_recv()
        outs[0].start()

        @pl.when(m == 0)
        def _():
            ws[0].wait()

        def qkv_step(i, _):
            r = pl.ds(pl.multiple_of(i * tb, tb), tb)
            xi = x_s[m, r, :]
            for j, b in ((0, bq), (1, None), (2, bv)):
                cols = slice(j * D, (j + 1) * D)
                v = dot(xi, wqkv[:, cols])
                if b is not None:
                    v = v + b[...].astype(F32)
                qkv[m, r, cols] = v.astype(BF)
            return 0
        lax.fori_loop(0, nb, qkv_step, 0)
        outs[1].start()
        lse_s[...] = jnp.zeros_like(lse_s)

        def att_step(p, _):
            cols = pl.ds(pl.multiple_of(p * 128, 128), 128)
            kcols = pl.ds(pl.multiple_of(p * 128 + D, 128), 128)
            vcols = pl.ds(pl.multiple_of(p * 128 + 2 * D, 128), 128)
            k2 = qkv[m, :, kcols]
            v2 = jnp.concatenate([qkv[m, :, vcols], jnp.ones((T, 128), BF)], axis=1)
            for i in range(T // qb):
                rows = slice(i * qb, (i + 1) * qb)
                q2 = qkv[m, rows, cols] * (HEAD_DIM ** -0.5)
                halves = []
                for h in range(2):
                    pick = low_half if h == 0 else jnp.logical_not(low_half)
                    s = dot_nt(jnp.where(pick, q2, 0), k2) + bias[rows, :]
                    mx = jnp.max(s, axis=-1, keepdims=True)
                    e = jnp.exp(s - mx).astype(BF)
                    c = dot(e, v2)
                    l = c[:, 128:]
                    halves.append(c[:, :128] / l)
                    lse_s[rows, :] = jnp.where(lane == 2 * p + h, mx + jnp.log(l), lse_s[rows, :])
                c_s[m, rows, cols] = jnp.where(low_half, halves[0], halves[1]).astype(BF)
            return 0
        lax.fori_loop(0, HEADS // 2, att_step, 0)
        outs[2].start()
        lse_o[m] = jnp.transpose(lse_s[...])[:16, :]

        @pl.when(m == 0)
        def _():
            ws[1].wait()

        def proj_step(i, _):
            r = pl.ds(pl.multiple_of(i * tb, tb), tb)
            r1 = x_s[m, r, :].astype(F32) + dot(c_s[m, r, :], wat[...]) + bat[...].astype(F32)
            z, scale = normed_rows(r1)
            h = z * g1[...].astype(F32) + b1[...].astype(F32)
            h_s[r, :] = h
            hb_s[m, r, :] = h.astype(BF)
            z1_s[m, r, :] = z.astype(BF)
            s1_o[m, r, :] = scale
            return 0
        lax.fori_loop(0, nb, proj_step, 0)
        outs[3].start()
        outs[4].start()

        @pl.when(m == 0)
        def _():
            ws[2].wait()
            ws[3].wait()

        def ffn_step(i, _):
            r = pl.ds(pl.multiple_of(i * tb, tb), tb)
            hi = hb_s[m, r, :]
            acc = h_s[r, :] + bout[...].astype(F32)
            nj = FF // fc
            us = [dot(hi, win[:, :fc])]
            for j in range(nj):
                cols = slice(j * fc, (j + 1) * fc)
                if j + 1 < nj:
                    us.append(dot(hi, win[:, (j + 1) * fc:(j + 2) * fc]))
                f, gp = gelu_pair(us[j] + bin_[:, cols].astype(F32))
                f = f.astype(BF)
                act_s[m, r, cols] = f
                gp_s[m, r, cols] = gp.astype(BF)
                acc = acc + dot(f, wout[cols, :])
            z, scale = normed_rows(acc)
            y = z * g2[...].astype(F32) + b2[...].astype(F32)
            z2_s[m, r, :] = z.astype(BF)
            s2_o[m, r, :] = scale
            y_s[m, r, :] = y.astype(BF)
            yf[r, :] = y

            @pl.when(sec == 0)
            def _():
                handoff(m, i).start()
            return 0
        lax.fori_loop(0, nb, ffn_step, 0)
        for o in outs[5:]:
            o.start()
        hi, mid, low = split3(yf[...])
        pool_o[m] = (dot(mem, hi) + dot(mem, mid)) + dot(mem, low)
        return 0
    lax.fori_loop(0, M, micro_step, 0)
    for m in range(M):
        for o in out_copies(m):
            o.wait()

    @pl.when(sec == 0)
    def _():
        for m in range(M):
            for i in range(nb):
                handoff(m, i).wait_send()


def stack_fwd(x, seg, weights, tb=256, fc=768, qb=256):
    M, T, D = x.shape
    FF = weights[7].shape[1]
    sds = jax.ShapeDtypeStruct
    out_shape = (sds((M, 16, D), F32), sds((M, T, D), BF), sds((M, T, 3 * D), BF), sds((M, 16, T), F32), sds((M, T, D), BF),
        sds((M, T, D), BF), sds((M, T, 1), F32), sds((M, T, D), BF), sds((M, T, FF), BF), sds((FF // D, M * T, D), BF), sds((M, T, D), BF), sds((M, T, 1), F32))
    out_specs = (VM, ANY, ANY, VM, ANY, ANY, VM, ANY, ANY, ANY, ANY, VM)
    V = pltpu.VMEM
    S = pltpu.SemaphoreType.DMA
    nb = T // tb
    scratch = [V((M, T, D), BF), V((D, 3 * D), BF), V((D, D), BF), V((D, FF), BF), V((FF, D), BF), V((M, T, 3 * D), BF), V((T, T), F32),
        V((M, T, D), BF), V((T, D), F32), V((M, T, D), BF), V((M, T, D), BF), V((M, T, FF), BF), V((M, T, FF), BF), V((M, T, D), BF), V((M, T, D), BF),
        V((T, 128), F32), V((T, D), F32), S((M,)), S((4,)), S((M, 7 + FF // D)), S((M, nb)), S((M, nb))]
    in_specs = (ANY, VM, ANY, VM, VM, ANY, VM, VM, VM, ANY, VM, ANY, VM, VM, VM)
    return pl.pallas_call(functools.partial(fwd_kernel, tb, fc, qb), out_shape=out_shape, in_specs=in_specs, out_specs=out_specs,
        scratch_shapes=scratch, compiler_params=pltpu.CompilerParams(vmem_limit_bytes=VMEM_LIMIT, collective_id=0, has_side_effects=True),
        name="stack_fwd")(x, seg, *weights)


def rowsum8(v):
    return jnp.sum(v.reshape(v.shape[0] // 8, 8, v.shape[1]), axis=0)


def bwd_kernel(tb, fc, kb,
    seg, dp, lse, s1, s2, qkv_h, c_h, z1_h, gp_h, z2_h, wqkv_h, wat_h, g1, win_h, wout_h, g2,
    vec_o, dx_h, dxb_h, db2_h, du_h, db1_h, dqkv_h,
    dyr, wqkv, wat, win, wout, qkv, c_s, z1, gp, z2, bias, dy_s, dr1, dc, delta, du, db2, db1, dqkv, dx, dxb, vacc, bacc,
    insem, wsem, outsem, send_sem, recv_sem):
    sec = lax.axis_index("section")
    other = {"section": 1 - sec}
    M, T, D = c_s.shape
    FF = win.shape[1]
    nb = T // tb

    ws = [pltpu.make_async_copy(a, b, wsem.at[i]) for i, (a, b) in enumerate(
        ((wout_h, wout), (win_h, win), (wat_h, wat), (wqkv_h, wqkv)))]

    def in_copies(m):
        pairs = [(z2_h, z2), (gp_h, gp), (z1_h, z1), (c_h, c_s), (qkv_h, qkv)]
        return [pltpu.make_async_copy(a.at[m], b.at[m], insem.at[m, i]) for i, (a, b) in enumerate(pairs)]
    first = in_copies(0)
    first[0].start()
    ws[0].start()
    barrier = pltpu.get_barrier_semaphore()
    pl.semaphore_signal(barrier, inc=1, device_id=other, device_id_type=MESH)
    for a, b in zip(first[1:], ws[1:]):
        a.start()
        b.start()
    first[4].start()
    for m in range(1, M):
        for a in in_copies(m):
            a.start()
    vacc[...] = jnp.zeros_like(vacc)
    bacc[...] = jnp.zeros_like(bacc)
    pl.semaphore_wait(barrier, 1)

    lane = lax.broadcasted_iota(jnp.int32, (1, 128), 1)
    low_half = lane < HEAD_DIM
    indicator = jnp.where(lax.broadcasted_iota(jnp.int32, (16, D), 1) // HEAD_DIM == lax.broadcasted_iota(jnp.int32, (16, D), 0), 1.0, 0.0).astype(BF)

    def out_copies(m):
        pairs = [(db2, db2_h), (du, du_h), (db1, db1_h), (dqkv, dqkv_h), (dx, dx_h), (dxb, dxb_h)]
        return [pltpu.make_async_copy(a.at[m], b.at[m], outsem.at[m, i]) for i, (a, b) in enumerate(pairs)]

    def handoff(m, i):
        r = pl.ds(i * tb if isinstance(i, int) else pl.multiple_of(i * tb, tb), tb)
        return pltpu.make_async_remote_copy(src_ref=dxb.at[m, r], dst_ref=dyr.at[m, r], send_sem=send_sem.at[m, i],
            recv_sem=recv_sem.at[m, i], device_id=other, device_id_type=MESH)

    def norm_pull(z, scale, gain, dy):
        g = dy * gain
        return scale * (g - jnp.mean(g, axis=-1, keepdims=True) - z * jnp.mean(g * z, axis=-1, keepdims=True))

    def micro_step(m, _):
        ins = in_copies(m)
        outs = out_copies(m)
        mem = members(seg[pl.ds(m, 1), :])
        bias[...] = (dot_tn(mem, mem) - 1.0) * MASK_FILL
        dp3 = jnp.concatenate(split3(dp[m]), axis=0)

        @pl.when(sec == 0)
        def _():
            for i in range(nb):
                handoff(m, i).wait_recv()

        @pl.when(m == 0)
        def _():
            ws[0].wait()
            ws[1].wait()
            ws[2].wait()
        for a in ins[:4]:
            a.wait()

        def tok_step(i, _):
            r = pl.ds(pl.multiple_of(i * tb, tb), tb)

            @pl.when(sec == 0)
            def _():
                dy_s[...] = dyr[m, r, :].astype(F32)

            @pl.when(sec != 0)
            def _():
                blk = members(seg[pl.ds(m, 1), r])
                dy_s[...] = dot_tn(jnp.concatenate([blk, blk, blk], axis=0), dp3)
            dy = dy_s[...]
            z = z2[m, r, :].astype(F32)
            dr2 = norm_pull(z, s2[m, r, :], g2[...].astype(F32), dy)
            vacc[0] += rowsum8(dy * z)
            vacc[1] += rowsum8(dy)
            d2 = dr2.astype(BF)
            db2[m, r, :] = d2
            vacc[2] += rowsum8(d2.astype(F32))
            dh = dr2
            nj = FF // fc
            dfs = [dot_nt(d2, wout[:fc, :])]
            for j in range(nj):
                cols = slice(j * fc, (j + 1) * fc)
                if j + 1 < nj:
                    dfs.append(dot_nt(d2, wout[(j + 1) * fc:(j + 2) * fc, :]))
                dub = (dfs[j] * gp[m, r, cols].astype(F32)).astype(BF)
                du[m, r, cols] = dub
                bacc[:, cols] += rowsum8(dub.astype(F32))
                dh = dh + dot_nt(dub, win[:, cols])
            z = z1[m, r, :].astype(F32)
            d1 = norm_pull(z, s1[m, r, :], g1[...].astype(F32), dh)
            vacc[3] += rowsum8(dh * z)
            vacc[4] += rowsum8(dh)
            dr1[r, :] = d1
            d1 = d1.astype(BF)
            db1[m, r, :] = d1
            vacc[5] += rowsum8(d1.astype(F32))
            dcb = dot_nt(d1, wat[...]).astype(BF)
            dc[r, :] = dcb
            prod = dcb.astype(F32) * c_s[m, r, :].astype(F32)
            hi = prod.astype(BF)
            low = (prod - hi.astype(F32)).astype(BF)
            delta[:, r] = dot_nt(indicator, hi) + dot_nt(indicator, low)
            return 0
        lax.fori_loop(0, nb, tok_step, 0)
        for o in outs[:3]:
            o.start()
        ins[4].wait()

        def att_step(p, _):
            cols = pl.ds(pl.multiple_of(p * 128, 128), 128)
            kcols = pl.ds(pl.multiple_of(p * 128 + D, 128), 128)
            vcols = pl.ds(pl.multiple_of(p * 128 + 2 * D, 128), 128)
            q2 = qkv[m, :, cols] * (HEAD_DIM ** -0.5)
            dc2 = dc[:, cols]
            dqt = jnp.zeros((128, T), F32)
            for i in range(T // kb):
                rows = slice(i * kb, (i + 1) * kb)
                k2 = qkv[m, rows, kcols]
                v2 = qkv[m, rows, vcols]
                dks, dvs = [], []
                for h in range(2):
                    pick = low_half if h == 0 else jnp.logical_not(low_half)
                    kh = jnp.where(pick, k2, 0)
                    vh = jnp.where(pick, v2, 0)
                    st = dot_nt(kh, q2) + bias[rows, :]
                    pt = jnp.exp(st - lse[m, pl.ds(2 * p + h, 1), :])
                    dpt = dot_nt(vh, dc2)
                    da = (pt * (dpt - delta[pl.ds(2 * p + h, 1), :])).astype(BF)
                    dvs.append(dot(pt.astype(BF), dc2))
                    dks.append(dot(da, q2))
                    dqt = dqt + dot_tn(kh, da)
                dqkv[m, rows, kcols] = jnp.where(low_half, dks[0], dks[1]).astype(BF)
                dqkv[m, rows, vcols] = jnp.where(low_half, dvs[0], dvs[1]).astype(BF)
            dqkv[m, :, cols] = (jnp.transpose(dqt) * (HEAD_DIM ** -0.5)).astype(BF)
            return 0
        lax.fori_loop(0, HEADS // 2, att_step, 0)
        outs[3].start()

        @pl.when(m == 0)
        def _():
            ws[3].wait()

        def dx_step(i, _):
            r = pl.ds(pl.multiple_of(i * tb, tb), tb)
            v = dr1[r, :] + dot_nt(dqkv[m, r, :], wqkv[...])
            dx[m, r, :] = v
            dxb[m, r, :] = v.astype(BF)
            vacc[6] += rowsum8(dqkv[m, r, :D].astype(F32))
            vacc[7] += rowsum8(dqkv[m, r, 2 * D:].astype(F32))

            @pl.when(sec != 0)
            def _():
                handoff(m, i).start()
            return 0
        lax.fori_loop(0, nb, dx_step, 0)
        outs[4].start()
        outs[5].start()
        return 0
    lax.fori_loop(0, M, micro_step, 0)
    vec_o[...] = jnp.concatenate([jnp.sum(vacc[...], axis=1)]
        + [jnp.sum(bacc[:, j * D:(j + 1) * D], axis=0, keepdims=True) for j in range(FF // D)] + [jnp.zeros((4, D), F32)], axis=0)
    for m in range(M):
        for o in out_copies(m):
            o.wait()

    @pl.when(sec != 0)
    def _():
        for m in range(M):
            for i in range(nb):
                handoff(m, i).wait_send()


def stack_bwd(seg, dp, stash, weights, tb=256, fc=768, kb=256):
    qkv, lse, c, z1, s1, gp, z2, s2 = stash
    wqkv, bq, bv, wat, bat, g1, b1, win, bin_, wout, bout, g2, b2 = weights
    M, T, D = c.shape
    FF = win.shape[1]
    sds = jax.ShapeDtypeStruct
    out_shape = (sds((16, D), F32), sds((M, T, D), F32), sds((M, T, D), BF), sds((M, T, D), BF), sds((M, T, FF), BF), sds((M, T, D), BF), sds((M, T, 3 * D), BF))
    out_specs = (VM, ANY, ANY, ANY, ANY, ANY, ANY)
    V = pltpu.VMEM
    S = pltpu.SemaphoreType.DMA
    nb = T // tb
    scratch = [V((M, T, D), BF), V((D, 3 * D), BF), V((D, D), BF), V((D, FF), BF), V((FF, D), BF),
        V((M, T, 3 * D), BF), V((M, T, D), BF), V((M, T, D), BF), V((M, T, FF), BF), V((M, T, D), BF),
        V((T, T), F32), V((tb, D), F32), V((T, D), F32), V((T, D), BF), V((16, T), F32),
        V((M, T, FF), BF), V((M, T, D), BF), V((M, T, D), BF), V((M, T, 3 * D), BF), V((M, T, D), F32), V((M, T, D), BF),
        V((8, 8, D), F32), V((8, FF), F32), S((M, 5)), S((4,)), S((M, 6)), S((M, nb)), S((M, nb))]
    in_specs = (VM, VM, VM, VM, VM, ANY, ANY, ANY, ANY, ANY, ANY, ANY, VM, ANY, ANY, VM)
    return pl.pallas_call(functools.partial(bwd_kernel, tb, fc, kb), out_shape=out_shape, in_specs=in_specs, out_specs=out_specs,
        scratch_shapes=scratch, compiler_params=pltpu.CompilerParams(vmem_limit_bytes=VMEM_LIMIT, collective_id=1, has_side_effects=True),
        name="stack_bwd")(seg, dp, lse, s1, s2, qkv, c, z1, gp, z2, wqkv, wat, g1, win, wout, g2)


def back_kernel(tb, fc, kb,
    seg, pool, pairs, lse, s1, s2, z2_h, gp_h, z1_h, c_h, qkv_h, hb_h, x_h, act_h, wout_h, win_h, wat_h, wqkv_h, g1, g2,
    vec_o, pooled_o, loss_o, g_qkv, g_at, g_in, g_out, dx_o, dxr_o,
    dyr, wqkv, wat, win, wout, qkv, c_s, z1, gp, z2, bias, dy_s, dr1, dc, delta, db2, db1, dxb, vacc, bacc,
    msgs, dps, loss_w, dn_s, loss_s, pooled_r, loss_r, lhs, rows_s, got_a, got_b, got_c, va, vb, vc,
    insem, wsem, latesem, outsem, send_sem, recv_sem, msg_send, msg_recv, pool_sem, dx_sem, send_a, recv_a, send_b, recv_b, send_c, recv_c):
    sec = lax.axis_index("section")
    me = lax.axis_index("dp")
    peers = msgs.shape[0]
    core = lax.rem(me, 2)
    y = lax.rem(lax.div(me, 2), 2)
    z = lax.div(me, 4)
    other = {"section": 1 - sec}
    sibling = {"dp": me + 1 - 2 * core}
    across = {"dp": me + 2 - 4 * y}

    def along(d):
        return {"dp": lax.rem(z + d, 4) * 4 + lax.rem(me, 4)}

    def remote(src, dst, ss, rs, target):
        return pltpu.make_async_remote_copy(src_ref=src, dst_ref=dst, send_sem=ss, recv_sem=rs, device_id=target, device_id_type=MESH)
    M, T, D = c_s.shape
    N = M * T
    FF = gp.shape[2]
    half = D // 2
    nb = T // tb
    nj = FF // D
    chunks = got_a.shape[0]
    rows = got_a.shape[3]
    SL = M * SEGS

    wcp = [pltpu.make_async_copy(wout_h, wout, wsem.at[0])]
    wcp += [pltpu.make_async_copy(win_h.at[:, :, :, :, j * D:(j + 1) * D], win.at[j], wsem.at[1 + j]) for j in range(nj)]
    wcp += [pltpu.make_async_copy(wat_h, wat, wsem.at[1 + nj]), pltpu.make_async_copy(wqkv_h, wqkv, wsem.at[2 + nj])]

    def in_copies(m):
        pairs_of = [(z2_h, z2), (gp_h, gp), (z1_h, z1), (c_h, c_s), (qkv_h, qkv)]
        return [pltpu.make_async_copy(a.at[m], b.at[m], insem.at[m, i]) for i, (a, b) in enumerate(pairs_of)]
    first = in_copies(0)
    first[0].start()
    wcp[0].start()
    hb_copy = pltpu.make_async_copy(hb_h, rows_s, latesem.at[0])
    x_copy = pltpu.make_async_copy(x_h, rows_s, latesem.at[1])
    barrier = pltpu.get_barrier_semaphore()
    pl.semaphore_signal(barrier, inc=1, device_id=other, device_id_type=MESH)
    for d in range(1, peers):
        pl.semaphore_signal(barrier, inc=1, device_id={"dp": lax.rem(me + d, peers)}, device_id_type=MESH)
    for a in first[1:4] + wcp[1:] + first[4:]:
        a.start()
    for m in range(1, M):
        for a in in_copies(m):
            a.start()
    hb_copy.start()
    vacc[...] = jnp.zeros_like(vacc)
    bacc[...] = jnp.zeros_like(bacc)

    def msg_copy(d):
        return remote(msgs.at[me], msgs.at[me], msg_send.at[d - 1], msg_recv.at[d - 1], {"dp": lax.rem(me + d, peers)})
    pool_copy = remote(dn_s.at[pl.ds(0, SL)], pooled_r, pool_sem.at[0], pool_sem.at[1], other)
    loss_copy = remote(loss_s, loss_r, pool_sem.at[2], pool_sem.at[3], other)
    pl.semaphore_wait(barrier, peers)

    @pl.when(sec != 0)
    def _():
        parts, counts = [], []
        for m in range(M):
            n = jnp.sum(members(seg[m:m + 1, :]).astype(F32), axis=1, keepdims=True)[:SEGS]
            counts.append(n)
            parts.append(pool[m, :SEGS, :] / n)
        pooled = jnp.concatenate(parts, axis=0)
        counts = jnp.concatenate(counts, axis=0)
        radius = lax.rsqrt(jnp.sum(pooled * pooled, axis=-1, keepdims=True) + UNIT_EPS)
        unit = pooled * radius
        tag = jnp.broadcast_to(pairs[...].astype(F32), (SL, 128))
        msgs[me] = jnp.concatenate([jnp.concatenate([unit[:, :half], tag], axis=1), jnp.concatenate([unit[:, half:], tag], axis=1)], axis=0).astype(BF)
        for d in range(1, peers):
            msg_copy(d).start()
        dn_s[0:SL, :] = pooled
        pool_copy.start()
        for d in range(1, peers):
            msg_copy(d).wait_recv()
        G = peers * SL
        lo = msgs[:, :SL, :half].astype(F32).reshape(G, half).astype(BF)
        hi = msgs[:, SL:, :half].astype(F32).reshape(G, half).astype(BF)
        partner = msgs[:, :SL, half:].astype(F32).reshape(G, 128)
        rid = lax.broadcasted_iota(jnp.int32, (G, G), 0)
        cid = lax.broadcasted_iota(jnp.int32, (G, G), 1)
        same = lax.rem(lax.div(rid, SEGS), M) == lax.rem(lax.div(cid, SEGS), M)
        logits = TEMPER * (dot_nt(lo, lo) + dot_nt(hi, hi))
        logits = jnp.where(jnp.logical_and(same, rid != cid), logits, -MASK_FILL)
        peak = jnp.max(logits, axis=-1, keepdims=True)
        exponent = jnp.exp(logits - peak)
        denom = jnp.sum(exponent, axis=-1, keepdims=True)
        doc = (lax.div(cid, SL) * SEGS + lax.rem(cid, SEGS)).astype(F32)
        target = jnp.where(jnp.logical_and(same, doc == partner[:, :1]), 1.0, 0.0)
        loss = peak + jnp.log(denom) - jnp.sum(target * logits, axis=-1, keepdims=True)
        dl = (exponent / denom - target).astype(BF)
        own = pl.ds(pl.multiple_of(me * SL, SL), SL)
        for side, part_of in ((0, lo), (1, hi)):
            dn_s[SL:, side * half:(side + 1) * half] = TEMPER * (dot(dl, part_of) + dot_tn(dl, part_of))
        dn_s2 = dn_s[pl.ds(pl.multiple_of(SL + me * SL, SL), SL), :]
        loss_all = jnp.broadcast_to(loss, (G, 128))
        loss_w[...] = loss_all
        loss_s[...] = loss_w[own, :]
        loss_copy.start()
        dp = (radius * dn_s2 - radius * radius * radius * jnp.sum(pooled * dn_s2, axis=-1, keepdims=True) * pooled) / counts
        dps[...] = dp
        for d in range(1, peers):
            msg_copy(d).wait_send()

    lane = lax.broadcasted_iota(jnp.int32, (1, 128), 1)
    low_half = lane < HEAD_DIM
    indicator = jnp.where(lax.broadcasted_iota(jnp.int32, (16, D), 1) // HEAD_DIM == lax.broadcasted_iota(jnp.int32, (16, D), 0), 1.0, 0.0).astype(BF)

    def out_copy(m):
        return pltpu.make_async_copy(dxb.at[m], dx_o.at[m], outsem.at[m])

    def handoff(m, i):
        r = pl.ds(i * tb if isinstance(i, int) else pl.multiple_of(i * tb, tb), tb)
        return remote(dxb.at[m, r], dyr.at[m, r], send_sem.at[m, i], recv_sem.at[m, i], other)
    theirs = slice(half, D)

    def dx_copy(m):
        return remote(dxb.at[m, :, theirs], dxr_o.at[m], dx_sem.at[m, 0], dx_sem.at[m, 1], other)

    def norm_pull(zz, scale, gain, dy):
        g = dy * gain
        return scale * (g - jnp.mean(g, axis=-1, keepdims=True) - zz * jnp.mean(g * zz, axis=-1, keepdims=True))

    part = win

    def slot(k):
        return k % nj

    def copy_a(k):
        return remote(part.at[slot(k), :, :, 1 - core], got_a.at[k], send_a.at[k], recv_a.at[k], sibling)

    def copy_b(k):
        return remote(got_a.at[k, :, 1 - y], got_b.at[k], send_b.at[k], recv_b.at[k], across)

    def copy_c(k, d):
        return remote(got_b.at[k, lax.rem(z + d, 4)], got_c.at[k, d - 1], send_c.at[k, d - 1], recv_c.at[k, d - 1], along(d))

    def after_a(k):
        copy_a(k).wait_recv()
        got_a[k] = (got_a[k].astype(F32) + part[slot(k), :, :, core].astype(F32)).astype(BF)
        copy_b(k).start()
        copy_a(k).wait_send()

    def after_b(k):
        copy_b(k).wait_recv()
        got_b[k] = (got_b[k].astype(F32) + got_a[k, :, y].astype(F32)).astype(BF)
        for d in (1, 2, 3):
            copy_c(k, d).start()

    def after_c(k):
        for d in (1, 2, 3):
            copy_c(k, d).wait_recv()
        return (got_b[k, z].astype(F32) + got_c[k, 0].astype(F32)) + (got_c[k, 1].astype(F32) + got_c[k, 2].astype(F32))

    def act_copy(t):
        return pltpu.make_async_copy(act_h.at[t], wout.at[pl.ds((t % 3) * N, N)], latesem.at[2 + t])

    def tile_out(k, v):
        part[slot(k)] = v.astype(BF).reshape(part.shape[1:])
        copy_a(k).start()

    def products_one():
        lhs[...] = jnp.transpose(rows_s[...])
        x_copy.start()
        for j in range(nj):
            du = gp[:, :, j * D:(j + 1) * D].reshape(N, D)
            tile_out(j, dot(lhs[...], du))
            if j:
                after_a(j - 1)
        after_a(nj - 1)
        for t in range(nj):
            act_copy(t).wait()
            base = (t % 3) * N
            tile = dot_tn(wout[base:base + N, :], db2[...].reshape(N, D)).astype(BF)
            for q in range(4):
                for s in range(4):
                    part[s, t, q // 2, q % 2] = tile[(q * 4 + s) * rows:(q * 4 + s + 1) * rows]
            if t == 0:
                act_copy(3).start()
            if t == 1:
                after_b(0)
        for s in range(4):
            copy_a(nj + s).start()
        for s in range(4):
            after_a(nj + s)
        after_b(1)
        tile_out(2 * nj, dot_tn(c_s[...].reshape(N, D), db1[...].reshape(N, D)))

    for m in range(M):
        last = m == M - 1
        ins = in_copies(m)
        mem = members(seg[m:m + 1, :])
        bias[...] = (dot_tn(mem, mem) - 1.0) * MASK_FILL

        @pl.when(sec == 0)
        def _():
            for i in range(nb):
                handoff(m, i).wait_recv()
        if m == 0:
            for w in wcp[:2 + nj]:
                w.wait()
        for a in ins[:4]:
            a.wait()
        if last:
            hb_copy.wait()

        def tok_step(i, _):
            r = pl.ds(pl.multiple_of(i * tb, tb), tb)

            @pl.when(sec == 0)
            def _():
                dy_s[...] = dyr[m, r, :].astype(F32)

            @pl.when(sec != 0)
            def _():
                blk = members(seg[m:m + 1, r])
                dp3 = jnp.concatenate(split3(jnp.concatenate([dps[m * SEGS:(m + 1) * SEGS, :], jnp.zeros((16 - SEGS, D), F32)], axis=0)), axis=0)
                dy_s[...] = dot_tn(jnp.concatenate([blk, blk, blk], axis=0), dp3)
            dy = dy_s[...]
            zz = z2[m, r, :].astype(F32)
            dr2 = norm_pull(zz, s2[m, r, :], g2[...].astype(F32), dy)
            vacc[0] += rowsum8(dy * zz)
            vacc[1] += rowsum8(dy)
            d2 = dr2.astype(BF)
            db2[m, r, :] = d2
            vacc[2] += rowsum8(d2.astype(F32))
            dh = dr2
            dfs = [dot_nt(d2, wout[:D, :])]
            for j in range(nj):
                cols = slice(j * D, (j + 1) * D)
                if j + 1 < nj:
                    dfs.append(dot_nt(d2, wout[(j + 1) * D:(j + 2) * D, :]))
                dub = (dfs[j] * gp[m, r, cols].astype(F32)).astype(BF)
                gp[m, r, cols] = dub
                bacc[:, cols] += rowsum8(dub.astype(F32))
                dh = dh + dot_nt(dub, win[j].reshape(D, D))
            zz = z1[m, r, :].astype(F32)
            d1 = norm_pull(zz, s1[m, r, :], g1[...].astype(F32), dh)
            vacc[3] += rowsum8(dh * zz)
            vacc[4] += rowsum8(dh)
            dr1[r, :] = d1
            d1 = d1.astype(BF)
            db1[m, r, :] = d1
            vacc[5] += rowsum8(d1.astype(F32))
            dcb = dot_nt(d1, wat[...]).astype(BF)
            dc[r, :] = dcb
            prod = dcb.astype(F32) * c_s[m, r, :].astype(F32)
            hi = prod.astype(BF)
            low = (prod - hi.astype(F32)).astype(BF)
            delta[:, r] = dot_nt(indicator, hi) + dot_nt(indicator, low)
            return 0
        lax.fori_loop(0, nb, tok_step, 0)
        ins[4].wait()
        if last:
            for t in range(3):
                act_copy(t).start()

            @pl.when(sec == 0)
            def _():
                products_one()

        def att_step(p, _):
            cols = pl.ds(pl.multiple_of(p * 128, 128), 128)
            kcols = pl.ds(pl.multiple_of(p * 128 + D, 128), 128)
            vcols = pl.ds(pl.multiple_of(p * 128 + 2 * D, 128), 128)
            q2 = qkv[m, :, cols] * (HEAD_DIM ** -0.5)
            dc2 = dc[:, cols]
            dqt = jnp.zeros((128, T), F32)
            for i in range(T // kb):
                r = slice(i * kb, (i + 1) * kb)
                k2 = qkv[m, r, kcols]
                v2 = qkv[m, r, vcols]
                dks, dvs = [], []
                for h in range(2):
                    pick = low_half if h == 0 else jnp.logical_not(low_half)
                    kh = jnp.where(pick, k2, 0)
                    vh = jnp.where(pick, v2, 0)
                    st = dot_nt(kh, q2) + bias[r, :]
                    pt = jnp.exp(st - lse[m, pl.ds(2 * p + h, 1), :])
                    dpt = dot_nt(vh, dc2)
                    da = (pt * (dpt - delta[pl.ds(2 * p + h, 1), :])).astype(BF)
                    dvs.append(dot(pt.astype(BF), dc2))
                    dks.append(dot(da, q2))
                    dqt = dqt + dot_tn(kh, da)
                qkv[m, r, kcols] = jnp.where(low_half, dks[0], dks[1]).astype(BF)
                qkv[m, r, vcols] = jnp.where(low_half, dvs[0], dvs[1]).astype(BF)
            qkv[m, :, cols] = (jnp.transpose(dqt) * (HEAD_DIM ** -0.5)).astype(BF)
            if last:
                for at, k in ((1, 2), (3, 3), (5, 4)):
                    @pl.when(jnp.logical_and(sec == 0, p == at))
                    def _():
                        after_b(k)
            return 0
        lax.fori_loop(0, HEADS // 2, att_step, 0)
        if m == 0:
            wcp[2 + nj].wait()

        def dx_step(i, _):
            r = pl.ds(pl.multiple_of(i * tb, tb), tb)
            v = dr1[r, :] + dot_nt(qkv[m, r, :], wqkv[...])
            dxb[m, r, :] = v.astype(BF)
            vacc[6] += rowsum8(qkv[m, r, :D].astype(F32))
            vacc[7] += rowsum8(qkv[m, r, 2 * D:].astype(F32))

            @pl.when(sec != 0)
            def _():
                handoff(m, i).start()
            return 0
        lax.fori_loop(0, nb, dx_step, 0)
        out_copy(m).start()

        @pl.when(sec == 0)
        def _():
            dx_copy(m).start()

    @pl.when(sec == 0)
    def _():
        after_b(5)

    @pl.when(sec != 0)
    def _():
        products_one()
        for k in range(2, 6):
            after_b(k)
    nk = chunks
    va[...] = jnp.concatenate([jnp.sum(vacc[...], axis=1)]
        + [jnp.sum(bacc[:, j * D:(j + 1) * D], axis=0, keepdims=True) for j in range(nj)] + [jnp.zeros((8 - nj, D), F32)], axis=0)
    vec_a = remote(va, vb.at[0], send_a.at[nk], recv_a.at[nk], sibling)
    vec_a.start()
    k = 2 * nj
    x_copy.wait()
    lhs[...] = jnp.transpose(rows_s[...])
    after_a(k)
    for j in range(3):
        tile_out(k + 1 + j, dot(lhs[...], qkv[:, :, j * D:(j + 1) * D].reshape(N, D)))
        if j:
            after_a(k + j)
    after_a(k + 3)
    vec_a.wait()
    va[...] = va[...] + vb[0]
    vec_b = remote(va, vb.at[1], send_b.at[nk], recv_b.at[nk], across)
    vec_b.start()
    after_b(6)
    after_b(7)
    vec_b.wait()
    va[...] = va[...] + vb[1]
    vec_c = [remote(va, vc.at[d - 1], send_c.at[nk, d - 1], recv_c.at[nk, d - 1], along(d)) for d in (1, 2, 3)]
    for cp in vec_c:
        cp.start()
    for j in range(4):
        g_in[:, j * D:(j + 1) * D] = after_c(j)
    after_b(8)
    g_out[0:rows, :] = after_c(4)
    g_out[rows:2 * rows, :] = after_c(5)
    after_b(9)
    for cp in vec_c:
        cp.wait()
    vec_o[...] = (va[...] + vc[0]) + (vc[1] + vc[2])
    g_out[2 * rows:3 * rows, :] = after_c(6)
    after_b(10)
    g_out[3 * rows:4 * rows, :] = after_c(7)
    after_b(11)
    g_at[...] = after_c(8)
    for j in range(3):
        g_qkv[:, j * D:(j + 1) * D] = after_c(9 + j)

    @pl.when(sec == 0)
    def _():
        pool_copy.wait_recv()
        loss_copy.wait_recv()
        pooled_o[...] = pooled_r[:, :half]
        loss_o[...] = loss_r[...]
        for m in range(M):
            dx_copy(m).wait_send()

    @pl.when(sec != 0)
    def _():
        pool_copy.wait_send()
        loss_copy.wait_send()
        pooled_o[...] = dn_s[0:SL, half:]
        loss_o[...] = loss_s[...]
        for m in range(M):
            for i in range(nb):
                handoff(m, i).wait_send()
            dx_copy(m).wait_recv()
    for m in range(M):
        out_copy(m).wait()
    for k in range(chunks):
        copy_b(k).wait_send()
        for d in (1, 2, 3):
            copy_c(k, d).wait_send()


def stack_back(seg, pool, pairs, stash, weights, tb=256, fc=768, kb=256):
    x, qkv, lse, c, z1, s1, hb, gp, act, z2, s2 = stash
    wqkv, bq, bv, wat, bat, g1, b1, win, bin_, wout, bout, g2, b2 = weights
    M, T, D = c.shape
    N = M * T
    FF = win.shape[1]
    count = lax.axis_size("dp")
    rows = D // count
    chunks = (4 * D + 2 * FF) // D
    SL = M * SEGS
    sds = jax.ShapeDtypeStruct
    out_shape = (sds((16, D), F32), sds((SL, D // 2), F32), sds((SL, 128), F32), sds((rows, 3 * D), F32), sds((rows, D), F32), sds((rows, FF), F32),
        sds((FF // count, D), F32), sds((M, T, D), BF), sds((M, T, D // 2), BF))
    out_specs = (VM,) * 7 + (ANY, ANY)
    V = pltpu.VMEM
    S = pltpu.SemaphoreType.DMA
    nb = T // tb
    split = (4, 2, 2, rows)
    nj = FF // D
    scratch = [V((M, T, D), BF), V((D, 3 * D), BF), V((D, D), BF), V((nj,) + split + (D,), BF), V((FF, D), BF),
        V((M, T, 3 * D), BF), V((M, T, D), BF), V((M, T, D), BF), V((M, T, FF), BF), V((M, T, D), BF),
        V((T, T), F32), V((tb, D), F32), V((T, D), F32), V((T, D), BF), V((16, T), F32),
        V((M, T, D), BF), V((M, T, D), BF), V((M, T, D), BF), V((8, 8, D), F32), V((8, FF), F32),
        V((count, 16, D // 2 + 128), BF), V((SL, D), F32), V((count * SL, 128), F32), V((SL + count * SL, D), F32), V((SL, 128), F32), V((SL, D), F32), V((SL, 128), F32),
        V((D, N), BF), V((N, D), BF), V((chunks, 4, 2, rows, D), BF), V((chunks, 4, rows, D), BF), V((chunks, 3, rows, D), BF),
        V((16, D), F32), V((2, 16, D), F32), V((3, 16, D), F32),
        S((M, 5)), S((3 + nj,)), S((2 + nj,)), S((M,)), S((M, nb)), S((M, nb)), S((count - 1,)), S((count - 1,)), S((4,)), S((M, 2)),
        S((chunks + 1,)), S((chunks + 1,)), S((chunks + 1,)), S((chunks + 1,)), S((chunks + 1, 3)), S((chunks + 1, 3))]
    in_specs = (VM,) * 6 + (ANY,) * 12 + (VM, VM)
    return pl.pallas_call(functools.partial(back_kernel, tb, fc, kb), out_shape=out_shape, in_specs=in_specs, out_specs=out_specs,
        scratch_shapes=scratch, compiler_params=pltpu.CompilerParams(vmem_limit_bytes=62 * 2**20, collective_id=3, has_side_effects=True),
        name="stack_back")(seg, pool, pairs, lse, s1, s2, z2, gp, z1, c, qkv, hb.reshape(N, D), x.reshape(N, D), act,
            wout, win.reshape(split + (FF,)), wat, wqkv, g1, g2)


def contrast_head(pool, seg, pairs, all_pairs):
    M, S = pairs.shape
    D = pool.shape[-1]
    counts = jnp.sum((seg[:, :, None] == jnp.arange(SEGS)).astype(F32), axis=1)[:, :, None]
    pooled = pool[:, :SEGS] / counts
    radius = lax.rsqrt(jnp.sum(pooled * pooled, axis=-1, keepdims=True) + UNIT_EPS)
    unit = (pooled * radius).astype(BF)
    every = lax.all_gather(unit, "dp", axis=1, tiled=True)
    total = every.shape[1]
    start = lax.axis_index("dp") * S
    logits = TEMPER * jnp.einsum("mgd,mkd->mgk", every, every, preferred_element_type=F32)
    cols = jnp.arange(total)
    logits = jnp.where(cols[:, None] == cols[None, :], -MASK_FILL, logits)
    peak = jnp.max(logits, axis=-1, keepdims=True)
    exponent = jnp.exp(logits - peak)
    denom = jnp.sum(exponent, axis=-1, keepdims=True)
    target = cols[None, None, :] == all_pairs[:, :, None]
    loss = peak[..., 0] + jnp.log(denom[..., 0]) - jnp.sum(jnp.where(target, logits, 0.0), axis=-1)
    dl = (exponent / denom - target.astype(F32)).astype(BF)
    rows = lax.dynamic_slice_in_dim(dl, start, S, 1)
    columns = lax.dynamic_slice_in_dim(dl, start, S, 2)
    dn = TEMPER * (jnp.einsum("mgk,mkd->mgd", rows, every, preferred_element_type=F32)
        + jnp.einsum("mkg,mkd->mgd", columns, every, preferred_element_type=F32))
    dp = radius * dn - radius * radius * radius * jnp.sum(pooled * dn, axis=-1, keepdims=True) * pooled
    loss = lax.dynamic_slice_in_dim(loss, start, S, 1)
    return pooled, loss, jnp.pad(dp / counts, ((0, 0), (0, 16 - SEGS), (0, 0)))


def scattered(grads):
    count = lax.axis_size("dp")
    packed = jnp.concatenate([g.reshape(count, -1) for g in grads], axis=1)
    part = lax.psum_scatter(packed, "dp", scatter_dimension=0, tiled=True)[0].astype(F32)
    outs, at = [], 0
    for g in grads:
        size = g.size // count
        outs.append(part[at:at + size].reshape((1, g.shape[0] // count) + g.shape[1:]))
        at += size
    return outs


def swapped(value):
    return lax.ppermute(value, "section", [(0, 1), (1, 0)])


def local(hidden_in, seg_ids, pair_ids, w_qkv, b_query, b_value, w_attn_out, b_attn_out, ln1_gain, ln1_bias, w_in, b_in, w_out, b_out, ln2_gain, ln2_bias):
    M, _, T, D = hidden_in.shape
    sec = lax.axis_index("section")
    first = sec == 0
    seg = seg_ids[:, 0]
    weights = (w_qkv[0], b_query, b_value, w_attn_out[0], b_attn_out, ln1_gain, ln1_bias, w_in[0], b_in, w_out[0], b_out, ln2_gain, ln2_bias)
    half = D // 2
    count = lax.axis_size("dp")
    pool, x, qkv, lse, c, z1, s1, hb, gp, act, z2, s2 = stack_fwd(hidden_in[:, 0], seg, weights)
    if count == 16:
        vec, pooled, loss, g_qkv, g_at, g_in, g_out, dxb, dxr = stack_back(
            seg, pool, pair_ids.reshape(-1, 1), (x, qkv, lse, c, z1, s1, hb, gp, act, z2, s2), weights)
        pooled_out = pooled.reshape(M, SEGS, half)
        loss_out = loss[:, 0].reshape(M, SEGS)
        g_qkv, g_at, g_in, g_out = (g[None] for g in (g_qkv, g_at, g_in, g_out))
        me = lax.axis_index("dp")
        width = D // count
        small = lax.dynamic_slice_in_dim(vec[:8], me * width, width, 1)
        gg2, gb2, gbo, gg1, gb1, gba, gbq, gbv = (small[i:i + 1] for i in range(8))
        wide = w_in.shape[2] // count
        gbi = lax.dynamic_slice_in_dim(vec[8:8 + w_in.shape[2] // D].reshape(1, -1), me * wide, wide, 1)
        grad_input = jnp.where(first, dxb[:, :, :half], dxr).astype(F32)
    else:
        all_pairs = lax.all_gather(pair_ids, "dp", axis=1, tiled=True)
        pooled, loss, dp = contrast_head(pool, seg, pair_ids, all_pairs)
        vec, dx, dxb, db2, du, db1, dqkv = stack_bwd(seg, dp, (qkv, lse, c, z1, s1, gp, z2, s2), weights)
        act = jnp.moveaxis(act, 0, 1).reshape(M, T, -1)
        big = [jnp.einsum("mta,mtb->ab", a, b, preferred_element_type=F32).astype(BF) for a, b in ((x, dqkv), (c, db1), (hb, du), (act, db2))]
        g_qkv, g_at, g_in, g_out = scattered(big)
        small = scattered([vec[i] for i in range(8)] + [vec[8:8 + w_in.shape[2] // D].reshape(-1)])
        gg2, gb2, gbo, gg1, gb1, gba, gbq, gbv, gbi = small
        kept = lax.dynamic_slice_in_dim(dx, sec * half, half, 2)
        sent = lax.dynamic_slice_in_dim(dxb, (1 - sec) * half, half, 2)
        grad_input = jnp.where(first, kept, swapped(sent).astype(F32))
        pooled_kept = lax.dynamic_slice_in_dim(pooled, sec * half, half, 2)
        pooled_sent = lax.dynamic_slice_in_dim(pooled, (1 - sec) * half, half, 2).astype(BF)
        pooled_out = jnp.where(first, swapped(pooled_sent).astype(F32), pooled_kept)
        loss_out = jnp.where(first, swapped(loss.astype(BF)).astype(F32), loss)
    return (pooled_out, loss_out, grad_input[:, None], g_qkv, gbq, gbv, g_at, gba, gg1, gb1, g_in, gbi, g_out, gbo, gg2, gb2)


def solution(mesh):
    in_specs = (
        P(None, "dp", None, None),
        P(None, "dp", None),
        P(None, "dp"),
        P("section", None, None),
        P("section", None),
        P("section", None),
        P("section", None, None),
        P("section", None),
        P("section", None),
        P("section", None),
        P("section", None, None),
        P("section", None),
        P("section", None, None),
        P("section", None),
        P("section", None),
        P("section", None),
    )
    out_specs = (
        P(None, "dp", "section"),
        P(None, "dp"),
        P(None, "dp", None, "section"),
        P("section", "dp", None),
        P("section", "dp"),
        P("section", "dp"),
        P("section", "dp", None),
        P("section", "dp"),
        P("section", "dp"),
        P("section", "dp"),
        P("section", "dp", None),
        P("section", "dp"),
        P("section", "dp", None),
        P("section", "dp"),
        P("section", "dp"),
        P("section", "dp"),
    )
    return jax.shard_map(local, mesh=mesh, in_specs=in_specs, out_specs=out_specs, check_vma=False)
```

```python
import functools
import jax, jax.numpy as jnp
from jax import lax
from jax.experimental import pallas as pl
from jax.experimental.pallas import tpu as pltpu
from jax.sharding import PartitionSpec as P

HEADS = 12
HEAD_DIM = 64
SEGS = 4
UNIT_EPS = 1e-06
TEMPER = 20.0
MASK_FILL = 1000000000.0
NORM_EPS = 1e-12
BF = jnp.bfloat16
F32 = jnp.float32
VMEM_LIMIT = 60 * 2**20
MESH = pl.DeviceIdType.MESH
ANY = pl.BlockSpec(memory_space=pl.ANY)
VM = pl.BlockSpec(memory_space=pltpu.VMEM)


def dot(a, b):
    return jnp.dot(a, b, preferred_element_type=F32)


def dot_nt(a, b):
    return lax.dot_general(a, b, (((1,), (1,)), ((), ())), preferred_element_type=F32)


def dot_tn(a, b):
    return lax.dot_general(a, b, (((0,), (0,)), ((), ())), preferred_element_type=F32)


def split3(v):
    hi = v.astype(BF)
    rest = v - hi.astype(F32)
    mid = rest.astype(BF)
    low = (rest - mid.astype(F32)).astype(BF)
    return hi, mid, low


def members(seg_row):
    rows = lax.broadcasted_iota(jnp.int32, (16, seg_row.shape[1]), 0)
    return jnp.where(rows == seg_row, 1.0, 0.0).astype(BF)


def normed_rows(rows):
    centre = rows - jnp.mean(rows, axis=-1, keepdims=True)
    scale = lax.rsqrt(jnp.mean(centre * centre, axis=-1, keepdims=True) + NORM_EPS)
    return centre * scale, scale


def gelu_pair(u):
    mag = jnp.abs(u)
    t = 1.0 / (1.0 + (0.3275911 * 0.7071067811865476) * mag)
    e = jnp.exp(-0.5 * (u * u))
    poly = t * (0.127414796 + t * (-0.142248368 + t * (0.7107068705 + t * (-0.7265760135 + t * 0.5307027145))))
    tail = poly * e
    cdf = jnp.where(u >= 0.0, 1.0 - tail, tail)
    return u * cdf, cdf + (u * 0.3989422804014327) * e


def codes(mem):
    lanes = lax.rem(lax.broadcasted_iota(jnp.int32, (16, 128), 1), HEAD_DIM)
    pick = jnp.where(lanes == lax.broadcasted_iota(jnp.int32, (16, 128), 0), 1.0, 0.0)
    pick = jnp.where(lanes < SEGS, pick, 0.0).astype(BF)
    key_code = dot_tn(mem, pick)
    active = jnp.where(lanes[:1] < SEGS, 1.0, 0.0)
    return key_code.astype(BF), ((key_code - active) * MASK_FILL).astype(BF)


def fwd_kernel(tb, fc,
    x_h, seg, wqkv_h, bq, bv, wat_h, bat, g1, b1, win_h, bin_, wout_h, bout, g2, b2,
    pool_o, x_o, qkv_h, lse_o, c_h, z1_h, s12_o, hb_h, gp_h, act_h, z2_h,
    x_s, wqkv, wat, win, wout, qkv, c_s, hb_s, z1_s, gp_s, act_s, z2_s, y_s, yf,
    insem, wsem, outsem, send_sem, recv_sem):
    sec = lax.axis_index("section")
    other = {"section": 1 - sec}
    M, T, D = x_s.shape
    FF = win.shape[1]
    nb = T // tb

    ws = [pltpu.make_async_copy(a, b, wsem.at[i]) for i, (a, b) in enumerate(
        ((wqkv_h, wqkv), (wat_h, wat), (win_h, win), (wout_h, wout)))]
    barrier = pltpu.get_barrier_semaphore()

    @pl.when(sec == 0)
    def _():
        pltpu.make_async_copy(x_h.at[0], x_s.at[0], insem.at[0]).start()
    ws[0].start()
    pl.semaphore_signal(barrier, inc=1, device_id=other, device_id_type=MESH)
    for w in ws[1:]:
        w.start()

    @pl.when(sec == 0)
    def _():
        for m in range(1, M):
            pltpu.make_async_copy(x_h.at[m], x_s.at[m], insem.at[m]).start()

    lane = lax.broadcasted_iota(jnp.int32, (1, 128), 1)
    low_half = lane < HEAD_DIM

    def out_copies(m, i):
        r = pl.ds(i * tb, tb)
        span = pl.ds(m * T + i * tb if isinstance(m, int) else pl.multiple_of(m * T + i * tb, tb), tb)
        pairs = [(a.at[m, r], b.at[m, r]) for a, b in ((c_s, c_h), (hb_s, hb_h), (z1_s, z1_h), (z2_s, z2_h), (gp_s, gp_h))]
        pairs += [(act_s.at[m, r, j * D:(j + 1) * D], act_h.at[j, span]) for j in range(FF // D)]
        return [pltpu.make_async_copy(a, b, outsem.at[m, i, j]) for j, (a, b) in enumerate(pairs)]

    def whole_copies(m):
        return [pltpu.make_async_copy(a.at[m], b.at[m], outsem.at[m, nb, j]) for j, (a, b) in enumerate(((x_s, x_o), (qkv, qkv_h)))]

    def handoff(m, i):
        r = pl.ds(i * tb, tb)
        return pltpu.make_async_remote_copy(src_ref=y_s.at[m, r], dst_ref=x_s.at[m, r], send_sem=send_sem.at[m, i],
            recv_sem=recv_sem.at[m, i], device_id=other, device_id_type=MESH)

    def micro_step(m, _):
        mem = members(seg[pl.ds(m, 1), :])
        key_code, query_code = codes(mem)

        @pl.when(sec == 0)
        def _():
            pltpu.make_async_copy(x_h.at[m], x_s.at[m], insem.at[m]).wait()

        @pl.when(m == 0)
        def _():
            ws[0].wait()

        @pl.when(sec != 0)
        def _():
            for i in range(nb):
                handoff(m, i).wait_recv()
        xi = x_s[m]
        for j, b in ((0, bq), (1, None), (2, bv)):
            cols = slice(j * D, (j + 1) * D)
            v = dot(xi, wqkv[:, cols])
            if b is not None:
                v = v + b[...].astype(F32)
            qkv[m, :, cols] = v.astype(BF)
        for cp in whole_copies(m):
            cp.start()
        ones = jnp.ones((T, 128), BF)
        for i in range(nb):
            r = slice(i * tb, (i + 1) * tb)
            lses = jnp.zeros((tb, 128), F32)
            for p in range(HEADS // 2):
                cols = slice(p * 128, (p + 1) * 128)
                k2 = qkv[m, :, D + p * 128:D + (p + 1) * 128]
                v2 = jnp.concatenate([qkv[m, :, 2 * D + p * 128:2 * D + (p + 1) * 128], ones], axis=1)
                q2 = qkv[m, r, cols] * (HEAD_DIM ** -0.5)
                qc = query_code[r]
                halves = []
                for h in range(2):
                    if h == 0:
                        s = dot_nt(jnp.where(low_half, q2, qc), jnp.where(low_half, k2, key_code))
                    else:
                        s = dot_nt(jnp.where(low_half, qc, q2), jnp.where(low_half, key_code, k2))
                    mx = jnp.max(s, axis=-1, keepdims=True)
                    e = jnp.exp(s - mx).astype(BF)
                    c = dot(e, v2)
                    l = c[:, 128:]
                    halves.append(c[:, :128] / l)
                    lses = jnp.where(lane == 2 * p + h, mx + jnp.log(l), lses)
                c_s[m, r, cols] = jnp.where(low_half, halves[0], halves[1]).astype(BF)
            lse_o[m, :, r] = jnp.transpose(lses)[:16, :]
            if i == 0:
                @pl.when(m == 0)
                def _():
                    for w in ws[1:]:
                        w.wait()
                    pl.semaphore_wait(barrier, 1)
            r1 = x_s[m, r, :].astype(F32) + dot(c_s[m, r, :], wat[...]) + bat[...].astype(F32)
            z, scale = normed_rows(r1)
            acc = z * g1[...].astype(F32) + b1[...].astype(F32)
            hi = acc.astype(BF)
            hb_s[m, r, :] = hi
            z1_s[m, r, :] = z.astype(BF)
            s12_o[m, r, 0:1] = scale
            acc = acc + bout[...].astype(F32)
            nj = FF // fc
            us = [dot(hi, win[:, :fc])]
            for j in range(nj):
                cols = slice(j * fc, (j + 1) * fc)
                if j + 1 < nj:
                    us.append(dot(hi, win[:, (j + 1) * fc:(j + 2) * fc]))
                f, gp = gelu_pair(us[j] + bin_[:, cols].astype(F32))
                f = f.astype(BF)
                act_s[m, r, cols] = f
                gp_s[m, r, cols] = gp.astype(BF)
                acc = acc + dot(f, wout[cols, :])
            z, scale = normed_rows(acc)
            y = z * g2[...].astype(F32) + b2[...].astype(F32)
            y_s[m, r, :] = y.astype(BF)

            @pl.when(sec == 0)
            def _():
                handoff(m, i).start()
            z2_s[m, r, :] = z.astype(BF)
            s12_o[m, r, 1:2] = scale
            yf[r, :] = y
            for cp in out_copies(m, i):
                cp.start()

        @pl.when(sec != 0)
        def _():
            hi, mid, low = split3(yf[...])
            pool_o[m] = (dot(mem, hi) + dot(mem, mid)) + dot(mem, low)
        return 0
    lax.fori_loop(0, M, micro_step, 0)

    @pl.when(sec == 0)
    def _():
        pool_o[...] = jnp.zeros_like(pool_o)
    for m in range(M):
        for cp in whole_copies(m):
            cp.wait()
        for i in range(nb):
            for cp in out_copies(m, i):
                cp.wait()

    @pl.when(sec == 0)
    def _():
        for m in range(M):
            for i in range(nb):
                handoff(m, i).wait_send()


def stack_fwd(x, seg, weights, tb=256, fc=768):
    M, T, D = x.shape
    FF = weights[7].shape[1]
    sds = jax.ShapeDtypeStruct
    out_shape = (sds((M, 16, D), F32), sds((M, T, D), BF), sds((M, T, 3 * D), BF), sds((M, 16, T), F32), sds((M, T, D), BF),
        sds((M, T, D), BF), sds((M, T, 2), F32), sds((M, T, D), BF), sds((M, T, FF), BF), sds((FF // D, M * T, D), BF), sds((M, T, D), BF))
    out_specs = (VM, ANY, ANY, VM, ANY, ANY, VM, ANY, ANY, ANY, ANY)
    V = pltpu.VMEM
    S = pltpu.SemaphoreType.DMA
    nb = T // tb
    scratch = [V((M, T, D), BF), V((D, 3 * D), BF), V((D, D), BF), V((D, FF), BF), V((FF, D), BF), V((M, T, 3 * D), BF),
        V((M, T, D), BF), V((M, T, D), BF), V((M, T, D), BF), V((M, T, FF), BF), V((M, T, FF), BF), V((M, T, D), BF), V((M, T, D), BF),
        V((T, D), F32), S((M,)), S((4,)), S((M, nb + 1, 5 + FF // D)), S((M, nb)), S((M, nb))]
    in_specs = (ANY, VM, ANY, VM, VM, ANY, VM, VM, VM, ANY, VM, ANY, VM, VM, VM)
    return pl.pallas_call(functools.partial(fwd_kernel, tb, fc), out_shape=out_shape, in_specs=in_specs, out_specs=out_specs,
        scratch_shapes=scratch, compiler_params=pltpu.CompilerParams(vmem_limit_bytes=VMEM_LIMIT, collective_id=0, has_side_effects=True),
        name="stack_fwd")(x, seg, *weights)


def rowsum8(v):
    return jnp.sum(v.reshape(v.shape[0] // 8, 8, v.shape[1]), axis=0)


def bwd_kernel(tb, fc, kb,
    seg, dp, lse, s12, qkv_h, c_h, z1_h, gp_h, z2_h, wqkv_h, wat_h, g1, win_h, wout_h, g2,
    vec_o, dx_h, dxb_h, db2_h, du_h, db1_h, dqkv_h,
    dyr, wqkv, wat, win, wout, qkv, c_s, z1, gp, z2, bias, dy_s, dr1, dc, delta, du, db2, db1, dqkv, dx, dxb, vacc, bacc,
    insem, wsem, outsem, send_sem, recv_sem):
    sec = lax.axis_index("section")
    other = {"section": 1 - sec}
    M, T, D = c_s.shape
    FF = win.shape[1]
    nb = T // tb

    ws = [pltpu.make_async_copy(a, b, wsem.at[i]) for i, (a, b) in enumerate(
        ((wout_h, wout), (win_h, win), (wat_h, wat), (wqkv_h, wqkv)))]

    def in_copies(m):
        pairs = [(z2_h, z2), (gp_h, gp), (z1_h, z1), (c_h, c_s), (qkv_h, qkv)]
        return [pltpu.make_async_copy(a.at[m], b.at[m], insem.at[m, i]) for i, (a, b) in enumerate(pairs)]
    first = in_copies(0)
    first[0].start()
    ws[0].start()
    barrier = pltpu.get_barrier_semaphore()
    pl.semaphore_signal(barrier, inc=1, device_id=other, device_id_type=MESH)
    for a, b in zip(first[1:], ws[1:]):
        a.start()
        b.start()
    first[4].start()
    for m in range(1, M):
        for a in in_copies(m):
            a.start()
    vacc[...] = jnp.zeros_like(vacc)
    bacc[...] = jnp.zeros_like(bacc)
    pl.semaphore_wait(barrier, 1)

    lane = lax.broadcasted_iota(jnp.int32, (1, 128), 1)
    low_half = lane < HEAD_DIM
    indicator = jnp.where(lax.broadcasted_iota(jnp.int32, (16, D), 1) // HEAD_DIM == lax.broadcasted_iota(jnp.int32, (16, D), 0), 1.0, 0.0).astype(BF)

    def out_copies(m):
        pairs = [(db2, db2_h), (du, du_h), (db1, db1_h), (dqkv, dqkv_h), (dx, dx_h), (dxb, dxb_h)]
        return [pltpu.make_async_copy(a.at[m], b.at[m], outsem.at[m, i]) for i, (a, b) in enumerate(pairs)]

    def handoff(m, i):
        r = pl.ds(i * tb if isinstance(i, int) else pl.multiple_of(i * tb, tb), tb)
        return pltpu.make_async_remote_copy(src_ref=dxb.at[m, r], dst_ref=dyr.at[m, r], send_sem=send_sem.at[m, i],
            recv_sem=recv_sem.at[m, i], device_id=other, device_id_type=MESH)

    def norm_pull(z, scale, gain, dy):
        g = dy * gain
        return scale * (g - jnp.mean(g, axis=-1, keepdims=True) - z * jnp.mean(g * z, axis=-1, keepdims=True))

    def micro_step(m, _):
        ins = in_copies(m)
        outs = out_copies(m)
        mem = members(seg[pl.ds(m, 1), :])
        bias[...] = (dot_tn(mem, mem) - 1.0) * MASK_FILL
        dp3 = jnp.concatenate(split3(dp[m]), axis=0)

        @pl.when(sec == 0)
        def _():
            for i in range(nb):
                handoff(m, i).wait_recv()

        @pl.when(m == 0)
        def _():
            ws[0].wait()
            ws[1].wait()
            ws[2].wait()
        for a in ins[:4]:
            a.wait()

        def tok_step(i, _):
            r = pl.ds(pl.multiple_of(i * tb, tb), tb)

            @pl.when(sec == 0)
            def _():
                dy_s[...] = dyr[m, r, :].astype(F32)

            @pl.when(sec != 0)
            def _():
                blk = members(seg[pl.ds(m, 1), r])
                dy_s[...] = dot_tn(jnp.concatenate([blk, blk, blk], axis=0), dp3)
            dy = dy_s[...]
            z = z2[m, r, :].astype(F32)
            dr2 = norm_pull(z, s12[m, r, 1:2], g2[...].astype(F32), dy)
            vacc[0] += rowsum8(dy * z)
            vacc[1] += rowsum8(dy)
            d2 = dr2.astype(BF)
            db2[m, r, :] = d2
            vacc[2] += rowsum8(d2.astype(F32))
            dh = dr2
            nj = FF // fc
            dfs = [dot_nt(d2, wout[:fc, :])]
            for j in range(nj):
                cols = slice(j * fc, (j + 1) * fc)
                if j + 1 < nj:
                    dfs.append(dot_nt(d2, wout[(j + 1) * fc:(j + 2) * fc, :]))
                dub = (dfs[j] * gp[m, r, cols].astype(F32)).astype(BF)
                du[m, r, cols] = dub
                bacc[:, cols] += rowsum8(dub.astype(F32))
                dh = dh + dot_nt(dub, win[:, cols])
            z = z1[m, r, :].astype(F32)
            d1 = norm_pull(z, s12[m, r, 0:1], g1[...].astype(F32), dh)
            vacc[3] += rowsum8(dh * z)
            vacc[4] += rowsum8(dh)
            dr1[r, :] = d1
            d1 = d1.astype(BF)
            db1[m, r, :] = d1
            vacc[5] += rowsum8(d1.astype(F32))
            dcb = dot_nt(d1, wat[...]).astype(BF)
            dc[r, :] = dcb
            prod = dcb.astype(F32) * c_s[m, r, :].astype(F32)
            hi = prod.astype(BF)
            low = (prod - hi.astype(F32)).astype(BF)
            delta[:, r] = dot_nt(indicator, hi) + dot_nt(indicator, low)
            return 0
        lax.fori_loop(0, nb, tok_step, 0)
        for o in outs[:3]:
            o.start()
        ins[4].wait()

        def att_step(p, _):
            cols = pl.ds(pl.multiple_of(p * 128, 128), 128)
            kcols = pl.ds(pl.multiple_of(p * 128 + D, 128), 128)
            vcols = pl.ds(pl.multiple_of(p * 128 + 2 * D, 128), 128)
            q2 = qkv[m, :, cols] * (HEAD_DIM ** -0.5)
            dc2 = dc[:, cols]
            dqt = jnp.zeros((128, T), F32)
            for i in range(T // kb):
                rows = slice(i * kb, (i + 1) * kb)
                k2 = qkv[m, rows, kcols]
                v2 = qkv[m, rows, vcols]
                dks, dvs = [], []
                for h in range(2):
                    pick = low_half if h == 0 else jnp.logical_not(low_half)
                    kh = jnp.where(pick, k2, 0)
                    vh = jnp.where(pick, v2, 0)
                    st = dot_nt(kh, q2) + bias[rows, :]
                    pt = jnp.exp(st - lse[m, pl.ds(2 * p + h, 1), :])
                    dpt = dot_nt(vh, dc2)
                    da = (pt * (dpt - delta[pl.ds(2 * p + h, 1), :])).astype(BF)
                    dvs.append(dot(pt.astype(BF), dc2))
                    dks.append(dot(da, q2))
                    dqt = dqt + dot_tn(kh, da)
                dqkv[m, rows, kcols] = jnp.where(low_half, dks[0], dks[1]).astype(BF)
                dqkv[m, rows, vcols] = jnp.where(low_half, dvs[0], dvs[1]).astype(BF)
            dqkv[m, :, cols] = (jnp.transpose(dqt) * (HEAD_DIM ** -0.5)).astype(BF)
            return 0
        lax.fori_loop(0, HEADS // 2, att_step, 0)
        outs[3].start()

        @pl.when(m == 0)
        def _():
            ws[3].wait()

        def dx_step(i, _):
            r = pl.ds(pl.multiple_of(i * tb, tb), tb)
            v = dr1[r, :] + dot_nt(dqkv[m, r, :], wqkv[...])
            dx[m, r, :] = v
            dxb[m, r, :] = v.astype(BF)
            vacc[6] += rowsum8(dqkv[m, r, :D].astype(F32))
            vacc[7] += rowsum8(dqkv[m, r, 2 * D:].astype(F32))

            @pl.when(sec != 0)
            def _():
                handoff(m, i).start()
            return 0
        lax.fori_loop(0, nb, dx_step, 0)
        outs[4].start()
        outs[5].start()
        return 0
    lax.fori_loop(0, M, micro_step, 0)
    vec_o[...] = jnp.concatenate([jnp.sum(vacc[...], axis=1)]
        + [jnp.sum(bacc[:, j * D:(j + 1) * D], axis=0, keepdims=True) for j in range(FF // D)] + [jnp.zeros((4, D), F32)], axis=0)
    for m in range(M):
        for o in out_copies(m):
            o.wait()

    @pl.when(sec != 0)
    def _():
        for m in range(M):
            for i in range(nb):
                handoff(m, i).wait_send()


def stack_bwd(seg, dp, stash, weights, tb=256, fc=768, kb=256):
    qkv, lse, c, z1, s12, gp, z2 = stash
    wqkv, bq, bv, wat, bat, g1, b1, win, bin_, wout, bout, g2, b2 = weights
    M, T, D = c.shape
    FF = win.shape[1]
    sds = jax.ShapeDtypeStruct
    out_shape = (sds((16, D), F32), sds((M, T, D), F32), sds((M, T, D), BF), sds((M, T, D), BF), sds((M, T, FF), BF), sds((M, T, D), BF), sds((M, T, 3 * D), BF))
    out_specs = (VM, ANY, ANY, ANY, ANY, ANY, ANY)
    V = pltpu.VMEM
    S = pltpu.SemaphoreType.DMA
    nb = T // tb
    scratch = [V((M, T, D), BF), V((D, 3 * D), BF), V((D, D), BF), V((D, FF), BF), V((FF, D), BF),
        V((M, T, 3 * D), BF), V((M, T, D), BF), V((M, T, D), BF), V((M, T, FF), BF), V((M, T, D), BF),
        V((T, T), F32), V((tb, D), F32), V((T, D), F32), V((T, D), BF), V((16, T), F32),
        V((M, T, FF), BF), V((M, T, D), BF), V((M, T, D), BF), V((M, T, 3 * D), BF), V((M, T, D), F32), V((M, T, D), BF),
        V((8, 8, D), F32), V((8, FF), F32), S((M, 5)), S((4,)), S((M, 6)), S((M, nb)), S((M, nb))]
    in_specs = (VM, VM, VM, VM, ANY, ANY, ANY, ANY, ANY, ANY, ANY, VM, ANY, ANY, VM)
    return pl.pallas_call(functools.partial(bwd_kernel, tb, fc, kb), out_shape=out_shape, in_specs=in_specs, out_specs=out_specs,
        scratch_shapes=scratch, compiler_params=pltpu.CompilerParams(vmem_limit_bytes=VMEM_LIMIT, collective_id=1, has_side_effects=True),
        name="stack_bwd")(seg, dp, lse, s12, qkv, c, z1, gp, z2, wqkv, wat, g1, win, wout, g2)


BEFORE_TOKENS = " ".join(("T0 T1 a0 T2", "a1 T3",))
AFTER_TOKENS = (" ".join(("a2 a3 b0",)), " ".join(("b1 W0 W1 a4", "c0 W2 a5 b2", "W3 a6 c1 A0", "b3",)))
AFTER_PAIR = (" ".join(("a7 b4",)), " ".join(("a8",)), " ".join(("b5",)), " ".join(()), " ".join(("c2",)), " ".join(()))
SECOND_CATCHES_UP = " ".join(("T0 T1 a0 T2", "a1 T3 a2 W0", "a3 W1 a4 b0", "W2 a5 W3 a6", "b1 A0 a7 b4", "b2 a8 c0 b3", "c1 b5 c2",))
AT_THE_END = " ".join(("b6 c4 c3 Q0", "Q1 a9 v0 c5", "b7 Q2 a10 c6", "v1 b8 a11 d5", "d4 d3 c7 v2", "d6 b9 c8 v3", "d7 c9 b10 d8", "d9 c10 b11 d10", "c11 d11",))


def back_kernel(tb, xb, kb,
    seg, pool, pairs, lse, s12, z2_h, gp_h, z1_h, c_h, qkv_h, hb_h, x_h, act_h, wout_h, win_h, wat_h, wqkv_h, g1, g2,
    vec_o, pooled_o, loss_o, g_qkv, g_at, g_in, g_out, dx_o, dxr_o,
    dyx, wqkv, wat, win, wout, qkv, c_s, z1, gp, z2, dr, dc, delta, db2, db1, vacc, bacc,
    msgs, dps, loss_w, dn_s, loss_s, pooled_r, loss_r, rhs, part, got_a, got_b, got_c, got_d, got_t, va, vb,
    insem, wsem, latesem, outsem, send_sem, recv_sem, msg_send, msg_recv, pool_sem, dx_sem,
    send_a, recv_a, send_b, recv_b, send_c, recv_c, send_d, recv_d):
    sec = lax.axis_index("section")
    me = lax.axis_index("dp")
    peers = msgs.shape[0]
    core = lax.rem(me, 2)
    y = lax.rem(lax.div(me, 2), 2)
    z = lax.div(me, 4)
    zlow = lax.rem(z, 2)
    zhigh = lax.div(z, 2)
    other = {"section": 1 - sec}
    sibling = {"dp": me + 1 - 2 * core}
    across = {"dp": me + 2 - 4 * y}
    near = {"dp": me + 4 - 8 * zlow}
    far = {"dp": me + 8 - 16 * zhigh}

    def remote(src, dst, ss, rs, target):
        return pltpu.make_async_remote_copy(src_ref=src, dst_ref=dst, send_sem=ss, recv_sem=rs, device_id=target, device_id_type=MESH)
    M, T, D = c_s.shape
    N = M * T
    FF = gp.shape[2]
    half = D // 2
    nb = T // tb
    nx = T // xb
    nj = FF // D
    chunks = got_a.shape[0]
    rows = got_a.shape[4]
    SL = M * SEGS
    first_z, first_y = nj, nj + 1

    wcp = [pltpu.make_async_copy(a, b, wsem.at[i]) for i, (a, b) in enumerate(
        ((wout_h, wout), (win_h, win), (wat_h, wat), (wqkv_h, wqkv)))]

    def norm_copies(m):
        return [pltpu.make_async_copy(a.at[m], b, insem.at[m, i]) for i, (a, b) in enumerate(((z2_h, z2), (z1_h, z1)))]

    def in_copies(m):
        return [pltpu.make_async_copy(a.at[m], b.at[m], insem.at[m, 2 + i]) for i, (a, b) in enumerate(((gp_h, gp), (c_h, c_s), (qkv_h, qkv)))]

    def act_copy(t):
        return pltpu.make_async_copy(act_h.at[t], rhs.at[t % 2 if isinstance(t, int) else lax.rem(t, 2)], latesem.at[t])
    hb_copy = pltpu.make_async_copy(hb_h, rhs.at[0], latesem.at[nj])
    x_copy = pltpu.make_async_copy(x_h, rhs.at[1], latesem.at[nj + 1])
    norms = norm_copies(0)
    ins = in_copies(0)
    norms[0].start()
    wcp[0].start()
    barrier = pltpu.get_barrier_semaphore()
    pl.semaphore_signal(barrier, inc=1, device_id=other, device_id_type=MESH)
    for d in range(1, peers):
        pl.semaphore_signal(barrier, inc=1, device_id={"dp": lax.rem(me + d, peers)}, device_id_type=MESH)
    for a in [ins[0], wcp[1], norms[1], wcp[2], ins[1], ins[2], wcp[3]]:
        a.start()
    for m in range(1, M):
        for a in in_copies(m):
            a.start()
    act_copy(0).start()
    act_copy(1).start()
    vacc[...] = jnp.zeros_like(vacc)
    bacc[...] = jnp.zeros_like(bacc)

    def msg_copy(d):
        return remote(msgs.at[me], msgs.at[me], msg_send.at[d - 1], msg_recv.at[d - 1], {"dp": lax.rem(me + d, peers)})
    pool_copy = remote(dn_s.at[pl.ds(0, SL)], pooled_r, pool_sem.at[0], pool_sem.at[1], other)
    loss_copy = remote(loss_s, loss_r, pool_sem.at[2], pool_sem.at[3], other)
    pl.semaphore_wait(barrier, peers)

    @pl.when(sec != 0)
    def _():
        parts, counts = [], []
        for m in range(M):
            n = jnp.sum(members(seg[m:m + 1, :]).astype(F32), axis=1, keepdims=True)[:SEGS]
            counts.append(n)
            parts.append(pool[m, :SEGS, :] / n)
        pooled = jnp.concatenate(parts, axis=0)
        counts = jnp.concatenate(counts, axis=0)
        radius = lax.rsqrt(jnp.sum(pooled * pooled, axis=-1, keepdims=True) + UNIT_EPS)
        unit = pooled * radius
        tag = jnp.concatenate([jnp.broadcast_to(pairs[m:m + 1, j:j + 1].astype(F32), (1, 128)) for m in range(M) for j in range(SEGS)], axis=0)
        msgs[me] = jnp.concatenate([jnp.concatenate([unit[:, :half], tag], axis=1), jnp.concatenate([unit[:, half:], tag], axis=1)], axis=0).astype(BF)
        for d in range(1, peers):
            msg_copy(d).start()
        dn_s[0:SL, :] = pooled
        pool_copy.start()
        for d in range(1, peers):
            msg_copy(d).wait_recv()
        G = peers * SL
        lo = msgs[:, :SL, :half].astype(F32).reshape(G, half).astype(BF)
        hi = msgs[:, SL:, :half].astype(F32).reshape(G, half).astype(BF)
        partner = msgs[:, :SL, half:].astype(F32).reshape(G, 128)
        rid = lax.broadcasted_iota(jnp.int32, (G, G), 0)
        cid = lax.broadcasted_iota(jnp.int32, (G, G), 1)
        same = lax.rem(lax.div(rid, SEGS), M) == lax.rem(lax.div(cid, SEGS), M)
        logits = TEMPER * (dot_nt(lo, lo) + dot_nt(hi, hi))
        logits = jnp.where(jnp.logical_and(same, rid != cid), logits, -MASK_FILL)
        peak = jnp.max(logits, axis=-1, keepdims=True)
        exponent = jnp.exp(logits - peak)
        denom = jnp.sum(exponent, axis=-1, keepdims=True)
        doc = (lax.div(cid, SL) * SEGS + lax.rem(cid, SEGS)).astype(F32)
        target = jnp.where(jnp.logical_and(same, doc == partner[:, :1]), 1.0, 0.0)
        loss = peak + jnp.log(denom) - jnp.sum(target * logits, axis=-1, keepdims=True)
        dl = (exponent / denom - target).astype(BF)
        own = pl.ds(pl.multiple_of(me * SL, SL), SL)
        for side, part_of in ((0, lo), (1, hi)):
            dn_s[SL:, side * half:(side + 1) * half] = TEMPER * (dot(dl, part_of) + dot_tn(dl, part_of))
        dn = dn_s[pl.ds(pl.multiple_of(SL + me * SL, SL), SL), :]
        loss_w[...] = jnp.broadcast_to(loss, (G, 128))
        loss_s[...] = loss_w[own, :]
        loss_copy.start()
        dps[...] = (radius * dn - radius * radius * radius * jnp.sum(pooled * dn, axis=-1, keepdims=True) * pooled) / counts
        for d in range(1, peers):
            msg_copy(d).wait_send()

    lane = lax.broadcasted_iota(jnp.int32, (1, 128), 1)
    low_half = lane < HEAD_DIM
    indicator = jnp.where(lax.broadcasted_iota(jnp.int32, (16, D), 1) // HEAD_DIM == lax.broadcasted_iota(jnp.int32, (16, D), 0), 1.0, 0.0).astype(BF)

    def out_copy(m):
        return pltpu.make_async_copy(dyx.at[m], dx_o.at[m], outsem.at[m])

    def handoff(m, i):
        r = pl.ds(i * xb if isinstance(i, int) else pl.multiple_of(i * xb, xb), xb)
        return remote(dyx.at[m, r], dyx.at[m, r], send_sem.at[m, i], recv_sem.at[m, i], other)

    def dx_copy(m):
        return remote(dyx.at[m, :, half:], dxr_o.at[m], dx_sem.at[m, 0], dx_sem.at[m, 1], other)

    def norm_pull(zz, scale, gain, dy):
        g = dy * gain
        return scale * (g - jnp.mean(g, axis=-1, keepdims=True) - zz * jnp.mean(g * zz, axis=-1, keepdims=True))

    def slot(k):
        return k % 2 if isinstance(k, int) else lax.rem(k, 2)

    def copy_a(k):
        return remote(part.at[slot(k), :, :, :, 1 - core], got_a.at[k], send_a.at[k], recv_a.at[k], sibling)

    def copy_b(k):
        if not isinstance(k, int) or k < first_z or k >= first_y:
            return remote(got_a.at[k, :, :, 1 - y], got_b.at[k], send_b.at[k], recv_b.at[k], across)
        return remote(got_a.at[k, zhigh, zlow, 1 - y], got_d.at[k], send_b.at[k], recv_b.at[k], across)

    def copy_c(k):
        if k < first_z:
            return remote(got_b.at[k], got_c.at[pl.ds(2 * (k // 2), 2)], send_c.at[k], recv_c.at[k], near)
        if k < first_y:
            return remote(got_a.at[k, :, 1 - zlow], got_b.at[k], send_c.at[k], recv_c.at[k], near)
        return remote(got_b.at[k, :, 1 - zlow], got_c.at[k], send_c.at[k], recv_c.at[k], near)

    def copy_d(k):
        if not isinstance(k, int) or k < first_z:
            return remote(got_b.at[k], got_t, send_d.at[k], recv_d.at[k], far)
        if k < first_y:
            return remote(got_a.at[k, 1 - zhigh, zlow], got_c.at[k], send_d.at[k], recv_d.at[k], far)
        return remote(got_b.at[k, 1 - zhigh, zlow], got_d.at[k], send_d.at[k], recv_d.at[k], far)

    def e1(k):
        copy_a(k).wait_recv()

        for h in range(2):
            got_a[k, h] = got_a[k, h] + part[slot(k), h, :, :, core]
        if isinstance(k, int) and first_z <= k < first_y:
            copy_c(k).start()
        else:
            copy_b(k).start()
        copy_a(k).wait_send()

    def e2(k):
        if first_z <= k < first_y:
            copy_c(k).wait_recv()
            for h in range(2):
                got_a[k, h, zlow] = got_a[k, h, zlow] + got_b[k, h]
            copy_d(k).start()
            return
        copy_b(k).wait_recv()
        for h in range(2):
            got_b[k, h] = got_b[k, h] + got_a[k, h, :, y]
        if k < first_z:
            @pl.when(zlow != k % 2)
            def _():
                copy_c(k).start()
        else:
            copy_c(k).start()

    def e3(k):
        if k < first_z:
            @pl.when(zlow == k % 2)
            def _():
                copy_c(k).wait_recv()
                for h in range(2):
                    got_b[k, h] = got_b[k, h] + got_c[2 * (k // 2) + h]

                @pl.when(z != k)
                def _():
                    copy_d(k).start()
        elif k < first_y:
            copy_d(k).wait_recv()
            got_a[k, zhigh, zlow] = got_a[k, zhigh, zlow] + got_c[k]
            copy_b(k).start()
        else:
            copy_c(k).wait_recv()
            for h in range(2):
                got_b[k, h, zlow] = got_b[k, h, zlow] + got_c[k, h]
            copy_d(k).start()

    def e4(k):
        if k < first_y:
            copy_b(k).wait_recv()
            return got_a[k, zhigh, zlow, y].astype(F32) + got_d[k].astype(F32)
        copy_d(k).wait_recv()
        return got_b[k, zhigh, zlow].astype(F32) + got_d[k].astype(F32)

    def tile_out(k, lhs, right):
        def side(i, _):
            cols = pl.ds(pl.multiple_of(i * half, half), half)
            v = dot_tn(lhs[:, cols], right)
            part[slot(k), i] = v.astype(BF).reshape(part.shape[2:])
            return 0
        lax.fori_loop(0, 2, side, 0)
        copy_a(k).start()

    def tile_w_out(t):
        act_copy(t).wait()

        def side(i, _):
            cols = pl.ds(pl.multiple_of(i * half, half), half)
            v = dot_tn(rhs[t % 2, :, cols], db2[...].reshape(N, D)).astype(BF)
            for c in range(2):
                for s in range(4):
                    part[slot(t), s // 2, s % 2, i, c] = v[(c * 4 + s) * rows:(c * 4 + s + 1) * rows]
            return 0
        lax.fori_loop(0, 2, side, 0)
        copy_a(t).start()
        (act_copy(t + 2) if t < nj - 2 else hb_copy if t == nj - 2 else x_copy).start()

    def store(k):
        v = e4(k)
        if k < 2 * nj:
            g_in[:, (k - nj) * D:(k - nj + 1) * D] = v
        elif k == 2 * nj:
            g_at[...] = v
        else:
            g_qkv[:, (k - 2 * nj - 1) * D:(k - 2 * nj) * D] = v

    def store_w_out():
        copy_d(z).wait_recv()
        for s in range(4):
            g_out[s * rows:(s + 1) * rows, :] = got_b[z, s // 2, s % 2].astype(F32) + got_t[s // 2, s % 2].astype(F32)

    def run(step):
        what, k = step[0], int(step[1:])
        if what == "T":
            tile_w_out(k)
        elif what == "W":
            if k == 0:
                hb_copy.wait()
            tile_out(nj + k, rhs.at[0], gp[:, :, k * D:(k + 1) * D].reshape(N, D))
        elif what == "A":
            def side(i, _):
                cols = pl.ds(pl.multiple_of(i * half, half), half)
                v = dot_tn(c_s[:, :, cols].reshape(N, half), db1[...].reshape(N, D))
                part[slot(2 * nj), i] = v.astype(BF).reshape(part.shape[2:])
                return 0
            lax.fori_loop(0, 2, side, 0)
            copy_a(2 * nj).start()
        elif what == "Q":
            if k == 0:
                x_copy.wait()
            tile_out(2 * nj + 1 + k, rhs.at[1], qkv[:, :, k * D:(k + 1) * D].reshape(N, D))
        elif what == "v":
            vec_step(k)
        elif what == "d":
            if k >= first_z:
                store(k)
            elif k == nj - 1:
                store_w_out()
        else:
            {"a": e1, "b": e2, "c": e3}[what](k)

    def run_on(where, steps):
        @pl.when(sec == where)
        def _():
            for step in steps.split():
                run(step)

    for m in range(M):
        last = m == M - 1
        norms = norm_copies(m)
        ins = in_copies(m)
        mem = members(seg[m:m + 1, :])
        key_code, query_code = codes(mem)
        norms[0].wait()

        def norm_step(i, _):
            r = pl.ds(pl.multiple_of(i * xb, xb), xb)

            @pl.when(sec == 0)
            def _():
                handoff(m, i).wait_recv()
                dr[r, :] = dyx[m, r, :].astype(F32)

            @pl.when(sec != 0)
            def _():
                blk = members(seg[m:m + 1, r])
                dp3 = jnp.concatenate(split3(jnp.concatenate([dps[m * SEGS:(m + 1) * SEGS, :], jnp.zeros((16 - SEGS, D), F32)], axis=0)), axis=0)
                dr[r, :] = dot_tn(jnp.concatenate([blk, blk, blk], axis=0), dp3)
            dy = dr[r, :]
            zz = z2[r, :].astype(F32)
            dr2 = norm_pull(zz, s12[m, r, 1:2], g2[...].astype(F32), dy)
            vacc[0] += rowsum8(dy * zz)
            vacc[1] += rowsum8(dy)
            d2 = dr2.astype(BF)
            dr[r, :] = dr2
            db2[m, r, :] = d2
            vacc[2] += rowsum8(d2.astype(F32))
            return 0
        lax.fori_loop(0, nx, norm_step, 0)
        if last:
            @pl.when(sec == 0)
            def _():
                for step in BEFORE_TOKENS.split():
                    run(step)
        if m == 0:
            for w in wcp[:3]:
                w.wait()
        norms[1].wait()
        ins[0].wait()
        ins[1].wait()
        for i in range(nb):
            r = slice(i * tb, (i + 1) * tb)
            d2 = db2[m, r, :]
            dh = dr[r, :]
            dfs = [dot_nt(d2, wout[:D, :])]
            for j in range(nj):
                cols = slice(j * D, (j + 1) * D)
                if j + 1 < nj:
                    dfs.append(dot_nt(d2, wout[(j + 1) * D:(j + 2) * D, :]))
                dub = (dfs[j] * gp[m, r, cols].astype(F32)).astype(BF)
                gp[m, r, cols] = dub
                bacc[:, cols] += rowsum8(dub.astype(F32))
                dh = dh + dot_nt(dub, win[:, cols])
            zz = z1[r, :].astype(F32)
            d1 = norm_pull(zz, s12[m, r, 0:1], g1[...].astype(F32), dh)
            vacc[3] += rowsum8(dh * zz)
            vacc[4] += rowsum8(dh)
            dr[r, :] = d1
            d1 = d1.astype(BF)
            db1[m, r, :] = d1
            vacc[5] += rowsum8(d1.astype(F32))
            dcb = dot_nt(d1, wat[...]).astype(BF)
            dc[r, :] = dcb
            prod = dcb.astype(F32) * c_s[m, r, :].astype(F32)
            hi = prod.astype(BF)
            low = (prod - hi.astype(F32)).astype(BF)
            delta[:, r] = dot_nt(indicator, hi) + dot_nt(indicator, low)
            if last:
                run_on(0, AFTER_TOKENS[i])
        if not last:
            for cp in norm_copies(m + 1):
                cp.start()
        ins[2].wait()

        for p in range(HEADS // 2):
            cols = slice(p * 128, (p + 1) * 128)
            kcols = slice(D + p * 128, D + (p + 1) * 128)
            vcols = slice(2 * D + p * 128, 2 * D + (p + 1) * 128)
            q2 = qkv[m, :, cols] * (HEAD_DIM ** -0.5)
            qh = [jnp.where(low_half, q2, query_code), jnp.where(low_half, query_code, q2)]
            dc2 = dc[:, cols]
            dqt = jnp.zeros((128, T), F32)
            for i in range(T // kb):
                r = slice(i * kb, (i + 1) * kb)
                k2 = qkv[m, r, kcols]
                v2 = qkv[m, r, vcols]
                kc = key_code[r]
                dks, dvs = [], []
                for h in range(2):
                    pick = low_half if h == 0 else jnp.logical_not(low_half)
                    kh = jnp.where(low_half, k2, kc) if h == 0 else jnp.where(low_half, kc, k2)
                    pt = jnp.exp(dot_nt(kh, qh[h]) - lse[m, 2 * p + h:2 * p + h + 1, :])
                    dpt = dot_nt(jnp.where(pick, v2, 0), dc2)
                    da = (pt * (dpt - delta[2 * p + h:2 * p + h + 1, :])).astype(BF)
                    dvs.append(dot(pt.astype(BF), dc2))
                    dks.append(dot(da, q2))
                    dqt = dqt + dot_tn(jnp.where(pick, k2, 0), da)
                qkv[m, r, kcols] = jnp.where(low_half, dks[0], dks[1]).astype(BF)
                qkv[m, r, vcols] = jnp.where(low_half, dvs[0], dvs[1]).astype(BF)
            qkv[m, :, cols] = (jnp.transpose(dqt) * (HEAD_DIM ** -0.5)).astype(BF)
            if last:
                run_on(0, AFTER_PAIR[p])
        if m == 0:
            wcp[3].wait()

        def dx_step(i, _):
            r = pl.ds(pl.multiple_of(i * xb, xb), xb)
            dyx[m, r, :] = (dr[r, :] + dot_nt(qkv[m, r, :], wqkv[...])).astype(BF)

            @pl.when(sec != 0)
            def _():
                handoff(m, i).start()
            vacc[6] += rowsum8(qkv[m, r, :D].astype(F32))
            vacc[7] += rowsum8(qkv[m, r, 2 * D:].astype(F32))
            return 0
        lax.fori_loop(0, nx, dx_step, 0)

        @pl.when(sec == 0)
        def _():
            out_copy(m).start()
            dx_copy(m).start()

    run_on(1, SECOND_CATCHES_UP)

    vec = [remote(va.at[i], vb.at[i], s.at[chunks], r.at[chunks], target) for i, (s, r, target) in enumerate(
        ((send_a, recv_a, sibling), (send_b, recv_b, across), (send_c, recv_c, near), (send_d, recv_d, far)))]

    def vec_step(i):
        vec[i].wait_recv()
        total = va[i] + vb[i]
        if i < 3:
            va[i + 1] = total
            vec[i + 1].start()
        else:
            vec_o[...] = total
    va[0] = jnp.concatenate([jnp.sum(vacc[...], axis=1)]
        + [jnp.sum(bacc[:, j * D:(j + 1) * D], axis=0, keepdims=True) for j in range(nj)] + [jnp.zeros((8 - nj, D), F32)], axis=0)
    vec[0].start()
    for step in AT_THE_END.split():
        run(step)

    @pl.when(sec == 0)
    def _():
        pool_copy.wait_recv()
        loss_copy.wait_recv()
        pooled_o[...] = pooled_r[:, :half]
        loss_o[...] = loss_r[...]
        for m in range(M):
            dx_copy(m).wait_send()
            out_copy(m).wait()

    @pl.when(sec != 0)
    def _():
        pool_copy.wait_send()
        loss_copy.wait_send()
        pooled_o[...] = dn_s[0:SL, half:]
        loss_o[...] = loss_s[...]
        for m in range(M):
            for i in range(nx):
                handoff(m, i).wait_send()
            dx_copy(m).wait_recv()
    for v in vec:
        v.wait_send()
    for k in range(chunks):
        copy_b(k).wait_send()
        if k < first_z:
            @pl.when(zlow != k % 2)
            def _():
                copy_c(k).wait_send()

            @pl.when(jnp.logical_and(zlow == k % 2, z != k))
            def _():
                copy_d(k).wait_send()
        else:
            copy_c(k).wait_send()
            copy_d(k).wait_send()


def stack_back(seg, pool, pairs, stash, weights, tb=256, xb=128, kb=256):
    x, qkv, lse, c, z1, s12, hb, gp, act, z2 = stash
    wqkv, bq, bv, wat, bat, g1, b1, win, bin_, wout, bout, g2, b2 = weights
    M, T, D = c.shape
    N = M * T
    FF = win.shape[1]
    count = lax.axis_size("dp")
    rows = D // count
    chunks = (4 * D + 2 * FF) // D
    SL = M * SEGS
    sds = jax.ShapeDtypeStruct
    out_shape = (sds((16, D), F32), sds((SL, D // 2), F32), sds((SL, 128), F32), sds((rows, 3 * D), F32), sds((rows, D), F32), sds((rows, FF), F32),
        sds((FF // count, D), F32), sds((M, T, D), BF), sds((M, T, D // 2), BF))
    out_specs = (VM,) * 7 + (ANY, ANY)
    V = pltpu.VMEM
    S = pltpu.SemaphoreType.DMA
    nx = T // xb
    nj = FF // D
    piece = (rows, D)
    scratch = [V((M, T, D), BF), V((D, 3 * D), BF), V((D, D), BF), V((D, FF), BF), V((FF, D), BF),
        V((M, T, 3 * D), BF), V((M, T, D), BF), V((T, D), BF), V((M, T, FF), BF), V((T, D), BF),
        V((T, D), F32), V((T, D), BF), V((16, T), F32), V((M, T, D), BF), V((M, T, D), BF), V((8, 8, D), F32), V((8, FF), F32),
        V((count, 16, D // 2 + 128), BF), V((SL, D), F32), V((count * SL, 128), F32), V((SL + count * SL, D), F32), V((SL, 128), F32), V((SL, D), F32), V((SL, 128), F32),
        V((2, N, D), BF), V((2, 2, 2, 2, 2) + piece, BF), V((chunks, 2, 2, 2) + piece, BF), V((chunks, 2, 2) + piece, BF),
        V((chunks, 2) + piece, BF), V((chunks,) + piece, BF), V((2, 2) + piece, BF), V((4, 16, D), F32), V((4, 16, D), F32),
        S((M, 5)), S((4,)), S((2 + nj,)), S((M,)), S((M, nx)), S((M, nx)), S((count - 1,)), S((count - 1,)), S((4,)), S((M, 2))]
    scratch += [S((chunks + 1,)) for _ in range(8)]
    in_specs = (VM,) * 5 + (ANY,) * 12 + (VM, VM)
    return pl.pallas_call(functools.partial(back_kernel, tb, xb, kb), out_shape=out_shape, in_specs=in_specs, out_specs=out_specs,
        scratch_shapes=scratch, compiler_params=pltpu.CompilerParams(vmem_limit_bytes=62 * 2**20, collective_id=3, has_side_effects=True),
        name="stack_back")(seg, pool, pairs, lse, s12, z2, gp, z1, c, qkv, hb.reshape(N, D), x.reshape(N, D), act,
            wout, win, wat, wqkv, g1, g2)


def finish_kernel(vec, pooled, loss, g_qkv, g_at, g_in, g_out, dx_h, dxr_h,
    pooled_o, loss_o, gx_o, qkv_o, at_o, in_o, out_o, *rest):
    small, buf, sem = rest[:9], rest[9], rest[10]
    sec = lax.axis_index("section")
    me = lax.axis_index("dp")
    half = buf.shape[2]

    @pl.when(sec == 0)
    def _():
        pltpu.make_async_copy(dx_h.at[:, :, pl.ds(0, half)], buf, sem.at[0]).start()

    @pl.when(sec != 0)
    def _():
        pltpu.make_async_copy(dxr_h, buf, sem.at[0]).start()
    for a, b in ((g_qkv, qkv_o), (g_at, at_o), (g_in, in_o), (g_out, out_o)):
        b[...] = a[...]
    pooled_o[...] = pooled[...]
    loss_o[...] = loss[...]
    D = vec.shape[1]
    width, wide = small[0].shape[1], small[8].shape[1]
    parts = split3(vec[...])

    def columns(start, size):
        pick = lax.broadcasted_iota(jnp.int32, (D, size), 0) == lax.broadcasted_iota(jnp.int32, (D, size), 1) + start
        pick = jnp.where(pick, 1.0, 0.0).astype(BF)
        return (dot(parts[0], pick) + dot(parts[1], pick)) + dot(parts[2], pick)
    v = columns(me * width, 128)
    for i in range(8):
        small[i][...] = v[i:i + 1, :width]
    per = D // wide
    v = columns(lax.rem(me, per) * wide, 256)
    row = lax.broadcasted_iota(jnp.int32, (16, 256), 0) == 8 + lax.div(me, per)
    small[8][...] = jnp.sum(jnp.where(row, v, 0.0), axis=0, keepdims=True)[:, :wide]
    pltpu.make_async_copy(dxr_h, buf, sem.at[0]).wait()
    gx_o[...] = buf[...].astype(F32)


def finish(vec, pooled, loss, g_qkv, g_at, g_in, g_out, dx, dxr):
    M, T, D = dx.shape
    count = lax.axis_size("dp")
    sds = jax.ShapeDtypeStruct
    f = lambda a: sds(a.shape, F32)
    out_shape = (f(pooled), f(loss), sds((M, T, D // 2), F32), f(g_qkv), f(g_at), f(g_in), f(g_out)) + tuple(
        sds((1, D // count), F32) for _ in range(8)) + (sds((1, g_in.shape[1] // count), F32),)
    return pl.pallas_call(finish_kernel, out_shape=out_shape, in_specs=(VM,) * 7 + (ANY,) * 2, out_specs=(VM,) * 16,
        scratch_shapes=[pltpu.VMEM((M, T, D // 2), BF), pltpu.SemaphoreType.DMA((1,))],
        compiler_params=pltpu.CompilerParams(vmem_limit_bytes=VMEM_LIMIT), name="finish")(vec, pooled, loss, g_qkv, g_at, g_in, g_out, dx, dxr)


def contrast_head(pool, seg, pairs, all_pairs):
    M, S = pairs.shape
    D = pool.shape[-1]
    counts = jnp.sum((seg[:, :, None] == jnp.arange(SEGS)).astype(F32), axis=1)[:, :, None]
    pooled = pool[:, :SEGS] / counts
    radius = lax.rsqrt(jnp.sum(pooled * pooled, axis=-1, keepdims=True) + UNIT_EPS)
    unit = (pooled * radius).astype(BF)
    every = lax.all_gather(unit, "dp", axis=1, tiled=True)
    total = every.shape[1]
    start = lax.axis_index("dp") * S
    logits = TEMPER * jnp.einsum("mgd,mkd->mgk", every, every, preferred_element_type=F32)
    cols = jnp.arange(total)
    logits = jnp.where(cols[:, None] == cols[None, :], -MASK_FILL, logits)
    peak = jnp.max(logits, axis=-1, keepdims=True)
    exponent = jnp.exp(logits - peak)
    denom = jnp.sum(exponent, axis=-1, keepdims=True)
    target = cols[None, None, :] == all_pairs[:, :, None]
    loss = peak[..., 0] + jnp.log(denom[..., 0]) - jnp.sum(jnp.where(target, logits, 0.0), axis=-1)
    dl = (exponent / denom - target.astype(F32)).astype(BF)
    rows = lax.dynamic_slice_in_dim(dl, start, S, 1)
    columns = lax.dynamic_slice_in_dim(dl, start, S, 2)
    dn = TEMPER * (jnp.einsum("mgk,mkd->mgd", rows, every, preferred_element_type=F32)
        + jnp.einsum("mkg,mkd->mgd", columns, every, preferred_element_type=F32))
    dp = radius * dn - radius * radius * radius * jnp.sum(pooled * dn, axis=-1, keepdims=True) * pooled
    loss = lax.dynamic_slice_in_dim(loss, start, S, 1)
    return pooled, loss, jnp.pad(dp / counts, ((0, 0), (0, 16 - SEGS), (0, 0)))


def scattered(grads):
    count = lax.axis_size("dp")
    packed = jnp.concatenate([g.reshape(count, -1) for g in grads], axis=1)
    part = lax.psum_scatter(packed, "dp", scatter_dimension=0, tiled=True)[0].astype(F32)
    outs, at = [], 0
    for g in grads:
        size = g.size // count
        outs.append(part[at:at + size].reshape((1, g.shape[0] // count) + g.shape[1:]))
        at += size
    return outs


def swapped(value):
    return lax.ppermute(value, "section", [(0, 1), (1, 0)])


def local(hidden_in, seg_ids, pair_ids, w_qkv, b_query, b_value, w_attn_out, b_attn_out, ln1_gain, ln1_bias, w_in, b_in, w_out, b_out, ln2_gain, ln2_bias):
    M, _, T, D = hidden_in.shape
    sec = lax.axis_index("section")
    first = sec == 0
    seg = seg_ids[:, 0]
    weights = (w_qkv[0], b_query, b_value, w_attn_out[0], b_attn_out, ln1_gain, ln1_bias, w_in[0], b_in, w_out[0], b_out, ln2_gain, ln2_bias)
    half = D // 2
    count = lax.axis_size("dp")
    pool, x, qkv, lse, c, z1, s12, hb, gp, act, z2 = stack_fwd(hidden_in[:, 0], seg, weights)
    if count == 16:
        parts = stack_back(seg, pool, pair_ids, (x, qkv, lse, c, z1, s12, hb, gp, act, z2), weights)
        pooled, loss, grad_input, g_qkv, g_at, g_in, g_out, gg2, gb2, gbo, gg1, gb1, gba, gbq, gbv, gbi = finish(*parts)
        pooled_out = pooled.reshape(M, SEGS, half)
        loss_out = loss[:, 0].reshape(M, SEGS)
        g_qkv, g_at, g_in, g_out = (g[None] for g in (g_qkv, g_at, g_in, g_out))
    else:
        all_pairs = lax.all_gather(pair_ids, "dp", axis=1, tiled=True)
        pooled, loss, dp = contrast_head(pool, seg, pair_ids, all_pairs)
        vec, dx, dxb, db2, du, db1, dqkv = stack_bwd(seg, dp, (qkv, lse, c, z1, s12, gp, z2), weights)
        act = jnp.moveaxis(act, 0, 1).reshape(M, T, -1)
        big = [jnp.einsum("mta,mtb->ab", a, b, preferred_element_type=F32).astype(BF) for a, b in ((x, dqkv), (c, db1), (hb, du), (act, db2))]
        g_qkv, g_at, g_in, g_out = scattered(big)
        small = scattered([vec[i] for i in range(8)] + [vec[8:8 + w_in.shape[2] // D].reshape(-1)])
        gg2, gb2, gbo, gg1, gb1, gba, gbq, gbv, gbi = small
        kept = lax.dynamic_slice_in_dim(dx, sec * half, half, 2)
        sent = lax.dynamic_slice_in_dim(dxb, (1 - sec) * half, half, 2)
        grad_input = jnp.where(first, kept, swapped(sent).astype(F32))
        pooled_kept = lax.dynamic_slice_in_dim(pooled, sec * half, half, 2)
        pooled_sent = lax.dynamic_slice_in_dim(pooled, (1 - sec) * half, half, 2).astype(BF)
        pooled_out = jnp.where(first, swapped(pooled_sent).astype(F32), pooled_kept)
        loss_out = jnp.where(first, swapped(loss.astype(BF)).astype(F32), loss)
    return (pooled_out, loss_out, grad_input[:, None], g_qkv, gbq, gbv, g_at, gba, gg1, gb1, g_in, gbi, g_out, gbo, gg2, gb2)


def solution(mesh):
    in_specs = (
        P(None, "dp", None, None),
        P(None, "dp", None),
        P(None, "dp"),
        P("section", None, None),
        P("section", None),
        P("section", None),
        P("section", None, None),
        P("section", None),
        P("section", None),
        P("section", None),
        P("section", None, None),
        P("section", None),
        P("section", None, None),
        P("section", None),
        P("section", None),
        P("section", None),
    )
    out_specs = (
        P(None, "dp", "section"),
        P(None, "dp"),
        P(None, "dp", None, "section"),
        P("section", "dp", None),
        P("section", "dp"),
        P("section", "dp"),
        P("section", "dp", None),
        P("section", "dp"),
        P("section", "dp"),
        P("section", "dp"),
        P("section", "dp", None),
        P("section", "dp"),
        P("section", "dp", None),
        P("section", "dp"),
        P("section", "dp"),
        P("section", "dp"),
    )
    return jax.shard_map(local, mesh=mesh, in_specs=in_specs, out_specs=out_specs, check_vma=False)
```

```python
import functools
import jax, jax.numpy as jnp
from jax import lax
from jax.experimental import pallas as pl
from jax.experimental.pallas import tpu as pltpu
from jax.sharding import PartitionSpec as P

HEADS = 12
HEAD_DIM = 64
SEGS = 4
UNIT_EPS = 1e-06
TEMPER = 20.0
MASK_FILL = 1000000000.0
NORM_EPS = 1e-12
BF = jnp.bfloat16
F32 = jnp.float32
VMEM_LIMIT = 60 * 2**20
MESH = pl.DeviceIdType.MESH
ANY = pl.BlockSpec(memory_space=pl.ANY)
VM = pl.BlockSpec(memory_space=pltpu.VMEM)


def dot(a, b):
    return jnp.dot(a, b, preferred_element_type=F32)


def dot_nt(a, b):
    return lax.dot_general(a, b, (((1,), (1,)), ((), ())), preferred_element_type=F32)


def dot_tn(a, b):
    return lax.dot_general(a, b, (((0,), (0,)), ((), ())), preferred_element_type=F32)


def split3(v):
    hi = v.astype(BF)
    rest = v - hi.astype(F32)
    mid = rest.astype(BF)
    low = (rest - mid.astype(F32)).astype(BF)
    return hi, mid, low


def members(seg_row):
    rows = lax.broadcasted_iota(jnp.int32, (16, seg_row.shape[1]), 0)
    return jnp.where(rows == seg_row, 1.0, 0.0).astype(BF)


def normed_rows(rows):
    centre = rows - jnp.mean(rows, axis=-1, keepdims=True)
    scale = lax.rsqrt(jnp.mean(centre * centre, axis=-1, keepdims=True) + NORM_EPS)
    return centre * scale, scale


def gelu_pair(u):
    mag = jnp.abs(u)
    t = 1.0 / (1.0 + (0.3275911 * 0.7071067811865476) * mag)
    e = jnp.exp(-0.5 * (u * u))
    poly = t * (0.127414796 + t * (-0.142248368 + t * (0.7107068705 + t * (-0.7265760135 + t * 0.5307027145))))
    tail = poly * e
    cdf = jnp.where(u >= 0.0, 1.0 - tail, tail)
    return u * cdf, cdf + (u * 0.3989422804014327) * e


def codes(mem):
    lanes = lax.rem(lax.broadcasted_iota(jnp.int32, (16, 128), 1), HEAD_DIM)
    pick = jnp.where(lanes == lax.broadcasted_iota(jnp.int32, (16, 128), 0), 1.0, 0.0)
    pick = jnp.where(lanes < SEGS, pick, 0.0).astype(BF)
    key_code = dot_tn(mem, pick)
    active = jnp.where(lanes[:1] < SEGS, 1.0, 0.0)
    return key_code.astype(BF), ((key_code - active) * MASK_FILL).astype(BF)


def documents(mem, pool):
    counts = jnp.maximum(jnp.sum(mem.astype(F32), axis=1, keepdims=True)[:8], 1.0)
    pooled = pool[:8, :] / counts
    radius = lax.rsqrt(jnp.sum(pooled * pooled, axis=-1, keepdims=True) + UNIT_EPS)
    return pooled, radius, counts


def message(unit, pairs):
    half = unit.shape[1] // 2
    tag = [jnp.broadcast_to(pairs[:, j:j + 1].astype(F32), (1, 128)) for j in range(SEGS)]
    tag = jnp.concatenate(tag + [jnp.zeros((8 - SEGS, 128), F32)], axis=0)
    return jnp.concatenate([jnp.concatenate([unit[:, :half], tag], axis=1), jnp.concatenate([unit[:, half:], tag], axis=1)], axis=0).astype(BF)


def fwd_kernel(tb, fc, peers,
    x_h, seg, pairs, wqkv_h, bq, bv, wat_h, bat, g1, b1, win_h, bin_, wout_h, bout, g2, b2,
    pool_o, x_o, qkv_h, lse_o, c_h, z1_h, s12_o, hb_h, gp_h, act_h, z2_h, msgs_o,
    x_s, wqkv, wat, win, wout, qkv, c_s, hb_s, z1_s, gp_s, act_s, z2_s, y_s, yf, msgs,
    insem, wsem, outsem, send_sem, recv_sem, msg_send, msg_recv):
    sec = lax.axis_index("section")
    me = lax.axis_index("dp")
    other = {"section": 1 - sec}
    M, T, D = x_s.shape
    FF = win.shape[1]
    nb = T // tb

    ws = [pltpu.make_async_copy(a, b, wsem.at[i]) for i, (a, b) in enumerate(
        ((wqkv_h, wqkv), (wat_h, wat), (win_h, win), (wout_h, wout)))]
    barrier = pltpu.get_barrier_semaphore()

    @pl.when(sec == 0)
    def _():
        pltpu.make_async_copy(x_h.at[0], x_s.at[0], insem.at[0]).start()
    ws[0].start()
    pl.semaphore_signal(barrier, inc=1, device_id=other, device_id_type=MESH)
    for d in range(1, peers):
        pl.semaphore_signal(barrier, inc=1, device_id={"dp": lax.rem(me + d, peers)}, device_id_type=MESH)
    for w in ws[1:]:
        w.start()

    @pl.when(sec == 0)
    def _():
        for m in range(1, M):
            pltpu.make_async_copy(x_h.at[m], x_s.at[m], insem.at[m]).start()

    lane = lax.broadcasted_iota(jnp.int32, (1, 128), 1)
    low_half = lane < HEAD_DIM

    def out_copies(m, i):
        r = pl.ds(i * tb, tb)
        span = pl.ds(m * T + i * tb if isinstance(m, int) else pl.multiple_of(m * T + i * tb, tb), tb)
        pairs = [(a.at[m, r], b.at[m, r]) for a, b in ((c_s, c_h), (hb_s, hb_h), (z1_s, z1_h), (z2_s, z2_h), (gp_s, gp_h))]
        pairs += [(act_s.at[m, r, j * D:(j + 1) * D], act_h.at[j, span]) for j in range(FF // D)]
        return [pltpu.make_async_copy(a, b, outsem.at[m, i, j]) for j, (a, b) in enumerate(pairs)]

    def whole_copies(m):
        return [pltpu.make_async_copy(a.at[m], b.at[m], outsem.at[m, nb, j]) for j, (a, b) in enumerate(((x_s, x_o), (qkv, qkv_h)))]

    def handoff(m, i):
        r = pl.ds(i * tb, tb)
        return pltpu.make_async_remote_copy(src_ref=y_s.at[m, r], dst_ref=x_s.at[m, r], send_sem=send_sem.at[m, i],
            recv_sem=recv_sem.at[m, i], device_id=other, device_id_type=MESH)

    def msg_copy(d):
        return pltpu.make_async_remote_copy(src_ref=msgs.at[me], dst_ref=msgs.at[me], send_sem=msg_send.at[d - 1], recv_sem=msg_recv.at[d - 1],
            device_id={"dp": lax.rem(me + d, peers)}, device_id_type=MESH)

    def micro_step(m, _):
        mem = members(seg[m])
        key_code, query_code = codes(mem)

        @pl.when(sec == 0)
        def _():
            pltpu.make_async_copy(x_h.at[m], x_s.at[m], insem.at[m]).wait()

        @pl.when(m == 0)
        def _():
            ws[0].wait()

        @pl.when(sec != 0)
        def _():
            for i in range(nb):
                handoff(m, i).wait_recv()
        xi = x_s[m]
        for j, b in ((0, bq), (1, None), (2, bv)):
            cols = slice(j * D, (j + 1) * D)
            v = dot(xi, wqkv[:, cols])
            if b is not None:
                v = v + b[...].astype(F32)
            qkv[m, :, cols] = v.astype(BF)
        for cp in whole_copies(m):
            cp.start()
        ones = jnp.ones((T, 128), BF)
        for i in range(nb):
            r = slice(i * tb, (i + 1) * tb)
            lses = jnp.zeros((tb, 128), F32)
            for p in range(HEADS // 2):
                cols = slice(p * 128, (p + 1) * 128)
                k2 = qkv[m, :, D + p * 128:D + (p + 1) * 128]
                v2 = jnp.concatenate([qkv[m, :, 2 * D + p * 128:2 * D + (p + 1) * 128], ones], axis=1)
                q2 = qkv[m, r, cols] * (HEAD_DIM ** -0.5)
                qc = query_code[r]
                halves = []
                for h in range(2):
                    if h == 0:
                        s = dot_nt(jnp.where(low_half, q2, qc), jnp.where(low_half, k2, key_code))
                    else:
                        s = dot_nt(jnp.where(low_half, qc, q2), jnp.where(low_half, key_code, k2))
                    mx = jnp.max(s, axis=-1, keepdims=True)
                    e = jnp.exp(s - mx).astype(BF)
                    c = dot(e, v2)
                    l = c[:, 128:]
                    halves.append(c[:, :128] / l)
                    lses = jnp.where(lane == 2 * p + h, mx + jnp.log(l), lses)
                c_s[m, r, cols] = jnp.where(low_half, halves[0], halves[1]).astype(BF)
            lse_o[m, :, r] = jnp.transpose(lses)[:16, :]
            if i == 0:
                @pl.when(m == 0)
                def _():
                    for w in ws[1:]:
                        w.wait()
                    pl.semaphore_wait(barrier, max(peers, 1))
            r1 = x_s[m, r, :].astype(F32) + dot(c_s[m, r, :], wat[...]) + bat[...].astype(F32)
            z, scale = normed_rows(r1)
            acc = z * g1[...].astype(F32) + b1[...].astype(F32)
            hi = acc.astype(BF)
            hb_s[m, r, :] = hi
            z1_s[m, r, :] = z.astype(BF)
            s12_o[m, r, 0:1] = scale
            acc = acc + bout[...].astype(F32)
            nj = FF // fc
            us = [dot(hi, win[:, :fc])]
            for j in range(nj):
                cols = slice(j * fc, (j + 1) * fc)
                if j + 1 < nj:
                    us.append(dot(hi, win[:, (j + 1) * fc:(j + 2) * fc]))
                f, gp = gelu_pair(us[j] + bin_[:, cols].astype(F32))
                f = f.astype(BF)
                act_s[m, r, cols] = f
                gp_s[m, r, cols] = gp.astype(BF)
                acc = acc + dot(f, wout[cols, :])
            z, scale = normed_rows(acc)
            y = z * g2[...].astype(F32) + b2[...].astype(F32)
            y_s[m, r, :] = y.astype(BF)

            @pl.when(sec == 0)
            def _():
                handoff(m, i).start()
            z2_s[m, r, :] = z.astype(BF)
            s12_o[m, r, 1:2] = scale
            yf[r, :] = y
            for cp in out_copies(m, i):
                cp.start()

        @pl.when(sec != 0)
        def _():
            hi, mid, low = split3(yf[...])
            pool = (dot(mem, hi) + dot(mem, mid)) + dot(mem, low)
            pool_o[m] = pool
            if peers:
                @pl.when(m == 0)
                def _():
                    pooled, radius, _ = documents(mem, pool)
                    msgs[me] = message(pooled * radius, pairs[0:1, :])
                    for d in range(1, peers):
                        msg_copy(d).start()
        return 0
    lax.fori_loop(0, M, micro_step, 0)

    @pl.when(sec == 0)
    def _():
        pool_o[...] = jnp.zeros_like(pool_o)
        msgs_o[...] = jnp.zeros_like(msgs_o)

    if peers:
        @pl.when(sec != 0)
        def _():
            for d in range(1, peers):
                msg_copy(d).wait()
            msgs_o[...] = msgs[...]
    for m in range(M):
        for cp in whole_copies(m):
            cp.wait()
        for i in range(nb):
            for cp in out_copies(m, i):
                cp.wait()

    @pl.when(sec == 0)
    def _():
        for m in range(M):
            for i in range(nb):
                handoff(m, i).wait_send()


def stack_fwd(x, seg, pairs, weights, peers, tb=256, fc=768):
    M, T, D = x.shape
    FF = weights[7].shape[1]
    sds = jax.ShapeDtypeStruct
    out_shape = (sds((M, 16, D), F32), sds((M, T, D), BF), sds((M, T, 3 * D), BF), sds((M, 16, T), F32), sds((M, T, D), BF),
        sds((M, T, D), BF), sds((M, T, 2), F32), sds((M, T, D), BF), sds((M, T, FF), BF), sds((FF // D, M * T, D), BF), sds((M, T, D), BF), sds((max(peers, 1), 16, D // 2 + 128), BF))
    out_specs = (VM, ANY, ANY, VM, ANY, ANY, VM, ANY, ANY, ANY, ANY, VM)
    V = pltpu.VMEM
    S = pltpu.SemaphoreType.DMA
    nb = T // tb
    scratch = [V((M, T, D), BF), V((D, 3 * D), BF), V((D, D), BF), V((D, FF), BF), V((FF, D), BF), V((M, T, 3 * D), BF),
        V((M, T, D), BF), V((M, T, D), BF), V((M, T, D), BF), V((M, T, FF), BF), V((M, T, FF), BF), V((M, T, D), BF), V((M, T, D), BF),
        V((T, D), F32), V((max(peers, 1), 16, D // 2 + 128), BF), S((M,)), S((4,)), S((M, nb + 1, 5 + FF // D)), S((M, nb)), S((M, nb)),
        S((max(peers, 2) - 1,)), S((max(peers, 2) - 1,))]
    in_specs = (ANY, VM, VM, ANY, VM, VM, ANY, VM, VM, VM, ANY, VM, ANY, VM, VM, VM)
    return pl.pallas_call(functools.partial(fwd_kernel, tb, fc, peers), out_shape=out_shape, in_specs=in_specs, out_specs=out_specs,
        scratch_shapes=scratch, compiler_params=pltpu.CompilerParams(vmem_limit_bytes=VMEM_LIMIT, collective_id=0, has_side_effects=True),
        name="stack_fwd")(x, seg, pairs, *weights)


def rowsum8(v):
    return jnp.sum(v.reshape(v.shape[0] // 8, 8, v.shape[1]), axis=0)


def bwd_kernel(tb, fc, kb,
    seg, dp, lse, s12, qkv_h, c_h, z1_h, gp_h, z2_h, wqkv_h, wat_h, g1, win_h, wout_h, g2,
    vec_o, dx_h, dxb_h, db2_h, du_h, db1_h, dqkv_h,
    dyr, wqkv, wat, win, wout, qkv, c_s, z1, gp, z2, bias, dy_s, dr1, dc, delta, du, db2, db1, dqkv, dx, dxb, vacc, bacc,
    insem, wsem, outsem, send_sem, recv_sem):
    sec = lax.axis_index("section")
    other = {"section": 1 - sec}
    M, T, D = c_s.shape
    FF = win.shape[1]
    nb = T // tb

    ws = [pltpu.make_async_copy(a, b, wsem.at[i]) for i, (a, b) in enumerate(
        ((wout_h, wout), (win_h, win), (wat_h, wat), (wqkv_h, wqkv)))]

    def in_copies(m):
        pairs = [(z2_h, z2), (gp_h, gp), (z1_h, z1), (c_h, c_s), (qkv_h, qkv)]
        return [pltpu.make_async_copy(a.at[m], b.at[m], insem.at[m, i]) for i, (a, b) in enumerate(pairs)]
    first = in_copies(0)
    first[0].start()
    ws[0].start()
    barrier = pltpu.get_barrier_semaphore()
    pl.semaphore_signal(barrier, inc=1, device_id=other, device_id_type=MESH)
    for a, b in zip(first[1:], ws[1:]):
        a.start()
        b.start()
    first[4].start()
    for m in range(1, M):
        for a in in_copies(m):
            a.start()
    vacc[...] = jnp.zeros_like(vacc)
    bacc[...] = jnp.zeros_like(bacc)
    pl.semaphore_wait(barrier, 1)

    lane = lax.broadcasted_iota(jnp.int32, (1, 128), 1)
    low_half = lane < HEAD_DIM
    indicator = jnp.where(lax.broadcasted_iota(jnp.int32, (16, D), 1) // HEAD_DIM == lax.broadcasted_iota(jnp.int32, (16, D), 0), 1.0, 0.0).astype(BF)

    def out_copies(m):
        pairs = [(db2, db2_h), (du, du_h), (db1, db1_h), (dqkv, dqkv_h), (dx, dx_h), (dxb, dxb_h)]
        return [pltpu.make_async_copy(a.at[m], b.at[m], outsem.at[m, i]) for i, (a, b) in enumerate(pairs)]

    def handoff(m, i):
        r = pl.ds(i * tb if isinstance(i, int) else pl.multiple_of(i * tb, tb), tb)
        return pltpu.make_async_remote_copy(src_ref=dxb.at[m, r], dst_ref=dyr.at[m, r], send_sem=send_sem.at[m, i],
            recv_sem=recv_sem.at[m, i], device_id=other, device_id_type=MESH)

    def norm_pull(z, scale, gain, dy):
        g = dy * gain
        return scale * (g - jnp.mean(g, axis=-1, keepdims=True) - z * jnp.mean(g * z, axis=-1, keepdims=True))

    def micro_step(m, _):
        ins = in_copies(m)
        outs = out_copies(m)
        mem = members(seg[pl.ds(m, 1), :])
        bias[...] = (dot_tn(mem, mem) - 1.0) * MASK_FILL
        dp3 = jnp.concatenate(split3(dp[m]), axis=0)

        @pl.when(sec == 0)
        def _():
            for i in range(nb):
                handoff(m, i).wait_recv()

        @pl.when(m == 0)
        def _():
            ws[0].wait()
            ws[1].wait()
            ws[2].wait()
        for a in ins[:4]:
            a.wait()

        def tok_step(i, _):
            r = pl.ds(pl.multiple_of(i * tb, tb), tb)

            @pl.when(sec == 0)
            def _():
                dy_s[...] = dyr[m, r, :].astype(F32)

            @pl.when(sec != 0)
            def _():
                blk = members(seg[pl.ds(m, 1), r])
                dy_s[...] = dot_tn(jnp.concatenate([blk, blk, blk], axis=0), dp3)
            dy = dy_s[...]
            z = z2[m, r, :].astype(F32)
            dr2 = norm_pull(z, s12[m, r, 1:2], g2[...].astype(F32), dy)
            vacc[0] += rowsum8(dy * z)
            vacc[1] += rowsum8(dy)
            d2 = dr2.astype(BF)
            db2[m, r, :] = d2
            vacc[2] += rowsum8(d2.astype(F32))
            dh = dr2
            nj = FF // fc
            dfs = [dot_nt(d2, wout[:fc, :])]
            for j in range(nj):
                cols = slice(j * fc, (j + 1) * fc)
                if j + 1 < nj:
                    dfs.append(dot_nt(d2, wout[(j + 1) * fc:(j + 2) * fc, :]))
                dub = (dfs[j] * gp[m, r, cols].astype(F32)).astype(BF)
                du[m, r, cols] = dub
                bacc[:, cols] += rowsum8(dub.astype(F32))
                dh = dh + dot_nt(dub, win[:, cols])
            z = z1[m, r, :].astype(F32)
            d1 = norm_pull(z, s12[m, r, 0:1], g1[...].astype(F32), dh)
            vacc[3] += rowsum8(dh * z)
            vacc[4] += rowsum8(dh)
            dr1[r, :] = d1
            d1 = d1.astype(BF)
            db1[m, r, :] = d1
            vacc[5] += rowsum8(d1.astype(F32))
            dcb = dot_nt(d1, wat[...]).astype(BF)
            dc[r, :] = dcb
            prod = dcb.astype(F32) * c_s[m, r, :].astype(F32)
            hi = prod.astype(BF)
            low = (prod - hi.astype(F32)).astype(BF)
            delta[:, r] = dot_nt(indicator, hi) + dot_nt(indicator, low)
            return 0
        lax.fori_loop(0, nb, tok_step, 0)
        for o in outs[:3]:
            o.start()
        ins[4].wait()

        def att_step(p, _):
            cols = pl.ds(pl.multiple_of(p * 128, 128), 128)
            kcols = pl.ds(pl.multiple_of(p * 128 + D, 128), 128)
            vcols = pl.ds(pl.multiple_of(p * 128 + 2 * D, 128), 128)
            q2 = qkv[m, :, cols] * (HEAD_DIM ** -0.5)
            dc2 = dc[:, cols]
            dqt = jnp.zeros((128, T), F32)
            for i in range(T // kb):
                rows = slice(i * kb, (i + 1) * kb)
                k2 = qkv[m, rows, kcols]
                v2 = qkv[m, rows, vcols]
                dks, dvs = [], []
                for h in range(2):
                    pick = low_half if h == 0 else jnp.logical_not(low_half)
                    kh = jnp.where(pick, k2, 0)
                    vh = jnp.where(pick, v2, 0)
                    st = dot_nt(kh, q2) + bias[rows, :]
                    pt = jnp.exp(st - lse[m, pl.ds(2 * p + h, 1), :])
                    dpt = dot_nt(vh, dc2)
                    da = (pt * (dpt - delta[pl.ds(2 * p + h, 1), :])).astype(BF)
                    dvs.append(dot(pt.astype(BF), dc2))
                    dks.append(dot(da, q2))
                    dqt = dqt + dot_tn(kh, da)
                dqkv[m, rows, kcols] = jnp.where(low_half, dks[0], dks[1]).astype(BF)
                dqkv[m, rows, vcols] = jnp.where(low_half, dvs[0], dvs[1]).astype(BF)
            dqkv[m, :, cols] = (jnp.transpose(dqt) * (HEAD_DIM ** -0.5)).astype(BF)
            return 0
        lax.fori_loop(0, HEADS // 2, att_step, 0)
        outs[3].start()

        @pl.when(m == 0)
        def _():
            ws[3].wait()

        def dx_step(i, _):
            r = pl.ds(pl.multiple_of(i * tb, tb), tb)
            v = dr1[r, :] + dot_nt(dqkv[m, r, :], wqkv[...])
            dx[m, r, :] = v
            dxb[m, r, :] = v.astype(BF)
            vacc[6] += rowsum8(dqkv[m, r, :D].astype(F32))
            vacc[7] += rowsum8(dqkv[m, r, 2 * D:].astype(F32))

            @pl.when(sec != 0)
            def _():
                handoff(m, i).start()
            return 0
        lax.fori_loop(0, nb, dx_step, 0)
        outs[4].start()
        outs[5].start()
        return 0
    lax.fori_loop(0, M, micro_step, 0)
    vec_o[...] = jnp.concatenate([jnp.sum(vacc[...], axis=1)]
        + [jnp.sum(bacc[:, j * D:(j + 1) * D], axis=0, keepdims=True) for j in range(FF // D)] + [jnp.zeros((4, D), F32)], axis=0)
    for m in range(M):
        for o in out_copies(m):
            o.wait()

    @pl.when(sec != 0)
    def _():
        for m in range(M):
            for i in range(nb):
                handoff(m, i).wait_send()


def stack_bwd(seg, dp, stash, weights, tb=256, fc=768, kb=256):
    qkv, lse, c, z1, s12, gp, z2 = stash
    wqkv, bq, bv, wat, bat, g1, b1, win, bin_, wout, bout, g2, b2 = weights
    M, T, D = c.shape
    FF = win.shape[1]
    sds = jax.ShapeDtypeStruct
    out_shape = (sds((16, D), F32), sds((M, T, D), F32), sds((M, T, D), BF), sds((M, T, D), BF), sds((M, T, FF), BF), sds((M, T, D), BF), sds((M, T, 3 * D), BF))
    out_specs = (VM, ANY, ANY, ANY, ANY, ANY, ANY)
    V = pltpu.VMEM
    S = pltpu.SemaphoreType.DMA
    nb = T // tb
    scratch = [V((M, T, D), BF), V((D, 3 * D), BF), V((D, D), BF), V((D, FF), BF), V((FF, D), BF),
        V((M, T, 3 * D), BF), V((M, T, D), BF), V((M, T, D), BF), V((M, T, FF), BF), V((M, T, D), BF),
        V((T, T), F32), V((tb, D), F32), V((T, D), F32), V((T, D), BF), V((16, T), F32),
        V((M, T, FF), BF), V((M, T, D), BF), V((M, T, D), BF), V((M, T, 3 * D), BF), V((M, T, D), F32), V((M, T, D), BF),
        V((8, 8, D), F32), V((8, FF), F32), S((M, 5)), S((4,)), S((M, 6)), S((M, nb)), S((M, nb))]
    in_specs = (VM, VM, VM, VM, ANY, ANY, ANY, ANY, ANY, ANY, ANY, VM, ANY, ANY, VM)
    return pl.pallas_call(functools.partial(bwd_kernel, tb, fc, kb), out_shape=out_shape, in_specs=in_specs, out_specs=out_specs,
        scratch_shapes=scratch, compiler_params=pltpu.CompilerParams(vmem_limit_bytes=VMEM_LIMIT, collective_id=1, has_side_effects=True),
        name="stack_bwd")(seg, dp, lse, s12, qkv, c, z1, gp, z2, wqkv, wat, g1, win, wout, g2)


BEFORE_TOKENS = " ".join(("T0 T1 a0 T2", "a1 T3",))
AFTER_TOKENS = (" ".join(("a2 a3 b0",)), " ".join(("b1 W0 W1 a4", "c0 W2 a5 b2", "W3 a6 c1",)))
AFTER_NORM = " ".join(("A0 b3",))
AFTER_PAIR = (" ".join(("a7",)), " ".join(("a8 c2",)), " ".join(("b4",)), " ".join(()), " ".join(("c3",)), " ".join(()))
SECOND_CATCHES_UP = " ".join(("T0 T1 a0 T2", "a1 T3 a2 W0", "a3 W1 a4 b0", "W2 a5 W3 a6", "b1 A0 a7 c0", "b2 a8 c1 b3", "c2 b4 c3",))
AT_THE_END = " ".join(("b5 b8 Q0 Q1", "v0 a9 c4 b6", "Q2 v1 a10 c5", "d3 b7 a11 c8", "d4 c6 b9 d5", "c7 v2 b10 d6", "c9 v3 d7 b11", "c10 d8 d9 c11", "d10 d11",))


def back_kernel(tb, xb, kb,
    seg, pool, pairs, msgs0, lse, s12, z2_h, gp_h, z1_h, c_h, qkv_h, hb_h, x_h, act_h, wout_h, win_h, wat_h, wqkv_h, g1, g2,
    vec_o, pooled_o, loss_o, g_qkv, g_at, g_in, g_out, dx_o, dxr_o,
    dyx, wqkv, wat, win, wout, qkv, c_s, z1, gp, z2, dr, dc, delta, db2, db1, vacc, bacc,
    msgs, dps, loss_w, dn_s, pooled_s, loss_s, pooled_r, loss_r, rhs, part, got_a, got_b, got_c, got_d, got_t, va, vb,
    insem, wsem, latesem, outsem, send_sem, recv_sem, msg_send, msg_recv, pool_sem, dx_sem,
    send_a, recv_a, send_b, recv_b, send_c, recv_c, send_d, recv_d):
    sec = lax.axis_index("section")
    me = lax.axis_index("dp")
    peers = msgs.shape[0]
    core = lax.rem(me, 2)
    y = lax.rem(lax.div(me, 2), 2)
    z = lax.div(me, 4)
    zlow = lax.rem(z, 2)
    zhigh = lax.div(z, 2)
    other = {"section": 1 - sec}
    sibling = {"dp": me + 1 - 2 * core}
    across = {"dp": me + 2 - 4 * y}
    near = {"dp": me + 4 - 8 * zlow}
    far = {"dp": me + 8 - 16 * zhigh}

    def remote(src, dst, ss, rs, target):
        return pltpu.make_async_remote_copy(src_ref=src, dst_ref=dst, send_sem=ss, recv_sem=rs, device_id=target, device_id_type=MESH)
    M, T, D = c_s.shape
    N = M * T
    FF = gp.shape[2]
    half = D // 2
    nb = T // tb
    nx = T // xb
    nj = FF // D
    chunks = got_a.shape[0]
    rows = got_a.shape[4]
    SL = 8
    zchunk = 2 * nj

    wcp = [pltpu.make_async_copy(a, b, wsem.at[i]) for i, (a, b) in enumerate(
        ((wout_h, wout), (win_h, win), (wat_h, wat), (wqkv_h, wqkv)))]

    def norm_copies(m):
        return [pltpu.make_async_copy(a.at[m], b, insem.at[m, i]) for i, (a, b) in enumerate(((z2_h, z2), (z1_h, z1)))]

    def in_copies(m):
        return [pltpu.make_async_copy(a.at[m], b.at[m], insem.at[m, 2 + i]) for i, (a, b) in enumerate(((gp_h, gp), (c_h, c_s), (qkv_h, qkv)))]

    def act_copy(t):
        return pltpu.make_async_copy(act_h.at[t], rhs.at[t % 2 if isinstance(t, int) else lax.rem(t, 2)], latesem.at[t])
    hb_copy = pltpu.make_async_copy(hb_h, rhs.at[0], latesem.at[nj])
    x_copy = pltpu.make_async_copy(x_h, rhs.at[1], latesem.at[nj + 1])
    norms = norm_copies(0)
    ins = in_copies(0)
    norms[0].start()
    wcp[0].start()
    barrier = pltpu.get_barrier_semaphore()
    pl.semaphore_signal(barrier, inc=1, device_id=other, device_id_type=MESH)
    for d in range(1, peers):
        pl.semaphore_signal(barrier, inc=1, device_id={"dp": lax.rem(me + d, peers)}, device_id_type=MESH)
    for a in [ins[0], wcp[1], norms[1], wcp[2], ins[1], ins[2], wcp[3]]:
        a.start()
    for m in range(1, M):
        for a in in_copies(m):
            a.start()
    act_copy(0).start()
    act_copy(1).start()
    vacc[...] = jnp.zeros_like(vacc)
    bacc[...] = jnp.zeros_like(bacc)

    def msg_copy(d):
        return remote(msgs.at[me], msgs.at[me], msg_send.at[d - 1], msg_recv.at[d - 1], {"dp": lax.rem(me + d, peers)})
    pool_copy = remote(pooled_s, pooled_r, pool_sem.at[0], pool_sem.at[1], other)
    loss_copy = remote(loss_s, loss_r, pool_sem.at[2], pool_sem.at[3], other)
    pl.semaphore_wait(barrier, peers)

    def head(m, gathered):
        pooled, radius, counts = documents(members(seg[m]), pool[m])
        G = peers * SL
        lo = gathered[:, :SL, :half].astype(F32).reshape(G, half).astype(BF)
        hi = gathered[:, SL:, :half].astype(F32).reshape(G, half).astype(BF)
        partner = gathered[:, :SL, half:].astype(F32).reshape(G, 128)
        rid = lax.broadcasted_iota(jnp.int32, (G, G), 0)
        cid = lax.broadcasted_iota(jnp.int32, (G, G), 1)
        held = jnp.logical_and(lax.rem(rid, SL) < SEGS, lax.rem(cid, SL) < SEGS)
        logits = TEMPER * (dot_nt(lo, lo) + dot_nt(hi, hi))
        logits = jnp.where(jnp.logical_and(held, rid != cid), logits, -MASK_FILL)
        peak = jnp.max(logits, axis=-1, keepdims=True)
        exponent = jnp.exp(logits - peak)
        denom = jnp.sum(exponent, axis=-1, keepdims=True)
        doc = (lax.div(cid, SL) * SEGS + lax.rem(cid, SL)).astype(F32)
        target = jnp.where(jnp.logical_and(held, doc == partner[:, :1]), 1.0, 0.0)
        loss = peak + jnp.log(denom) - jnp.sum(target * logits, axis=-1, keepdims=True)
        dl = jnp.where(held, exponent / denom - target, 0.0).astype(BF)
        own = pl.ds(pl.multiple_of(me * SL, SL), SL)
        for side, part_of in ((0, lo), (1, hi)):
            dn_s[:, side * half:(side + 1) * half] = TEMPER * (dot(dl, part_of) + dot_tn(dl, part_of))
        dn = dn_s[own, :]
        loss_w[...] = jnp.broadcast_to(loss, (G, 128))
        loss_s[m * SL:(m + 1) * SL, :] = loss_w[own, :]
        dps[m * SL:(m + 1) * SL, :] = (radius * dn - radius * radius * radius * jnp.sum(pooled * dn, axis=-1, keepdims=True) * pooled) / counts

    @pl.when(sec != 0)
    def _():
        for m in range(M):
            pooled, radius, _ = documents(members(seg[m]), pool[m])
            pooled_s[m * SL:(m + 1) * SL, :] = pooled
            if m == 1:
                msgs[me] = message(pooled * radius, pairs[m:m + 1, :])
        for d in range(1, peers):
            msg_copy(d).start()
        pool_copy.start()
        head(0, msgs0)

    lane = lax.broadcasted_iota(jnp.int32, (1, 128), 1)
    low_half = lane < HEAD_DIM
    indicator = jnp.where(lax.broadcasted_iota(jnp.int32, (16, D), 1) // HEAD_DIM == lax.broadcasted_iota(jnp.int32, (16, D), 0), 1.0, 0.0).astype(BF)

    def out_copy(m):
        return pltpu.make_async_copy(dyx.at[m], dx_o.at[m], outsem.at[m])

    def handoff(m, i):
        r = pl.ds(i * xb if isinstance(i, int) else pl.multiple_of(i * xb, xb), xb)
        return remote(dyx.at[m, r], dyx.at[m, r], send_sem.at[m, i], recv_sem.at[m, i], other)

    def dx_copy(m):
        return remote(dyx.at[m, :, half:], dxr_o.at[m], dx_sem.at[m, 0], dx_sem.at[m, 1], other)

    def norm_pull(zz, scale, gain, dy):
        g = dy * gain
        return scale * (g - jnp.mean(g, axis=-1, keepdims=True) - zz * jnp.mean(g * zz, axis=-1, keepdims=True))

    def slot(k):
        return k % 2 if isinstance(k, int) else lax.rem(k, 2)

    def copy_a(k):
        return remote(part.at[slot(k), :, :, :, 1 - core], got_a.at[k], send_a.at[k], recv_a.at[k], sibling)

    def copy_b(k):
        if not isinstance(k, int) or k != zchunk:
            return remote(got_a.at[k, :, :, 1 - y], got_b.at[k], send_b.at[k], recv_b.at[k], across)
        return remote(got_a.at[k, zhigh, zlow, 1 - y], got_d.at[k], send_b.at[k], recv_b.at[k], across)

    def copy_c(k):
        if k < nj:
            return remote(got_b.at[k], got_c.at[pl.ds(2 * (k // 2), 2)], send_c.at[k], recv_c.at[k], near)
        if k == zchunk:
            return remote(got_a.at[k, :, 1 - zlow], got_b.at[k], send_c.at[k], recv_c.at[k], near)
        return remote(got_b.at[k, :, 1 - zlow], got_c.at[k], send_c.at[k], recv_c.at[k], near)

    def copy_d(k):
        if not isinstance(k, int) or k < nj:
            return remote(got_b.at[k], got_t, send_d.at[k], recv_d.at[k], far)
        if k == zchunk:
            return remote(got_a.at[k, 1 - zhigh, zlow], got_c.at[k], send_d.at[k], recv_d.at[k], far)
        return remote(got_b.at[k, 1 - zhigh, zlow], got_d.at[k], send_d.at[k], recv_d.at[k], far)

    def e1(k):
        copy_a(k).wait_recv()

        for h in range(2):
            got_a[k, h] = got_a[k, h] + part[slot(k), h, :, :, core]
        if isinstance(k, int) and k == zchunk:
            copy_c(k).start()
        else:
            copy_b(k).start()
        copy_a(k).wait_send()

    def e2(k):
        if k == zchunk:
            copy_c(k).wait_recv()
            for h in range(2):
                got_a[k, h, zlow] = got_a[k, h, zlow] + got_b[k, h]
            copy_d(k).start()
            return
        copy_b(k).wait_recv()
        for h in range(2):
            got_b[k, h] = got_b[k, h] + got_a[k, h, :, y]
        if k < nj:
            @pl.when(zlow != k % 2)
            def _():
                copy_c(k).start()
        else:
            copy_c(k).start()

    def e3(k):
        if k < nj:
            @pl.when(zlow == k % 2)
            def _():
                copy_c(k).wait_recv()
                for h in range(2):
                    got_b[k, h] = got_b[k, h] + got_c[2 * (k // 2) + h]

                @pl.when(z != k)
                def _():
                    copy_d(k).start()
        elif k == zchunk:
            copy_d(k).wait_recv()
            got_a[k, zhigh, zlow] = got_a[k, zhigh, zlow] + got_c[k]
            copy_b(k).start()
        else:
            copy_c(k).wait_recv()
            for h in range(2):
                got_b[k, h, zlow] = got_b[k, h, zlow] + got_c[k, h]
            copy_d(k).start()

    def e4(k):
        if k == zchunk:
            copy_b(k).wait_recv()
            return got_a[k, zhigh, zlow, y].astype(F32) + got_d[k].astype(F32)
        copy_d(k).wait_recv()
        return got_b[k, zhigh, zlow].astype(F32) + got_d[k].astype(F32)

    def tile_out(k, lhs, right):
        def side(i, _):
            cols = pl.ds(pl.multiple_of(i * half, half), half)
            v = dot_tn(lhs[:, cols], right)
            part[slot(k), i] = v.astype(BF).reshape(part.shape[2:])
            return 0
        lax.fori_loop(0, 2, side, 0)
        copy_a(k).start()

    def tile_w_out(t):
        act_copy(t).wait()

        def side(i, _):
            cols = pl.ds(pl.multiple_of(i * half, half), half)
            v = dot_tn(rhs[t % 2, :, cols], db2[...].reshape(N, D)).astype(BF)
            for c in range(2):
                for s in range(4):
                    part[slot(t), s // 2, s % 2, i, c] = v[(c * 4 + s) * rows:(c * 4 + s + 1) * rows]
            return 0
        lax.fori_loop(0, 2, side, 0)
        copy_a(t).start()
        (act_copy(t + 2) if t < nj - 2 else hb_copy if t == nj - 2 else x_copy).start()

    def store(k):
        v = e4(k)
        if k < 2 * nj:
            g_in[:, (k - nj) * D:(k - nj + 1) * D] = v
        elif k == 2 * nj:
            g_at[...] = v
        else:
            g_qkv[:, (k - 2 * nj - 1) * D:(k - 2 * nj) * D] = v

    def store_w_out():
        copy_d(z).wait_recv()
        for s in range(4):
            g_out[s * rows:(s + 1) * rows, :] = got_b[z, s // 2, s % 2].astype(F32) + got_t[s // 2, s % 2].astype(F32)

    def run(step):
        what, k = step[0], int(step[1:])
        if what == "T":
            tile_w_out(k)
        elif what == "W":
            if k == 0:
                hb_copy.wait()
            tile_out(nj + k, rhs.at[0], gp[:, :, k * D:(k + 1) * D].reshape(N, D))
        elif what == "A":
            def side(i, _):
                cols = pl.ds(pl.multiple_of(i * half, half), half)
                v = dot_tn(c_s[:, :, cols].reshape(N, half), db1[...].reshape(N, D))
                part[slot(2 * nj), i] = v.astype(BF).reshape(part.shape[2:])
                return 0
            lax.fori_loop(0, 2, side, 0)
            copy_a(2 * nj).start()
        elif what == "Q":
            if k == 0:
                x_copy.wait()
            tile_out(2 * nj + 1 + k, rhs.at[1], qkv[:, :, k * D:(k + 1) * D].reshape(N, D))
        elif what == "v":
            vec_step(k)
        elif what == "d":
            if k >= nj:
                store(k)
            elif k == nj - 1:
                store_w_out()
        else:
            {"a": e1, "b": e2, "c": e3}[what](k)

    def run_on(where, steps):
        @pl.when(sec == where)
        def _():
            for step in steps.split():
                run(step)

    for m in range(M):
        last = m == M - 1
        norms = norm_copies(m)
        ins = in_copies(m)
        mem = members(seg[m])
        key_code, query_code = codes(mem)
        norms[0].wait()
        if m == 1:
            @pl.when(sec != 0)
            def _():
                for d in range(1, peers):
                    msg_copy(d).wait()
                head(1, msgs)
                loss_copy.start()

        def norm_rows(r):
            dy = dr[r, :]
            zz = z2[r, :].astype(F32)
            dr2 = norm_pull(zz, s12[m, r, 1:2], g2[...].astype(F32), dy)
            vacc[0] += rowsum8(dy * zz)
            vacc[1] += rowsum8(dy)
            d2 = dr2.astype(BF)
            dr[r, :] = dr2
            db2[m, r, :] = d2
            vacc[2] += rowsum8(d2.astype(F32))

        @pl.when(sec == 0)
        def _():
            def norm_step(i, _):
                r = pl.ds(pl.multiple_of(i * xb, xb), xb)
                handoff(m, i).wait_recv()
                dr[r, :] = dyx[m, r, :].astype(F32)
                norm_rows(r)
                return 0
            lax.fori_loop(0, nx, norm_step, 0)

        @pl.when(sec != 0)
        def _():
            dp3 = jnp.concatenate(split3(jnp.concatenate([dps[m * SL:(m + 1) * SL, :], jnp.zeros((16 - SL, D), F32)], axis=0)), axis=0)
            dr[...] = dot_tn(jnp.concatenate([mem, mem, mem], axis=0), dp3)
            for i in range(nb):
                norm_rows(slice(i * tb, (i + 1) * tb))
        if last:
            @pl.when(sec == 0)
            def _():
                for step in BEFORE_TOKENS.split():
                    run(step)
        if m == 0:
            for w in wcp[:3]:
                w.wait()
        norms[1].wait()
        ins[0].wait()
        ins[1].wait()
        for i in range(nb):
            r = slice(i * tb, (i + 1) * tb)
            d2 = db2[m, r, :]
            dh = dr[r, :]
            dfs = [dot_nt(d2, wout[:D, :])]
            for j in range(nj):
                cols = slice(j * D, (j + 1) * D)
                if j + 1 < nj:
                    dfs.append(dot_nt(d2, wout[(j + 1) * D:(j + 2) * D, :]))
                dub = (dfs[j] * gp[m, r, cols].astype(F32)).astype(BF)
                gp[m, r, cols] = dub
                bacc[:, cols] += rowsum8(dub.astype(F32))
                dh = dh + dot_nt(dub, win[:, cols])
            dr[r, :] = dh
            if last:
                run_on(0, AFTER_TOKENS[i])
        for i in range(nb):
            r = slice(i * tb, (i + 1) * tb)
            dh = dr[r, :]
            zz = z1[r, :].astype(F32)
            d1 = norm_pull(zz, s12[m, r, 0:1], g1[...].astype(F32), dh)
            vacc[3] += rowsum8(dh * zz)
            vacc[4] += rowsum8(dh)
            dr[r, :] = d1
            d1 = d1.astype(BF)
            db1[m, r, :] = d1
            vacc[5] += rowsum8(d1.astype(F32))
            dcb = dot_nt(d1, wat[...]).astype(BF)
            dc[r, :] = dcb
            prod = dcb.astype(F32) * c_s[m, r, :].astype(F32)
            hi = prod.astype(BF)
            low = (prod - hi.astype(F32)).astype(BF)
            delta[:, r] = dot_nt(indicator, hi) + dot_nt(indicator, low)
        if not last:
            for cp in norm_copies(m + 1):
                cp.start()
        ins[2].wait()
        if last:
            run_on(0, AFTER_NORM)

        for p in range(HEADS // 2):
            cols = slice(p * 128, (p + 1) * 128)
            kcols = slice(D + p * 128, D + (p + 1) * 128)
            vcols = slice(2 * D + p * 128, 2 * D + (p + 1) * 128)
            q2 = qkv[m, :, cols] * (HEAD_DIM ** -0.5)
            qh = [jnp.where(low_half, q2, query_code), jnp.where(low_half, query_code, q2)]
            dc2 = dc[:, cols]
            dqt = jnp.zeros((128, T), F32)
            for i in range(T // kb):
                r = slice(i * kb, (i + 1) * kb)
                k2 = qkv[m, r, kcols]
                v2 = qkv[m, r, vcols]
                kc = key_code[r]
                dks, dvs = [], []
                for h in range(2):
                    pick = low_half if h == 0 else jnp.logical_not(low_half)
                    kh = jnp.where(low_half, k2, kc) if h == 0 else jnp.where(low_half, kc, k2)
                    pt = jnp.exp(dot_nt(kh, qh[h]) - lse[m, 2 * p + h:2 * p + h + 1, :])
                    dpt = dot_nt(jnp.where(pick, v2, 0), dc2)
                    da = (pt * (dpt - delta[2 * p + h:2 * p + h + 1, :])).astype(BF)
                    dvs.append(dot(pt.astype(BF), dc2))
                    dks.append(dot(da, q2))
                    dqt = dqt + dot_tn(jnp.where(pick, k2, 0), da)
                qkv[m, r, kcols] = jnp.where(low_half, dks[0], dks[1]).astype(BF)
                qkv[m, r, vcols] = jnp.where(low_half, dvs[0], dvs[1]).astype(BF)
            qkv[m, :, cols] = (jnp.transpose(dqt) * (HEAD_DIM ** -0.5)).astype(BF)
            if last:
                run_on(0, AFTER_PAIR[p])
        if m == 0:
            wcp[3].wait()

        def dx_step(i, _):
            r = pl.ds(pl.multiple_of(i * xb, xb), xb)
            dyx[m, r, :] = (dr[r, :] + dot_nt(qkv[m, r, :], wqkv[...])).astype(BF)

            @pl.when(sec != 0)
            def _():
                handoff(m, i).start()
            vacc[6] += rowsum8(qkv[m, r, :D].astype(F32))
            vacc[7] += rowsum8(qkv[m, r, 2 * D:].astype(F32))
            return 0
        lax.fori_loop(0, nx, dx_step, 0)

        @pl.when(sec == 0)
        def _():
            out_copy(m).start()
            dx_copy(m).start()

    run_on(1, SECOND_CATCHES_UP)

    vec = [remote(va.at[i], vb.at[i], s.at[chunks], r.at[chunks], target) for i, (s, r, target) in enumerate(
        ((send_a, recv_a, sibling), (send_b, recv_b, across), (send_c, recv_c, near), (send_d, recv_d, far)))]

    def vec_step(i):
        vec[i].wait_recv()
        total = va[i] + vb[i]
        if i < 3:
            va[i + 1] = total
            vec[i + 1].start()
        else:
            vec_o[...] = total
    va[0] = jnp.concatenate([jnp.sum(vacc[...], axis=1)]
        + [jnp.sum(bacc[:, j * D:(j + 1) * D], axis=0, keepdims=True) for j in range(nj)] + [jnp.zeros((8 - nj, D), F32)], axis=0)
    vec[0].start()
    for step in AT_THE_END.split():
        run(step)

    @pl.when(sec == 0)
    def _():
        pool_copy.wait_recv()
        loss_copy.wait_recv()
        pooled_o[...] = pooled_r[:, :half]
        loss_o[...] = loss_r[...]
        for m in range(M):
            dx_copy(m).wait_send()
            out_copy(m).wait()

    @pl.when(sec != 0)
    def _():
        pool_copy.wait_send()
        loss_copy.wait_send()
        pooled_o[...] = pooled_s[:, half:]
        loss_o[...] = loss_s[...]
        for m in range(M):
            for i in range(nx):
                handoff(m, i).wait_send()
            dx_copy(m).wait_recv()
    for v in vec:
        v.wait_send()
    for k in range(chunks):
        copy_b(k).wait_send()
        if k < nj:
            @pl.when(zlow != k % 2)
            def _():
                copy_c(k).wait_send()

            @pl.when(jnp.logical_and(zlow == k % 2, z != k))
            def _():
                copy_d(k).wait_send()
        else:
            copy_c(k).wait_send()
            copy_d(k).wait_send()


def stack_back(seg, pool, pairs, msgs0, stash, weights, tb=256, xb=128, kb=256):
    x, qkv, lse, c, z1, s12, hb, gp, act, z2 = stash
    wqkv, bq, bv, wat, bat, g1, b1, win, bin_, wout, bout, g2, b2 = weights
    M, T, D = c.shape
    N = M * T
    FF = win.shape[1]
    count = lax.axis_size("dp")
    rows = D // count
    chunks = (4 * D + 2 * FF) // D
    SL = 8
    sds = jax.ShapeDtypeStruct
    out_shape = (sds((16, D), F32), sds((M * SL, D // 2), F32), sds((M * SL, 128), F32), sds((rows, 3 * D), F32), sds((rows, D), F32), sds((rows, FF), F32),
        sds((FF // count, D), F32), sds((M, T, D), BF), sds((M, T, D // 2), BF))
    out_specs = (VM,) * 7 + (ANY, ANY)
    V = pltpu.VMEM
    S = pltpu.SemaphoreType.DMA
    nx = T // xb
    nj = FF // D
    piece = (rows, D)
    scratch = [V((M, T, D), BF), V((D, 3 * D), BF), V((D, D), BF), V((D, FF), BF), V((FF, D), BF),
        V((M, T, 3 * D), BF), V((M, T, D), BF), V((T, D), BF), V((M, T, FF), BF), V((T, D), BF),
        V((T, D), F32), V((T, D), BF), V((16, T), F32), V((M, T, D), BF), V((M, T, D), BF), V((8, 8, D), F32), V((8, FF), F32),
        V((count, 16, D // 2 + 128), BF), V((M * SL, D), F32), V((count * SL, 128), F32), V((count * SL, D), F32), V((M * SL, D), F32), V((M * SL, 128), F32), V((M * SL, D), F32), V((M * SL, 128), F32),
        V((2, N, D), BF), V((2, 2, 2, 2, 2) + piece, BF), V((chunks, 2, 2, 2) + piece, BF), V((chunks, 2, 2) + piece, BF),
        V((chunks, 2) + piece, BF), V((chunks,) + piece, BF), V((2, 2) + piece, BF), V((4, 16, D), F32), V((4, 16, D), F32),
        S((M, 5)), S((4,)), S((2 + nj,)), S((M,)), S((M, nx)), S((M, nx)), S((count - 1,)), S((count - 1,)), S((4,)), S((M, 2))]
    scratch += [S((chunks + 1,)) for _ in range(8)]
    in_specs = (VM,) * 6 + (ANY,) * 12 + (VM, VM)
    return pl.pallas_call(functools.partial(back_kernel, tb, xb, kb), out_shape=out_shape, in_specs=in_specs, out_specs=out_specs,
        scratch_shapes=scratch, compiler_params=pltpu.CompilerParams(vmem_limit_bytes=62 * 2**20, collective_id=3, has_side_effects=True),
        name="stack_back")(seg, pool, pairs, msgs0, lse, s12, z2, gp, z1, c, qkv, hb.reshape(N, D), x.reshape(N, D), act,
            wout, win, wat, wqkv, g1, g2)


def finish_kernel(vec, pooled, loss, g_qkv, g_at, g_in, g_out, dx_h, dxr_h,
    pooled_o, loss_o, gx_o, qkv_o, at_o, in_o, out_o, *rest):
    small, buf, sem = rest[:9], rest[9], rest[10]
    sec = lax.axis_index("section")
    me = lax.axis_index("dp")
    half = buf.shape[2]

    @pl.when(sec == 0)
    def _():
        pltpu.make_async_copy(dx_h.at[:, :, pl.ds(0, half)], buf, sem.at[0]).start()

    @pl.when(sec != 0)
    def _():
        pltpu.make_async_copy(dxr_h, buf, sem.at[0]).start()
    for a, b in ((g_qkv, qkv_o), (g_at, at_o), (g_in, in_o), (g_out, out_o)):
        b[...] = a[...]
    SL = 8
    lane = lax.broadcasted_iota(jnp.int32, (SL, 128), 1) == lax.broadcasted_iota(jnp.int32, (SL, 128), 0)
    for m in range(pooled_o.shape[0]):
        pooled_o[m] = pooled[m * SL:m * SL + SEGS, :]
        loss_o[m:m + 1, :] = jnp.sum(jnp.where(lane, loss[m * SL:(m + 1) * SL, :], 0.0), axis=0, keepdims=True)[:, :SEGS]
    D = vec.shape[1]
    width, wide = small[0].shape[1], small[8].shape[1]
    parts = split3(vec[...])

    def columns(start, size):
        pick = lax.broadcasted_iota(jnp.int32, (D, size), 0) == lax.broadcasted_iota(jnp.int32, (D, size), 1) + start
        pick = jnp.where(pick, 1.0, 0.0).astype(BF)
        return (dot(parts[0], pick) + dot(parts[1], pick)) + dot(parts[2], pick)
    v = columns(me * width, 128)
    for i in range(8):
        small[i][...] = v[i:i + 1, :width]
    per = D // wide
    v = columns(lax.rem(me, per) * wide, 256)
    row = lax.broadcasted_iota(jnp.int32, (16, 256), 0) == 8 + lax.div(me, per)
    small[8][...] = jnp.sum(jnp.where(row, v, 0.0), axis=0, keepdims=True)[:, :wide]
    pltpu.make_async_copy(dxr_h, buf, sem.at[0]).wait()
    gx_o[...] = buf[...].astype(F32)


def finish(vec, pooled, loss, g_qkv, g_at, g_in, g_out, dx, dxr):
    M, T, D = dx.shape
    count = lax.axis_size("dp")
    sds = jax.ShapeDtypeStruct
    f = lambda a: sds(a.shape, F32)
    out_shape = (sds((M, SEGS, D // 2), F32), sds((M, SEGS), F32), sds((M, T, D // 2), F32), f(g_qkv), f(g_at), f(g_in), f(g_out)) + tuple(
        sds((1, D // count), F32) for _ in range(8)) + (sds((1, g_in.shape[1] // count), F32),)
    return pl.pallas_call(finish_kernel, out_shape=out_shape, in_specs=(VM,) * 7 + (ANY,) * 2, out_specs=(VM,) * 16,
        scratch_shapes=[pltpu.VMEM((M, T, D // 2), BF), pltpu.SemaphoreType.DMA((1,))],
        compiler_params=pltpu.CompilerParams(vmem_limit_bytes=VMEM_LIMIT), name="finish")(vec, pooled, loss, g_qkv, g_at, g_in, g_out, dx, dxr)


def contrast_head(pool, seg, pairs, all_pairs):
    M, S = pairs.shape
    D = pool.shape[-1]
    counts = jnp.sum((seg[:, :, None] == jnp.arange(SEGS)).astype(F32), axis=1)[:, :, None]
    pooled = pool[:, :SEGS] / counts
    radius = lax.rsqrt(jnp.sum(pooled * pooled, axis=-1, keepdims=True) + UNIT_EPS)
    unit = (pooled * radius).astype(BF)
    every = lax.all_gather(unit, "dp", axis=1, tiled=True)
    total = every.shape[1]
    start = lax.axis_index("dp") * S
    logits = TEMPER * jnp.einsum("mgd,mkd->mgk", every, every, preferred_element_type=F32)
    cols = jnp.arange(total)
    logits = jnp.where(cols[:, None] == cols[None, :], -MASK_FILL, logits)
    peak = jnp.max(logits, axis=-1, keepdims=True)
    exponent = jnp.exp(logits - peak)
    denom = jnp.sum(exponent, axis=-1, keepdims=True)
    target = cols[None, None, :] == all_pairs[:, :, None]
    loss = peak[..., 0] + jnp.log(denom[..., 0]) - jnp.sum(jnp.where(target, logits, 0.0), axis=-1)
    dl = (exponent / denom - target.astype(F32)).astype(BF)
    rows = lax.dynamic_slice_in_dim(dl, start, S, 1)
    columns = lax.dynamic_slice_in_dim(dl, start, S, 2)
    dn = TEMPER * (jnp.einsum("mgk,mkd->mgd", rows, every, preferred_element_type=F32)
        + jnp.einsum("mkg,mkd->mgd", columns, every, preferred_element_type=F32))
    dp = radius * dn - radius * radius * radius * jnp.sum(pooled * dn, axis=-1, keepdims=True) * pooled
    loss = lax.dynamic_slice_in_dim(loss, start, S, 1)
    return pooled, loss, jnp.pad(dp / counts, ((0, 0), (0, 16 - SEGS), (0, 0)))


def scattered(grads):
    count = lax.axis_size("dp")
    packed = jnp.concatenate([g.reshape(count, -1) for g in grads], axis=1)
    part = lax.psum_scatter(packed, "dp", scatter_dimension=0, tiled=True)[0].astype(F32)
    outs, at = [], 0
    for g in grads:
        size = g.size // count
        outs.append(part[at:at + size].reshape((1, g.shape[0] // count) + g.shape[1:]))
        at += size
    return outs


def swapped(value):
    return lax.ppermute(value, "section", [(0, 1), (1, 0)])


def local(hidden_in, seg_ids, pair_ids, w_qkv, b_query, b_value, w_attn_out, b_attn_out, ln1_gain, ln1_bias, w_in, b_in, w_out, b_out, ln2_gain, ln2_bias):
    M, _, T, D = hidden_in.shape
    sec = lax.axis_index("section")
    first = sec == 0
    weights = (w_qkv[0], b_query, b_value, w_attn_out[0], b_attn_out, ln1_gain, ln1_bias, w_in[0], b_in, w_out[0], b_out, ln2_gain, ln2_bias)
    half = D // 2
    count = lax.axis_size("dp")
    pool, x, qkv, lse, c, z1, s12, hb, gp, act, z2, msgs = stack_fwd(hidden_in[:, 0], seg_ids, pair_ids, weights, count if count == 16 else 0)
    if count == 16:
        parts = stack_back(seg_ids, pool, pair_ids, msgs, (x, qkv, lse, c, z1, s12, hb, gp, act, z2), weights)
        pooled, loss, grad_input, g_qkv, g_at, g_in, g_out, gg2, gb2, gbo, gg1, gb1, gba, gbq, gbv, gbi = finish(*parts)
        pooled_out, loss_out = pooled, loss
        g_qkv, g_at, g_in, g_out = (g[None] for g in (g_qkv, g_at, g_in, g_out))
    else:
        seg = seg_ids[:, 0]
        all_pairs = lax.all_gather(pair_ids, "dp", axis=1, tiled=True)
        pooled, loss, dp = contrast_head(pool, seg, pair_ids, all_pairs)
        vec, dx, dxb, db2, du, db1, dqkv = stack_bwd(seg, dp, (qkv, lse, c, z1, s12, gp, z2), weights)
        act = jnp.moveaxis(act, 0, 1).reshape(M, T, -1)
        big = [jnp.einsum("mta,mtb->ab", a, b, preferred_element_type=F32).astype(BF) for a, b in ((x, dqkv), (c, db1), (hb, du), (act, db2))]
        g_qkv, g_at, g_in, g_out = scattered(big)
        small = scattered([vec[i] for i in range(8)] + [vec[8:8 + w_in.shape[2] // D].reshape(-1)])
        gg2, gb2, gbo, gg1, gb1, gba, gbq, gbv, gbi = small
        kept = lax.dynamic_slice_in_dim(dx, sec * half, half, 2)
        sent = lax.dynamic_slice_in_dim(dxb, (1 - sec) * half, half, 2)
        grad_input = jnp.where(first, kept, swapped(sent).astype(F32))
        pooled_kept = lax.dynamic_slice_in_dim(pooled, sec * half, half, 2)
        pooled_sent = lax.dynamic_slice_in_dim(pooled, (1 - sec) * half, half, 2).astype(BF)
        pooled_out = jnp.where(first, swapped(pooled_sent).astype(F32), pooled_kept)
        loss_out = jnp.where(first, swapped(loss.astype(BF)).astype(F32), loss)
    return (pooled_out, loss_out, grad_input[:, None], g_qkv, gbq, gbv, g_at, gba, gg1, gb1, g_in, gbi, g_out, gbo, gg2, gb2)


def solution(mesh):
    in_specs = (
        P(None, "dp", None, None),
        P(None, "dp", None),
        P(None, "dp"),
        P("section", None, None),
        P("section", None),
        P("section", None),
        P("section", None, None),
        P("section", None),
        P("section", None),
        P("section", None),
        P("section", None, None),
        P("section", None),
        P("section", None, None),
        P("section", None),
        P("section", None),
        P("section", None),
    )
    out_specs = (
        P(None, "dp", "section"),
        P(None, "dp"),
        P(None, "dp", None, "section"),
        P("section", "dp", None),
        P("section", "dp"),
        P("section", "dp"),
        P("section", "dp", None),
        P("section", "dp"),
        P("section", "dp"),
        P("section", "dp"),
        P("section", "dp", None),
        P("section", "dp"),
        P("section", "dp", None),
        P("section", "dp"),
        P("section", "dp"),
        P("section", "dp"),
    )
    return jax.shard_map(local, mesh=mesh, in_specs=in_specs, out_specs=out_specs, check_vma=False)
```

```python
import functools
import jax, jax.numpy as jnp
from jax import lax
from jax.experimental import pallas as pl
from jax.experimental.pallas import tpu as pltpu
from jax.sharding import PartitionSpec as P

HEADS = 12
HEAD_DIM = 64
SEGS = 4
UNIT_EPS = 1e-06
TEMPER = 20.0
MASK_FILL = 1000000000.0
NORM_EPS = 1e-12
BF = jnp.bfloat16
F32 = jnp.float32
VMEM_LIMIT = 60 * 2**20
MESH = pl.DeviceIdType.MESH
ANY = pl.BlockSpec(memory_space=pl.ANY)
VM = pl.BlockSpec(memory_space=pltpu.VMEM)


def dot(a, b):
    return jnp.dot(a, b, preferred_element_type=F32)


def dot_nt(a, b):
    return lax.dot_general(a, b, (((1,), (1,)), ((), ())), preferred_element_type=F32)


def dot_tn(a, b):
    return lax.dot_general(a, b, (((0,), (0,)), ((), ())), preferred_element_type=F32)


def split3(v):
    hi = v.astype(BF)
    rest = v - hi.astype(F32)
    mid = rest.astype(BF)
    low = (rest - mid.astype(F32)).astype(BF)
    return hi, mid, low


def members(seg_row):
    rows = lax.broadcasted_iota(jnp.int32, (16, seg_row.shape[1]), 0)
    return jnp.where(rows == seg_row, 1.0, 0.0).astype(BF)


def normed_rows(rows):
    centre = rows - jnp.mean(rows, axis=-1, keepdims=True)
    scale = lax.rsqrt(jnp.mean(centre * centre, axis=-1, keepdims=True) + NORM_EPS)
    return centre * scale, scale


def gelu_pair(u):
    mag = jnp.abs(u)
    t = 1.0 / (1.0 + (0.3275911 * 0.7071067811865476) * mag)
    e = jnp.exp(-0.5 * (u * u))
    poly = t * (0.127414796 + t * (-0.142248368 + t * (0.7107068705 + t * (-0.7265760135 + t * 0.5307027145))))
    tail = poly * e
    cdf = jnp.where(u >= 0.0, 1.0 - tail, tail)
    return u * cdf, cdf + (u * 0.3989422804014327) * e


def codes(mem):
    lanes = lax.rem(lax.broadcasted_iota(jnp.int32, (16, 128), 1), HEAD_DIM)
    pick = jnp.where(lanes == lax.broadcasted_iota(jnp.int32, (16, 128), 0), 1.0, 0.0)
    pick = jnp.where(lanes < SEGS, pick, 0.0).astype(BF)
    key_code = dot_tn(mem, pick)
    active = jnp.where(lanes[:1] < SEGS, 1.0, 0.0)
    return key_code.astype(BF), ((key_code - active) * MASK_FILL).astype(BF)


def documents(mem, pool):
    counts = jnp.maximum(jnp.sum(mem.astype(F32), axis=1, keepdims=True)[:8], 1.0)
    pooled = pool[:8, :] / counts
    radius = lax.rsqrt(jnp.sum(pooled * pooled, axis=-1, keepdims=True) + UNIT_EPS)
    return pooled, radius, counts


def message(unit, pairs):
    half = unit.shape[1] // 2
    tag = [jnp.broadcast_to(pairs[:, j:j + 1].astype(F32), (1, 128)) for j in range(SEGS)]
    tag = jnp.concatenate(tag + [jnp.zeros((8 - SEGS, 128), F32)], axis=0)
    return jnp.concatenate([jnp.concatenate([unit[:, :half], tag], axis=1), jnp.concatenate([unit[:, half:], tag], axis=1)], axis=0).astype(BF)


def fwd_kernel(tb, fc, peers,
    x_h, seg, pairs, wqkv_h, bq, bv, wat_h, bat, g1, b1, win_h, bin_, wout_h, bout, g2, b2,
    pool_o, x_o, qkv_h, lse_o, c_h, z1_h, s12_o, hb_h, gp_h, act_h, z2_h, msgs_o,
    x_s, wqkv, wat, win, wout, qkv, c_s, hb_s, z1_s, gp_s, act_s, z2_s, y_s, yf, msgs, kcode, qcode,
    insem, wsem, outsem, send_sem, recv_sem, msg_send, msg_recv):
    sec = lax.axis_index("section")
    me = lax.axis_index("dp")
    other = {"section": 1 - sec}
    M, T, D = x_s.shape
    FF = win.shape[1]
    nb = T // tb

    ws = [pltpu.make_async_copy(a, b, wsem.at[i]) for i, (a, b) in enumerate(
        ((wqkv_h, wqkv), (wat_h, wat), (win_h, win), (wout_h, wout)))]
    barrier = pltpu.get_barrier_semaphore()

    @pl.when(sec == 0)
    def _():
        pltpu.make_async_copy(x_h.at[0], x_s.at[0], insem.at[0]).start()
    ws[0].start()
    pl.semaphore_signal(barrier, inc=1, device_id=other, device_id_type=MESH)
    for d in range(1, peers):
        pl.semaphore_signal(barrier, inc=1, device_id={"dp": lax.rem(me + d, peers)}, device_id_type=MESH)
    for w in ws[1:]:
        w.start()

    @pl.when(sec == 0)
    def _():
        for m in range(1, M):
            pltpu.make_async_copy(x_h.at[m], x_s.at[m], insem.at[m]).start()

    lane = lax.broadcasted_iota(jnp.int32, (1, 128), 1)
    low_half = lane < HEAD_DIM

    def block(start):
        return pl.ds(start if isinstance(start, int) else pl.multiple_of(start, tb), tb)

    def out_copies(m, i):
        r = block(i * tb)
        span = block(m * T + i * tb)
        pairs = [(a.at[m, r], b.at[m, r]) for a, b in ((c_s, c_h), (hb_s, hb_h), (z1_s, z1_h), (z2_s, z2_h), (gp_s, gp_h))]
        pairs += [(act_s.at[m, r, j * D:(j + 1) * D], act_h.at[j, span]) for j in range(FF // D)]
        return [pltpu.make_async_copy(a, b, outsem.at[m, i, j]) for j, (a, b) in enumerate(pairs)]

    def whole_copies(m):
        return [pltpu.make_async_copy(a.at[m], b.at[m], outsem.at[m, nb, j]) for j, (a, b) in enumerate(((x_s, x_o), (qkv, qkv_h)))]

    def handoff(m, i):
        r = block(i * tb)
        return pltpu.make_async_remote_copy(src_ref=y_s.at[m, r], dst_ref=x_s.at[m, r], send_sem=send_sem.at[m, i],
            recv_sem=recv_sem.at[m, i], device_id=other, device_id_type=MESH)

    def msg_copy(d):
        return pltpu.make_async_remote_copy(src_ref=msgs.at[me], dst_ref=msgs.at[me], send_sem=msg_send.at[d - 1], recv_sem=msg_recv.at[d - 1],
            device_id={"dp": lax.rem(me + d, peers)}, device_id_type=MESH)

    def micro_step(m, _):
        mem = members(seg[m])
        kcode[...], qcode[...] = codes(mem)

        @pl.when(sec == 0)
        def _():
            pltpu.make_async_copy(x_h.at[m], x_s.at[m], insem.at[m]).wait()

        @pl.when(m == 0)
        def _():
            ws[0].wait()

        @pl.when(sec != 0)
        def _():
            for i in range(nb):
                handoff(m, i).wait_recv()
        xi = x_s[m]
        for j, b in ((0, bq), (1, None), (2, bv)):
            cols = slice(j * D, (j + 1) * D)
            v = dot(xi, wqkv[:, cols])
            if b is not None:
                v = v + b[...].astype(F32)
            qkv[m, :, cols] = v.astype(BF)
        for cp in whole_copies(m):
            cp.start()
        ones = jnp.ones((T, 128), BF)
        def block_step(i, _):
            r = block(i * tb)
            key_code = kcode[...]
            qc = qcode[r, :]
            lses = jnp.zeros((tb, 128), F32)
            for p in range(HEADS // 2):
                cols = slice(p * 128, (p + 1) * 128)
                k2 = qkv[m, :, D + p * 128:D + (p + 1) * 128]
                v2 = jnp.concatenate([qkv[m, :, 2 * D + p * 128:2 * D + (p + 1) * 128], ones], axis=1)
                q2 = qkv[m, r, cols] * (HEAD_DIM ** -0.5)
                halves = []
                for h in range(2):
                    if h == 0:
                        s = dot_nt(jnp.where(low_half, q2, qc), jnp.where(low_half, k2, key_code))
                    else:
                        s = dot_nt(jnp.where(low_half, qc, q2), jnp.where(low_half, key_code, k2))
                    mx = jnp.max(s, axis=-1, keepdims=True)
                    e = jnp.exp(s - mx).astype(BF)
                    c = dot(e, v2)
                    l = c[:, 128:]
                    halves.append(c[:, :128] / l)
                    lses = jnp.where(lane == 2 * p + h, mx + jnp.log(l), lses)
                c_s[m, r, cols] = jnp.where(low_half, halves[0], halves[1]).astype(BF)
            lse_o[m, :, r] = jnp.transpose(lses)[:16, :]

            @pl.when(jnp.logical_and(m == 0, i == 0))
            def _():
                for w in ws[1:]:
                    w.wait()
                pl.semaphore_wait(barrier, max(peers, 1))
            r1 = x_s[m, r, :].astype(F32) + dot(c_s[m, r, :], wat[...]) + bat[...].astype(F32)
            z, scale = normed_rows(r1)
            acc = z * g1[...].astype(F32) + b1[...].astype(F32)
            hi = acc.astype(BF)
            hb_s[m, r, :] = hi
            z1_s[m, r, :] = z.astype(BF)
            s12_o[m, r, 0:1] = scale
            acc = acc + bout[...].astype(F32)
            nj = FF // fc
            us = [dot(hi, win[:, :fc])]
            for j in range(nj):
                cols = slice(j * fc, (j + 1) * fc)
                if j + 1 < nj:
                    us.append(dot(hi, win[:, (j + 1) * fc:(j + 2) * fc]))
                f, gp = gelu_pair(us[j] + bin_[:, cols].astype(F32))
                f = f.astype(BF)
                act_s[m, r, cols] = f
                gp_s[m, r, cols] = gp.astype(BF)
                acc = acc + dot(f, wout[cols, :])
            z, scale = normed_rows(acc)
            y = z * g2[...].astype(F32) + b2[...].astype(F32)
            y_s[m, r, :] = y.astype(BF)

            @pl.when(sec == 0)
            def _():
                handoff(m, i).start()
            z2_s[m, r, :] = z.astype(BF)
            s12_o[m, r, 1:2] = scale
            yf[r, :] = y
            for cp in out_copies(m, i):
                cp.start()
            return 0
        lax.fori_loop(0, nb, block_step, 0)

        @pl.when(sec != 0)
        def _():
            hi, mid, low = split3(yf[...])
            pool = (dot(mem, hi) + dot(mem, mid)) + dot(mem, low)
            pool_o[m] = pool
            if peers:
                @pl.when(m == 0)
                def _():
                    pooled, radius, _ = documents(mem, pool)
                    msgs[me] = message(pooled * radius, pairs[0:1, :])
                    for d in range(1, peers):
                        msg_copy(d).start()
        return 0
    lax.fori_loop(0, M, micro_step, 0)

    @pl.when(sec == 0)
    def _():
        pool_o[...] = jnp.zeros_like(pool_o)
        msgs_o[...] = jnp.zeros_like(msgs_o)

    if peers:
        @pl.when(sec != 0)
        def _():
            for d in range(1, peers):
                msg_copy(d).wait()
            msgs_o[...] = msgs[...]
    for m in range(M):
        for cp in whole_copies(m):
            cp.wait()
        for i in range(nb):
            for cp in out_copies(m, i):
                cp.wait()

    @pl.when(sec == 0)
    def _():
        for m in range(M):
            for i in range(nb):
                handoff(m, i).wait_send()


def stack_fwd(x, seg, pairs, weights, peers, tb=256, fc=768):
    M, T, D = x.shape
    FF = weights[7].shape[1]
    sds = jax.ShapeDtypeStruct
    out_shape = (sds((M, 16, D), F32), sds((M, T, D), BF), sds((M, T, 3 * D), BF), sds((M, 16, T), F32), sds((M, T, D), BF),
        sds((M, T, D), BF), sds((M, T, 2), F32), sds((M, T, D), BF), sds((M, T, FF), BF), sds((FF // D, M * T, D), BF), sds((M, T, D), BF), sds((max(peers, 1), 16, D // 2 + 128), BF))
    out_specs = (VM, ANY, ANY, VM, ANY, ANY, VM, ANY, ANY, ANY, ANY, VM)
    V = pltpu.VMEM
    S = pltpu.SemaphoreType.DMA
    nb = T // tb
    scratch = [V((M, T, D), BF), V((D, 3 * D), BF), V((D, D), BF), V((D, FF), BF), V((FF, D), BF), V((M, T, 3 * D), BF),
        V((M, T, D), BF), V((M, T, D), BF), V((M, T, D), BF), V((M, T, FF), BF), V((M, T, FF), BF), V((M, T, D), BF), V((M, T, D), BF),
        V((T, D), F32), V((max(peers, 1), 16, D // 2 + 128), BF), V((T, 128), BF), V((T, 128), BF), S((M,)), S((4,)), S((M, nb + 1, 5 + FF // D)), S((M, nb)), S((M, nb)),
        S((max(peers, 2) - 1,)), S((max(peers, 2) - 1,))]
    in_specs = (ANY, VM, VM, ANY, VM, VM, ANY, VM, VM, VM, ANY, VM, ANY, VM, VM, VM)
    return pl.pallas_call(functools.partial(fwd_kernel, tb, fc, peers), out_shape=out_shape, in_specs=in_specs, out_specs=out_specs,
        scratch_shapes=scratch, compiler_params=pltpu.CompilerParams(vmem_limit_bytes=VMEM_LIMIT, collective_id=0, has_side_effects=True),
        name="stack_fwd")(x, seg, pairs, *weights)


def rowsum8(v):
    return jnp.sum(v.reshape(v.shape[0] // 8, 8, v.shape[1]), axis=0)


def bwd_kernel(tb, fc, kb,
    seg, dp, lse, s12, qkv_h, c_h, z1_h, gp_h, z2_h, wqkv_h, wat_h, g1, win_h, wout_h, g2,
    vec_o, dx_h, dxb_h, db2_h, du_h, db1_h, dqkv_h,
    dyr, wqkv, wat, win, wout, qkv, c_s, z1, gp, z2, bias, dy_s, dr1, dc, delta, du, db2, db1, dqkv, dx, dxb, vacc, bacc,
    insem, wsem, outsem, send_sem, recv_sem):
    sec = lax.axis_index("section")
    other = {"section": 1 - sec}
    M, T, D = c_s.shape
    FF = win.shape[1]
    nb = T // tb

    ws = [pltpu.make_async_copy(a, b, wsem.at[i]) for i, (a, b) in enumerate(
        ((wout_h, wout), (win_h, win), (wat_h, wat), (wqkv_h, wqkv)))]

    def in_copies(m):
        pairs = [(z2_h, z2), (gp_h, gp), (z1_h, z1), (c_h, c_s), (qkv_h, qkv)]
        return [pltpu.make_async_copy(a.at[m], b.at[m], insem.at[m, i]) for i, (a, b) in enumerate(pairs)]
    first = in_copies(0)
    first[0].start()
    ws[0].start()
    barrier = pltpu.get_barrier_semaphore()
    pl.semaphore_signal(barrier, inc=1, device_id=other, device_id_type=MESH)
    for a, b in zip(first[1:], ws[1:]):
        a.start()
        b.start()
    first[4].start()
    for m in range(1, M):
        for a in in_copies(m):
            a.start()
    vacc[...] = jnp.zeros_like(vacc)
    bacc[...] = jnp.zeros_like(bacc)
    pl.semaphore_wait(barrier, 1)

    lane = lax.broadcasted_iota(jnp.int32, (1, 128), 1)
    low_half = lane < HEAD_DIM
    indicator = jnp.where(lax.broadcasted_iota(jnp.int32, (16, D), 1) // HEAD_DIM == lax.broadcasted_iota(jnp.int32, (16, D), 0), 1.0, 0.0).astype(BF)

    def out_copies(m):
        pairs = [(db2, db2_h), (du, du_h), (db1, db1_h), (dqkv, dqkv_h), (dx, dx_h), (dxb, dxb_h)]
        return [pltpu.make_async_copy(a.at[m], b.at[m], outsem.at[m, i]) for i, (a, b) in enumerate(pairs)]

    def handoff(m, i):
        r = pl.ds(i * tb if isinstance(i, int) else pl.multiple_of(i * tb, tb), tb)
        return pltpu.make_async_remote_copy(src_ref=dxb.at[m, r], dst_ref=dyr.at[m, r], send_sem=send_sem.at[m, i],
            recv_sem=recv_sem.at[m, i], device_id=other, device_id_type=MESH)

    def norm_pull(z, scale, gain, dy):
        g = dy * gain
        return scale * (g - jnp.mean(g, axis=-1, keepdims=True) - z * jnp.mean(g * z, axis=-1, keepdims=True))

    def micro_step(m, _):
        ins = in_copies(m)
        outs = out_copies(m)
        mem = members(seg[pl.ds(m, 1), :])
        bias[...] = (dot_tn(mem, mem) - 1.0) * MASK_FILL
        dp3 = jnp.concatenate(split3(dp[m]), axis=0)

        @pl.when(sec == 0)
        def _():
            for i in range(nb):
                handoff(m, i).wait_recv()

        @pl.when(m == 0)
        def _():
            ws[0].wait()
            ws[1].wait()
            ws[2].wait()
        for a in ins[:4]:
            a.wait()

        def tok_step(i, _):
            r = pl.ds(pl.multiple_of(i * tb, tb), tb)

            @pl.when(sec == 0)
            def _():
                dy_s[...] = dyr[m, r, :].astype(F32)

            @pl.when(sec != 0)
            def _():
                blk = members(seg[pl.ds(m, 1), r])
                dy_s[...] = dot_tn(jnp.concatenate([blk, blk, blk], axis=0), dp3)
            dy = dy_s[...]
            z = z2[m, r, :].astype(F32)
            dr2 = norm_pull(z, s12[m, r, 1:2], g2[...].astype(F32), dy)
            vacc[0] += rowsum8(dy * z)
            vacc[1] += rowsum8(dy)
            d2 = dr2.astype(BF)
            db2[m, r, :] = d2
            vacc[2] += rowsum8(d2.astype(F32))
            dh = dr2
            nj = FF // fc
            dfs = [dot_nt(d2, wout[:fc, :])]
            for j in range(nj):
                cols = slice(j * fc, (j + 1) * fc)
                if j + 1 < nj:
                    dfs.append(dot_nt(d2, wout[(j + 1) * fc:(j + 2) * fc, :]))
                dub = (dfs[j] * gp[m, r, cols].astype(F32)).astype(BF)
                du[m, r, cols] = dub
                bacc[:, cols] += rowsum8(dub.astype(F32))
                dh = dh + dot_nt(dub, win[:, cols])
            z = z1[m, r, :].astype(F32)
            d1 = norm_pull(z, s12[m, r, 0:1], g1[...].astype(F32), dh)
            vacc[3] += rowsum8(dh * z)
            vacc[4] += rowsum8(dh)
            dr1[r, :] = d1
            d1 = d1.astype(BF)
            db1[m, r, :] = d1
            vacc[5] += rowsum8(d1.astype(F32))
            dcb = dot_nt(d1, wat[...]).astype(BF)
            dc[r, :] = dcb
            prod = dcb.astype(F32) * c_s[m, r, :].astype(F32)
            hi = prod.astype(BF)
            low = (prod - hi.astype(F32)).astype(BF)
            delta[:, r] = dot_nt(indicator, hi) + dot_nt(indicator, low)
            return 0
        lax.fori_loop(0, nb, tok_step, 0)
        for o in outs[:3]:
            o.start()
        ins[4].wait()

        def att_step(p, _):
            cols = pl.ds(pl.multiple_of(p * 128, 128), 128)
            kcols = pl.ds(pl.multiple_of(p * 128 + D, 128), 128)
            vcols = pl.ds(pl.multiple_of(p * 128 + 2 * D, 128), 128)
            q2 = qkv[m, :, cols] * (HEAD_DIM ** -0.5)
            dc2 = dc[:, cols]
            dqt = jnp.zeros((128, T), F32)
            for i in range(T // kb):
                rows = slice(i * kb, (i + 1) * kb)
                k2 = qkv[m, rows, kcols]
                v2 = qkv[m, rows, vcols]
                dks, dvs = [], []
                for h in range(2):
                    pick = low_half if h == 0 else jnp.logical_not(low_half)
                    kh = jnp.where(pick, k2, 0)
                    vh = jnp.where(pick, v2, 0)
                    st = dot_nt(kh, q2) + bias[rows, :]
                    pt = jnp.exp(st - lse[m, pl.ds(2 * p + h, 1), :])
                    dpt = dot_nt(vh, dc2)
                    da = (pt * (dpt - delta[pl.ds(2 * p + h, 1), :])).astype(BF)
                    dvs.append(dot(pt.astype(BF), dc2))
                    dks.append(dot(da, q2))
                    dqt = dqt + dot_tn(kh, da)
                dqkv[m, rows, kcols] = jnp.where(low_half, dks[0], dks[1]).astype(BF)
                dqkv[m, rows, vcols] = jnp.where(low_half, dvs[0], dvs[1]).astype(BF)
            dqkv[m, :, cols] = (jnp.transpose(dqt) * (HEAD_DIM ** -0.5)).astype(BF)
            return 0
        lax.fori_loop(0, HEADS // 2, att_step, 0)
        outs[3].start()

        @pl.when(m == 0)
        def _():
            ws[3].wait()

        def dx_step(i, _):
            r = pl.ds(pl.multiple_of(i * tb, tb), tb)
            v = dr1[r, :] + dot_nt(dqkv[m, r, :], wqkv[...])
            dx[m, r, :] = v
            dxb[m, r, :] = v.astype(BF)
            vacc[6] += rowsum8(dqkv[m, r, :D].astype(F32))
            vacc[7] += rowsum8(dqkv[m, r, 2 * D:].astype(F32))

            @pl.when(sec != 0)
            def _():
                handoff(m, i).start()
            return 0
        lax.fori_loop(0, nb, dx_step, 0)
        outs[4].start()
        outs[5].start()
        return 0
    lax.fori_loop(0, M, micro_step, 0)
    vec_o[...] = jnp.concatenate([jnp.sum(vacc[...], axis=1)]
        + [jnp.sum(bacc[:, j * D:(j + 1) * D], axis=0, keepdims=True) for j in range(FF // D)] + [jnp.zeros((4, D), F32)], axis=0)
    for m in range(M):
        for o in out_copies(m):
            o.wait()

    @pl.when(sec != 0)
    def _():
        for m in range(M):
            for i in range(nb):
                handoff(m, i).wait_send()


def stack_bwd(seg, dp, stash, weights, tb=256, fc=768, kb=256):
    qkv, lse, c, z1, s12, gp, z2 = stash
    wqkv, bq, bv, wat, bat, g1, b1, win, bin_, wout, bout, g2, b2 = weights
    M, T, D = c.shape
    FF = win.shape[1]
    sds = jax.ShapeDtypeStruct
    out_shape = (sds((16, D), F32), sds((M, T, D), F32), sds((M, T, D), BF), sds((M, T, D), BF), sds((M, T, FF), BF), sds((M, T, D), BF), sds((M, T, 3 * D), BF))
    out_specs = (VM, ANY, ANY, ANY, ANY, ANY, ANY)
    V = pltpu.VMEM
    S = pltpu.SemaphoreType.DMA
    nb = T // tb
    scratch = [V((M, T, D), BF), V((D, 3 * D), BF), V((D, D), BF), V((D, FF), BF), V((FF, D), BF),
        V((M, T, 3 * D), BF), V((M, T, D), BF), V((M, T, D), BF), V((M, T, FF), BF), V((M, T, D), BF),
        V((T, T), F32), V((tb, D), F32), V((T, D), F32), V((T, D), BF), V((16, T), F32),
        V((M, T, FF), BF), V((M, T, D), BF), V((M, T, D), BF), V((M, T, 3 * D), BF), V((M, T, D), F32), V((M, T, D), BF),
        V((8, 8, D), F32), V((8, FF), F32), S((M, 5)), S((4,)), S((M, 6)), S((M, nb)), S((M, nb))]
    in_specs = (VM, VM, VM, VM, ANY, ANY, ANY, ANY, ANY, ANY, ANY, VM, ANY, ANY, VM)
    return pl.pallas_call(functools.partial(bwd_kernel, tb, fc, kb), out_shape=out_shape, in_specs=in_specs, out_specs=out_specs,
        scratch_shapes=scratch, compiler_params=pltpu.CompilerParams(vmem_limit_bytes=VMEM_LIMIT, collective_id=1, has_side_effects=True),
        name="stack_bwd")(seg, dp, lse, s12, qkv, c, z1, gp, z2, wqkv, wat, g1, win, wout, g2)


AFTER_TOKENS = (" ".join(("a2 a3 b0",)), " ".join(("b1",)))
AFTER_W = ("", " ".join(("a4 c0",)), " ".join(("a5 b2",)), " ".join(("a6 c1",)))
AFTER_A = " ".join(("b3",))
AFTER_PAIR = (" ".join(("a7",)), " ".join(("a8 c2",)), " ".join(("b4",)), "", " ".join(("c3",)), "")
BEFORE_Q = " ".join(("b5 b8",))
AFTER_Q = ("", " ".join(("v0 a9 c4 b6",)), "")
AT_THE_END = " ".join(("v1 a10 c5 d3", "b7 a11 c8 d4", "c6 b9 d5 c7", "v2 b10 d6 c9", "v3 d7 b11 c10", "d8 d9 c11 d10", "d11",))


def back_kernel(tb, xb, kb,
    seg, pool, pairs, msgs0, lse, s12, z2_h, gp_h, z1_h, c_h, qkv_h, hb_h, x_h, act_h, wout_h, win_h, wat_h, wqkv_h, g1, g2,
    vec_o, pooled_o, loss_o, g_qkv, g_at, g_in, g_out, dx_o, dxr_o,
    dyx, wqkv, wat, win, wout, qkv, c_s, z1, gp, z2, dr, dc, delta, db2, db1, vacc, bacc,
    msgs, dps, loss_w, dn_s, pooled_s, loss_s, pooled_r, loss_r, kcode, qcode, gathered, rhs, part, got_a, got_b, got_c, got_d, got_t, va, vb,
    insem, wsem, latesem, outsem, send_sem, recv_sem, msg_send, msg_recv, pool_sem, dx_sem,
    send_a, recv_a, send_b, recv_b, send_c, recv_c, send_d, recv_d):
    sec = lax.axis_index("section")
    me = lax.axis_index("dp")
    peers = msgs.shape[0]
    core = lax.rem(me, 2)
    y = lax.rem(lax.div(me, 2), 2)
    z = lax.div(me, 4)
    zlow = lax.rem(z, 2)
    zhigh = lax.div(z, 2)
    other = {"section": 1 - sec}
    sibling = {"dp": me + 1 - 2 * core}
    across = {"dp": me + 2 - 4 * y}
    near = {"dp": me + 4 - 8 * zlow}
    far = {"dp": me + 8 - 16 * zhigh}

    def remote(src, dst, ss, rs, target):
        return pltpu.make_async_remote_copy(src_ref=src, dst_ref=dst, send_sem=ss, recv_sem=rs, device_id=target, device_id_type=MESH)
    M, T, D = c_s.shape
    N = M * T
    FF = gp.shape[2]
    half = D // 2
    nb = T // tb
    nx = T // xb
    nj = FF // D
    chunks = got_a.shape[0]
    rows = got_a.shape[4]
    SL = 8
    zchunk = 2 * nj

    wcp = [pltpu.make_async_copy(a, b, wsem.at[i]) for i, (a, b) in enumerate(
        ((wout_h, wout), (win_h, win), (wat_h, wat), (wqkv_h, wqkv)))]

    def norm_copies(m):
        return [pltpu.make_async_copy(a.at[m], b, insem.at[m, i]) for i, (a, b) in enumerate(((z2_h, z2), (z1_h, z1)))]

    def in_copies(m):
        return [pltpu.make_async_copy(a.at[m], b.at[m], insem.at[m, 2 + i]) for i, (a, b) in enumerate(((gp_h, gp), (c_h, c_s), (qkv_h, qkv)))]

    def act_copy(t):
        return pltpu.make_async_copy(act_h.at[t], rhs.at[t % 2 if isinstance(t, int) else lax.rem(t, 2)], latesem.at[t])
    hb_copy = pltpu.make_async_copy(hb_h, rhs.at[0], latesem.at[nj])
    x_copy = pltpu.make_async_copy(x_h, rhs.at[1], latesem.at[nj + 1])
    norms = norm_copies(0)
    ins = in_copies(0)
    norms[0].start()
    wcp[0].start()
    barrier = pltpu.get_barrier_semaphore()
    pl.semaphore_signal(barrier, inc=1, device_id=other, device_id_type=MESH)
    for d in range(1, peers):
        pl.semaphore_signal(barrier, inc=1, device_id={"dp": lax.rem(me + d, peers)}, device_id_type=MESH)
    for a in [ins[0], wcp[1], norms[1], wcp[2], ins[1], ins[2], wcp[3]]:
        a.start()
    for m in range(1, M):
        for a in in_copies(m):
            a.start()
    act_copy(0).start()
    act_copy(1).start()
    vacc[...] = jnp.zeros_like(vacc)
    bacc[...] = jnp.zeros_like(bacc)

    def msg_copy(d):
        return remote(msgs.at[me], msgs.at[me], msg_send.at[d - 1], msg_recv.at[d - 1], {"dp": lax.rem(me + d, peers)})
    pool_copy = remote(pooled_s, pooled_r, pool_sem.at[0], pool_sem.at[1], other)
    loss_copy = remote(loss_s, loss_r, pool_sem.at[2], pool_sem.at[3], other)
    pl.semaphore_wait(barrier, peers)

    def head(m):
        eight = pl.ds(pl.multiple_of(m * SL, SL), SL)
        pooled, radius, counts = documents(members(seg[m]), pool[m])
        G = peers * SL
        lo = gathered[:, :SL, :half].astype(F32).reshape(G, half).astype(BF)
        hi = gathered[:, SL:, :half].astype(F32).reshape(G, half).astype(BF)
        partner = gathered[:, :SL, half:].astype(F32).reshape(G, 128)
        rid = lax.broadcasted_iota(jnp.int32, (G, G), 0)
        cid = lax.broadcasted_iota(jnp.int32, (G, G), 1)
        held = jnp.logical_and(lax.rem(rid, SL) < SEGS, lax.rem(cid, SL) < SEGS)
        logits = TEMPER * (dot_nt(lo, lo) + dot_nt(hi, hi))
        logits = jnp.where(jnp.logical_and(held, rid != cid), logits, -MASK_FILL)
        peak = jnp.max(logits, axis=-1, keepdims=True)
        exponent = jnp.exp(logits - peak)
        denom = jnp.sum(exponent, axis=-1, keepdims=True)
        doc = (lax.div(cid, SL) * SEGS + lax.rem(cid, SL)).astype(F32)
        target = jnp.where(jnp.logical_and(held, doc == partner[:, :1]), 1.0, 0.0)
        loss = peak + jnp.log(denom) - jnp.sum(target * logits, axis=-1, keepdims=True)
        dl = jnp.where(held, exponent / denom - target, 0.0).astype(BF)
        own = pl.ds(pl.multiple_of(me * SL, SL), SL)
        for side, part_of in ((0, lo), (1, hi)):
            dn_s[:, side * half:(side + 1) * half] = TEMPER * (dot(dl, part_of) + dot_tn(dl, part_of))
        dn = dn_s[own, :]
        loss_w[...] = jnp.broadcast_to(loss, (G, 128))
        loss_s[eight, :] = loss_w[own, :]
        dps[eight, :] = (radius * dn - radius * radius * radius * jnp.sum(pooled * dn, axis=-1, keepdims=True) * pooled) / counts

    @pl.when(sec != 0)
    def _():
        for m in range(M):
            pooled, radius, _ = documents(members(seg[m]), pool[m])
            pooled_s[m * SL:(m + 1) * SL, :] = pooled
            if m == 1:
                msgs[me] = message(pooled * radius, pairs[m:m + 1, :])
        for d in range(1, peers):
            msg_copy(d).start()
        pool_copy.start()

    lane = lax.broadcasted_iota(jnp.int32, (1, 128), 1)
    low_half = lane < HEAD_DIM
    indicator = jnp.where(lax.broadcasted_iota(jnp.int32, (16, D), 1) // HEAD_DIM == lax.broadcasted_iota(jnp.int32, (16, D), 0), 1.0, 0.0).astype(BF)

    def out_copy(m):
        return pltpu.make_async_copy(dyx.at[m], dx_o.at[m], outsem.at[m])

    def handoff(m, i):
        r = pl.ds(i * xb if isinstance(i, int) else pl.multiple_of(i * xb, xb), xb)
        return remote(dyx.at[m, r], dyx.at[m, r], send_sem.at[m, i], recv_sem.at[m, i], other)

    def dx_copy(m):
        return remote(dyx.at[m, :, half:], dxr_o.at[m], dx_sem.at[m, 0], dx_sem.at[m, 1], other)

    def norm_pull(zz, scale, gain, dy):
        g = dy * gain
        return scale * (g - jnp.mean(g, axis=-1, keepdims=True) - zz * jnp.mean(g * zz, axis=-1, keepdims=True))

    def slot(k):
        return k % 2 if isinstance(k, int) else lax.rem(k, 2)

    def copy_a(k):
        return remote(part.at[slot(k), :, :, :, 1 - core], got_a.at[k], send_a.at[k], recv_a.at[k], sibling)

    def copy_b(k):
        if not isinstance(k, int) or k != zchunk:
            return remote(got_a.at[k, :, :, 1 - y], got_b.at[k], send_b.at[k], recv_b.at[k], across)
        return remote(got_a.at[k, zhigh, zlow, 1 - y], got_d.at[k], send_b.at[k], recv_b.at[k], across)

    def copy_c(k):
        if k < nj:
            return remote(got_b.at[k], got_c.at[pl.ds(2 * (k // 2), 2)], send_c.at[k], recv_c.at[k], near)
        if k == zchunk:
            return remote(got_a.at[k, :, 1 - zlow], got_b.at[k], send_c.at[k], recv_c.at[k], near)
        return remote(got_b.at[k, :, 1 - zlow], got_c.at[k], send_c.at[k], recv_c.at[k], near)

    def copy_d(k):
        if not isinstance(k, int) or k < nj:
            return remote(got_b.at[k], got_t, send_d.at[k], recv_d.at[k], far)
        if k == zchunk:
            return remote(got_a.at[k, 1 - zhigh, zlow], got_c.at[k], send_d.at[k], recv_d.at[k], far)
        return remote(got_b.at[k, 1 - zhigh, zlow], got_d.at[k], send_d.at[k], recv_d.at[k], far)

    def e1(k):
        copy_a(k).wait_recv()

        for h in range(2):
            got_a[k, h] = got_a[k, h] + part[slot(k), h, :, :, core]
        if isinstance(k, int) and k == zchunk:
            copy_c(k).start()
        else:
            copy_b(k).start()
        copy_a(k).wait_send()

    def e2(k):
        if k == zchunk:
            copy_c(k).wait_recv()
            for h in range(2):
                got_a[k, h, zlow] = got_a[k, h, zlow] + got_b[k, h]
            copy_d(k).start()
            return
        copy_b(k).wait_recv()
        for h in range(2):
            got_b[k, h] = got_b[k, h] + got_a[k, h, :, y]
        if k < nj:
            @pl.when(zlow != k % 2)
            def _():
                copy_c(k).start()
        else:
            copy_c(k).start()

    def e3(k):
        if k < nj:
            @pl.when(zlow == k % 2)
            def _():
                copy_c(k).wait_recv()
                for h in range(2):
                    got_b[k, h] = got_b[k, h] + got_c[2 * (k // 2) + h]

                @pl.when(z != k)
                def _():
                    copy_d(k).start()
        elif k == zchunk:
            copy_d(k).wait_recv()
            got_a[k, zhigh, zlow] = got_a[k, zhigh, zlow] + got_c[k]
            copy_b(k).start()
        else:
            copy_c(k).wait_recv()
            for h in range(2):
                got_b[k, h, zlow] = got_b[k, h, zlow] + got_c[k, h]
            copy_d(k).start()

    def e4(k):
        if k == zchunk:
            copy_b(k).wait_recv()
            return got_a[k, zhigh, zlow, y].astype(F32) + got_d[k].astype(F32)
        copy_d(k).wait_recv()
        return got_b[k, zhigh, zlow].astype(F32) + got_d[k].astype(F32)

    def tile_out(k, lhs, right):
        def side(i, _):
            cols = pl.ds(pl.multiple_of(i * half, half), half)
            v = dot_tn(lhs[:, cols], right)
            part[slot(k), i] = v.astype(BF).reshape(part.shape[2:])
            return 0
        lax.fori_loop(0, 2, side, 0)
        copy_a(k).start()

    def products_t():
        def one(t, _):
            act_copy(t).wait()

            def side(i, _):
                cols = pl.ds(pl.multiple_of(i * half, half), half)
                v = dot_tn(rhs[lax.rem(t, 2), :, cols], db2[...].reshape(N, D)).astype(BF)
                for c in range(2):
                    for s in range(4):
                        part[slot(t), s // 2, s % 2, i, c] = v[(c * 4 + s) * rows:(c * 4 + s + 1) * rows]
                return 0
            lax.fori_loop(0, 2, side, 0)
            copy_a(t).start()

            @pl.when(t < nj - 2)
            def _():
                act_copy(t + 2).start()

            @pl.when(t == nj - 2)
            def _():
                hb_copy.start()

            @pl.when(t == nj - 1)
            def _():
                x_copy.start()

            @pl.when(jnp.logical_and(t >= 1, t <= 2))
            def _():
                e1(t - 1)
            return 0
        lax.fori_loop(0, nj, one, 0)

    def products_w():
        hb_copy.wait()

        def one(j, _):
            tile_out(nj + j, rhs.at[0], gp[:, :, pl.ds(pl.multiple_of(j * D, D), D)].reshape(N, D))
            for n, steps in enumerate(AFTER_W):
                if steps:
                    run_when(j == n, steps)
            return 0
        lax.fori_loop(0, nj, one, 0)

        def side(i, _):
            cols = pl.ds(pl.multiple_of(i * half, half), half)
            v = dot_tn(c_s[:, :, cols].reshape(N, half), db1[...].reshape(N, D))
            part[slot(2 * nj), i] = v.astype(BF).reshape(part.shape[2:])
            return 0
        lax.fori_loop(0, 2, side, 0)
        copy_a(2 * nj).start()
        for step in AFTER_A.split():
            run(step)

    def products_q():
        x_copy.wait()

        def one(j, _):
            tile_out(2 * nj + 1 + j, rhs.at[1], qkv[:, :, pl.ds(pl.multiple_of(j * D, D), D)].reshape(N, D))
            for n, steps in enumerate(AFTER_Q):
                if steps:
                    run_when(j == n, steps)
            return 0
        lax.fori_loop(0, 3, one, 0)

    def store(k):
        v = e4(k)
        if k < 2 * nj:
            g_in[:, (k - nj) * D:(k - nj + 1) * D] = v
        elif k == 2 * nj:
            g_at[...] = v
        else:
            g_qkv[:, (k - 2 * nj - 1) * D:(k - 2 * nj) * D] = v

    def store_w_out():
        copy_d(z).wait_recv()
        for s in range(4):
            g_out[s * rows:(s + 1) * rows, :] = got_b[z, s // 2, s % 2].astype(F32) + got_t[s // 2, s % 2].astype(F32)

    def run(step):
        what, k = step[0], int(step[1:])
        if what == "v":
            vec_step(k)
        elif what == "d":
            if k >= nj:
                store(k)
            elif k == nj - 1:
                store_w_out()
        else:
            {"a": e1, "b": e2, "c": e3}[what](k)

    def run_when(where, steps):
        @pl.when(where)
        def _():
            for step in steps.split():
                run(step)

    def one_pass(step, _):
        m = jnp.minimum(step, M - 1)
        norms = norm_copies(m)
        ins = in_copies(m)
        forming = jnp.logical_or(jnp.logical_and(step == M - 1, sec == 0), jnp.logical_and(step == M, sec != 0))
        behind = jnp.logical_and(step == M, sec != 0)

        @pl.when(step < M)
        def _():
            norm_pass(m, norms)

        @pl.when(forming)
        def _():
            products_t()

        @pl.when(step < M)
        def _():
            token_pass(m, norms, ins)

        @pl.when(forming)
        def _():
            run_when(behind, " ".join(AFTER_TOKENS))
            products_w()
            run_when(behind, " ".join(AFTER_PAIR))

        @pl.when(step < M)
        def _():
            attention_pass(m)
        return 0

    def norm_pass(m, norms):
        norms = norm_copies(m)
        ins = in_copies(m)
        mem = members(seg[m])
        kcode[...], qcode[...] = codes(mem)
        norms[0].wait()

        @pl.when(sec != 0)
        def _():
            @pl.when(m == 0)
            def _():
                gathered[...] = msgs0[...]

            @pl.when(m == 1)
            def _():
                for d in range(1, peers):
                    msg_copy(d).wait()
                gathered[...] = msgs[...]
            head(m)

            @pl.when(m == M - 1)
            def _():
                loss_copy.start()

        def norm_rows(r):
            dy = dr[r, :]
            zz = z2[r, :].astype(F32)
            dr2 = norm_pull(zz, s12[m, r, 1:2], g2[...].astype(F32), dy)
            vacc[0] += rowsum8(dy * zz)
            vacc[1] += rowsum8(dy)
            d2 = dr2.astype(BF)
            dr[r, :] = dr2
            db2[m, r, :] = d2
            vacc[2] += rowsum8(d2.astype(F32))

        @pl.when(sec == 0)
        def _():
            def norm_step(i, _):
                r = pl.ds(pl.multiple_of(i * xb, xb), xb)
                handoff(m, i).wait_recv()
                dr[r, :] = dyx[m, r, :].astype(F32)
                norm_rows(r)
                return 0
            lax.fori_loop(0, nx, norm_step, 0)

        @pl.when(sec != 0)
        def _():
            dp3 = jnp.concatenate(split3(jnp.concatenate([dps[pl.ds(pl.multiple_of(m * SL, SL), SL), :], jnp.zeros((16 - SL, D), F32)], axis=0)), axis=0)
            dr[...] = dot_tn(jnp.concatenate([mem, mem, mem], axis=0), dp3)
            for i in range(nb):
                norm_rows(slice(i * tb, (i + 1) * tb))

    def token_pass(m, norms, ins):
        @pl.when(m == 0)
        def _():
            for w in wcp[:3]:
                w.wait()
        norms[1].wait()
        ins[0].wait()
        ins[1].wait()
        for i in range(nb):
            r = slice(i * tb, (i + 1) * tb)
            d2 = db2[m, r, :]
            dh = dr[r, :]
            dfs = [dot_nt(d2, wout[:D, :])]
            for j in range(nj):
                cols = slice(j * D, (j + 1) * D)
                if j + 1 < nj:
                    dfs.append(dot_nt(d2, wout[(j + 1) * D:(j + 2) * D, :]))
                dub = (dfs[j] * gp[m, r, cols].astype(F32)).astype(BF)
                gp[m, r, cols] = dub
                bacc[:, cols] += rowsum8(dub.astype(F32))
                dh = dh + dot_nt(dub, win[:, cols])
            dr[r, :] = dh
            run_when(jnp.logical_and(m == M - 1, sec == 0), AFTER_TOKENS[i])
        for i in range(nb):
            r = slice(i * tb, (i + 1) * tb)
            dh = dr[r, :]
            zz = z1[r, :].astype(F32)
            d1 = norm_pull(zz, s12[m, r, 0:1], g1[...].astype(F32), dh)
            vacc[3] += rowsum8(dh * zz)
            vacc[4] += rowsum8(dh)
            dr[r, :] = d1
            d1 = d1.astype(BF)
            db1[m, r, :] = d1
            vacc[5] += rowsum8(d1.astype(F32))
            dcb = dot_nt(d1, wat[...]).astype(BF)
            dc[r, :] = dcb
            prod = dcb.astype(F32) * c_s[m, r, :].astype(F32)
            hi = prod.astype(BF)
            low = (prod - hi.astype(F32)).astype(BF)
            delta[:, r] = dot_nt(indicator, hi) + dot_nt(indicator, low)
        @pl.when(m < M - 1)
        def _():
            for cp in norm_copies(m + 1):
                cp.start()
        ins[2].wait()

    def attention_pass(m):
        for p in range(HEADS // 2):
            cols = slice(p * 128, (p + 1) * 128)
            kcols = slice(D + p * 128, D + (p + 1) * 128)
            vcols = slice(2 * D + p * 128, 2 * D + (p + 1) * 128)
            q2 = qkv[m, :, cols] * (HEAD_DIM ** -0.5)
            qh = [jnp.where(low_half, q2, qcode[...]), jnp.where(low_half, qcode[...], q2)]
            dc2 = dc[:, cols]
            dqt = jnp.zeros((128, T), F32)
            for i in range(T // kb):
                r = slice(i * kb, (i + 1) * kb)
                k2 = qkv[m, r, kcols]
                v2 = qkv[m, r, vcols]
                kc = kcode[r, :]
                dks, dvs = [], []
                for h in range(2):
                    pick = low_half if h == 0 else jnp.logical_not(low_half)
                    kh = jnp.where(low_half, k2, kc) if h == 0 else jnp.where(low_half, kc, k2)
                    pt = jnp.exp(dot_nt(kh, qh[h]) - lse[m, 2 * p + h:2 * p + h + 1, :])
                    dpt = dot_nt(jnp.where(pick, v2, 0), dc2)
                    da = (pt * (dpt - delta[2 * p + h:2 * p + h + 1, :])).astype(BF)
                    dvs.append(dot(pt.astype(BF), dc2))
                    dks.append(dot(da, q2))
                    dqt = dqt + dot_tn(jnp.where(pick, k2, 0), da)
                qkv[m, r, kcols] = jnp.where(low_half, dks[0], dks[1]).astype(BF)
                qkv[m, r, vcols] = jnp.where(low_half, dvs[0], dvs[1]).astype(BF)
            qkv[m, :, cols] = (jnp.transpose(dqt) * (HEAD_DIM ** -0.5)).astype(BF)
            if AFTER_PAIR[p]:
                run_when(jnp.logical_and(m == M - 1, sec == 0), AFTER_PAIR[p])
        @pl.when(m == 0)
        def _():
            wcp[3].wait()

        def dx_step(i, _):
            r = pl.ds(pl.multiple_of(i * xb, xb), xb)
            dyx[m, r, :] = (dr[r, :] + dot_nt(qkv[m, r, :], wqkv[...])).astype(BF)

            @pl.when(sec != 0)
            def _():
                handoff(m, i).start()
            vacc[6] += rowsum8(qkv[m, r, :D].astype(F32))
            vacc[7] += rowsum8(qkv[m, r, 2 * D:].astype(F32))
            return 0
        lax.fori_loop(0, nx, dx_step, 0)

        @pl.when(sec == 0)
        def _():
            out_copy(m).start()
            dx_copy(m).start()

    lax.fori_loop(0, M + 1, one_pass, 0)

    vec = [remote(va.at[i], vb.at[i], s.at[chunks], r.at[chunks], target) for i, (s, r, target) in enumerate(
        ((send_a, recv_a, sibling), (send_b, recv_b, across), (send_c, recv_c, near), (send_d, recv_d, far)))]

    def vec_step(i):
        vec[i].wait_recv()
        total = va[i] + vb[i]
        if i < 3:
            va[i + 1] = total
            vec[i + 1].start()
        else:
            vec_o[...] = total
    va[0] = jnp.concatenate([jnp.sum(vacc[...], axis=1)]
        + [jnp.sum(bacc[:, j * D:(j + 1) * D], axis=0, keepdims=True) for j in range(nj)] + [jnp.zeros((8 - nj, D), F32)], axis=0)
    vec[0].start()
    for step in BEFORE_Q.split():
        run(step)
    products_q()
    for step in AT_THE_END.split():
        run(step)

    @pl.when(sec == 0)
    def _():
        pool_copy.wait_recv()
        loss_copy.wait_recv()
        pooled_o[...] = pooled_r[:, :half]
        loss_o[...] = loss_r[...]
        for m in range(M):
            dx_copy(m).wait_send()
            out_copy(m).wait()

    @pl.when(sec != 0)
    def _():
        pool_copy.wait_send()
        loss_copy.wait_send()
        pooled_o[...] = pooled_s[:, half:]
        loss_o[...] = loss_s[...]
        for m in range(M):
            for i in range(nx):
                handoff(m, i).wait_send()
            dx_copy(m).wait_recv()
    for v in vec:
        v.wait_send()
    for k in range(chunks):
        copy_b(k).wait_send()
        if k < nj:
            @pl.when(zlow != k % 2)
            def _():
                copy_c(k).wait_send()

            @pl.when(jnp.logical_and(zlow == k % 2, z != k))
            def _():
                copy_d(k).wait_send()
        else:
            copy_c(k).wait_send()
            copy_d(k).wait_send()


def stack_back(seg, pool, pairs, msgs0, stash, weights, tb=256, xb=128, kb=256):
    x, qkv, lse, c, z1, s12, hb, gp, act, z2 = stash
    wqkv, bq, bv, wat, bat, g1, b1, win, bin_, wout, bout, g2, b2 = weights
    M, T, D = c.shape
    N = M * T
    FF = win.shape[1]
    count = lax.axis_size("dp")
    rows = D // count
    chunks = (4 * D + 2 * FF) // D
    SL = 8
    sds = jax.ShapeDtypeStruct
    out_shape = (sds((16, D), F32), sds((M * SL, D // 2), F32), sds((M * SL, 128), F32), sds((rows, 3 * D), F32), sds((rows, D), F32), sds((rows, FF), F32),
        sds((FF // count, D), F32), sds((M, T, D), BF), sds((M, T, D // 2), BF))
    out_specs = (VM,) * 7 + (ANY, ANY)
    V = pltpu.VMEM
    S = pltpu.SemaphoreType.DMA
    nx = T // xb
    nj = FF // D
    piece = (rows, D)
    scratch = [V((M, T, D), BF), V((D, 3 * D), BF), V((D, D), BF), V((D, FF), BF), V((FF, D), BF),
        V((M, T, 3 * D), BF), V((M, T, D), BF), V((T, D), BF), V((M, T, FF), BF), V((T, D), BF),
        V((T, D), F32), V((T, D), BF), V((16, T), F32), V((M, T, D), BF), V((M, T, D), BF), V((8, 8, D), F32), V((8, FF), F32),
        V((count, 16, D // 2 + 128), BF), V((M * SL, D), F32), V((count * SL, 128), F32), V((count * SL, D), F32), V((M * SL, D), F32), V((M * SL, 128), F32), V((M * SL, D), F32), V((M * SL, 128), F32),
        V((T, 128), BF), V((T, 128), BF), V((count, 16, D // 2 + 128), BF), V((2, N, D), BF), V((2, 2, 2, 2, 2) + piece, BF), V((chunks, 2, 2, 2) + piece, BF), V((chunks, 2, 2) + piece, BF),
        V((chunks, 2) + piece, BF), V((chunks,) + piece, BF), V((2, 2) + piece, BF), V((4, 16, D), F32), V((4, 16, D), F32),
        S((M, 5)), S((4,)), S((2 + nj,)), S((M,)), S((M, nx)), S((M, nx)), S((count - 1,)), S((count - 1,)), S((4,)), S((M, 2))]
    scratch += [S((chunks + 1,)) for _ in range(8)]
    in_specs = (VM,) * 6 + (ANY,) * 12 + (VM, VM)
    return pl.pallas_call(functools.partial(back_kernel, tb, xb, kb), out_shape=out_shape, in_specs=in_specs, out_specs=out_specs,
        scratch_shapes=scratch, compiler_params=pltpu.CompilerParams(vmem_limit_bytes=62 * 2**20, collective_id=3, has_side_effects=True),
        name="stack_back")(seg, pool, pairs, msgs0, lse, s12, z2, gp, z1, c, qkv, hb.reshape(N, D), x.reshape(N, D), act,
            wout, win, wat, wqkv, g1, g2)


def finish_kernel(vec, pooled, loss, g_qkv, g_at, g_in, g_out, dx_h, dxr_h,
    pooled_o, loss_o, gx_o, qkv_o, at_o, in_o, out_o, *rest):
    small, buf, sem = rest[:9], rest[9], rest[10]
    sec = lax.axis_index("section")
    me = lax.axis_index("dp")
    half = buf.shape[2]

    @pl.when(sec == 0)
    def _():
        pltpu.make_async_copy(dx_h.at[:, :, pl.ds(0, half)], buf, sem.at[0]).start()

    @pl.when(sec != 0)
    def _():
        pltpu.make_async_copy(dxr_h, buf, sem.at[0]).start()
    for a, b in ((g_qkv, qkv_o), (g_at, at_o), (g_in, in_o), (g_out, out_o)):
        b[...] = a[...]
    SL = 8
    lane = lax.broadcasted_iota(jnp.int32, (SL, 128), 1) == lax.broadcasted_iota(jnp.int32, (SL, 128), 0)
    for m in range(pooled_o.shape[0]):
        pooled_o[m] = pooled[m * SL:m * SL + SEGS, :]
        loss_o[m:m + 1, :] = jnp.sum(jnp.where(lane, loss[m * SL:(m + 1) * SL, :], 0.0), axis=0, keepdims=True)[:, :SEGS]
    D = vec.shape[1]
    width, wide = small[0].shape[1], small[8].shape[1]
    parts = split3(vec[...])

    def columns(start, size):
        pick = lax.broadcasted_iota(jnp.int32, (D, size), 0) == lax.broadcasted_iota(jnp.int32, (D, size), 1) + start
        pick = jnp.where(pick, 1.0, 0.0).astype(BF)
        return (dot(parts[0], pick) + dot(parts[1], pick)) + dot(parts[2], pick)
    v = columns(me * width, 128)
    for i in range(8):
        small[i][...] = v[i:i + 1, :width]
    per = D // wide
    v = columns(lax.rem(me, per) * wide, 256)
    row = lax.broadcasted_iota(jnp.int32, (16, 256), 0) == 8 + lax.div(me, per)
    small[8][...] = jnp.sum(jnp.where(row, v, 0.0), axis=0, keepdims=True)[:, :wide]
    pltpu.make_async_copy(dxr_h, buf, sem.at[0]).wait()
    gx_o[...] = buf[...].astype(F32)


def finish(vec, pooled, loss, g_qkv, g_at, g_in, g_out, dx, dxr):
    M, T, D = dx.shape
    count = lax.axis_size("dp")
    sds = jax.ShapeDtypeStruct
    f = lambda a: sds(a.shape, F32)
    out_shape = (sds((M, SEGS, D // 2), F32), sds((M, SEGS), F32), sds((M, T, D // 2), F32), f(g_qkv), f(g_at), f(g_in), f(g_out)) + tuple(
        sds((1, D // count), F32) for _ in range(8)) + (sds((1, g_in.shape[1] // count), F32),)
    return pl.pallas_call(finish_kernel, out_shape=out_shape, in_specs=(VM,) * 7 + (ANY,) * 2, out_specs=(VM,) * 16,
        scratch_shapes=[pltpu.VMEM((M, T, D // 2), BF), pltpu.SemaphoreType.DMA((1,))],
        compiler_params=pltpu.CompilerParams(vmem_limit_bytes=VMEM_LIMIT), name="finish")(vec, pooled, loss, g_qkv, g_at, g_in, g_out, dx, dxr)


def contrast_head(pool, seg, pairs, all_pairs):
    M, S = pairs.shape
    D = pool.shape[-1]
    counts = jnp.sum((seg[:, :, None] == jnp.arange(SEGS)).astype(F32), axis=1)[:, :, None]
    pooled = pool[:, :SEGS] / counts
    radius = lax.rsqrt(jnp.sum(pooled * pooled, axis=-1, keepdims=True) + UNIT_EPS)
    unit = (pooled * radius).astype(BF)
    every = lax.all_gather(unit, "dp", axis=1, tiled=True)
    total = every.shape[1]
    start = lax.axis_index("dp") * S
    logits = TEMPER * jnp.einsum("mgd,mkd->mgk", every, every, preferred_element_type=F32)
    cols = jnp.arange(total)
    logits = jnp.where(cols[:, None] == cols[None, :], -MASK_FILL, logits)
    peak = jnp.max(logits, axis=-1, keepdims=True)
    exponent = jnp.exp(logits - peak)
    denom = jnp.sum(exponent, axis=-1, keepdims=True)
    target = cols[None, None, :] == all_pairs[:, :, None]
    loss = peak[..., 0] + jnp.log(denom[..., 0]) - jnp.sum(jnp.where(target, logits, 0.0), axis=-1)
    dl = (exponent / denom - target.astype(F32)).astype(BF)
    rows = lax.dynamic_slice_in_dim(dl, start, S, 1)
    columns = lax.dynamic_slice_in_dim(dl, start, S, 2)
    dn = TEMPER * (jnp.einsum("mgk,mkd->mgd", rows, every, preferred_element_type=F32)
        + jnp.einsum("mkg,mkd->mgd", columns, every, preferred_element_type=F32))
    dp = radius * dn - radius * radius * radius * jnp.sum(pooled * dn, axis=-1, keepdims=True) * pooled
    loss = lax.dynamic_slice_in_dim(loss, start, S, 1)
    return pooled, loss, jnp.pad(dp / counts, ((0, 0), (0, 16 - SEGS), (0, 0)))


def scattered(grads):
    count = lax.axis_size("dp")
    packed = jnp.concatenate([g.reshape(count, -1) for g in grads], axis=1)
    part = lax.psum_scatter(packed, "dp", scatter_dimension=0, tiled=True)[0].astype(F32)
    outs, at = [], 0
    for g in grads:
        size = g.size // count
        outs.append(part[at:at + size].reshape((1, g.shape[0] // count) + g.shape[1:]))
        at += size
    return outs


def swapped(value):
    return lax.ppermute(value, "section", [(0, 1), (1, 0)])


def local(hidden_in, seg_ids, pair_ids, w_qkv, b_query, b_value, w_attn_out, b_attn_out, ln1_gain, ln1_bias, w_in, b_in, w_out, b_out, ln2_gain, ln2_bias):
    M, _, T, D = hidden_in.shape
    sec = lax.axis_index("section")
    first = sec == 0
    weights = (w_qkv[0], b_query, b_value, w_attn_out[0], b_attn_out, ln1_gain, ln1_bias, w_in[0], b_in, w_out[0], b_out, ln2_gain, ln2_bias)
    half = D // 2
    count = lax.axis_size("dp")
    pool, x, qkv, lse, c, z1, s12, hb, gp, act, z2, msgs = stack_fwd(hidden_in[:, 0], seg_ids, pair_ids, weights, count if count == 16 else 0)
    if count == 16:
        parts = stack_back(seg_ids, pool, pair_ids, msgs, (x, qkv, lse, c, z1, s12, hb, gp, act, z2), weights)
        pooled, loss, grad_input, g_qkv, g_at, g_in, g_out, gg2, gb2, gbo, gg1, gb1, gba, gbq, gbv, gbi = finish(*parts)
        pooled_out, loss_out = pooled, loss
        g_qkv, g_at, g_in, g_out = (g[None] for g in (g_qkv, g_at, g_in, g_out))
    else:
        seg = seg_ids[:, 0]
        all_pairs = lax.all_gather(pair_ids, "dp", axis=1, tiled=True)
        pooled, loss, dp = contrast_head(pool, seg, pair_ids, all_pairs)
        vec, dx, dxb, db2, du, db1, dqkv = stack_bwd(seg, dp, (qkv, lse, c, z1, s12, gp, z2), weights)
        act = jnp.moveaxis(act, 0, 1).reshape(M, T, -1)
        big = [jnp.einsum("mta,mtb->ab", a, b, preferred_element_type=F32).astype(BF) for a, b in ((x, dqkv), (c, db1), (hb, du), (act, db2))]
        g_qkv, g_at, g_in, g_out = scattered(big)
        small = scattered([vec[i] for i in range(8)] + [vec[8:8 + w_in.shape[2] // D].reshape(-1)])
        gg2, gb2, gbo, gg1, gb1, gba, gbq, gbv, gbi = small
        kept = lax.dynamic_slice_in_dim(dx, sec * half, half, 2)
        sent = lax.dynamic_slice_in_dim(dxb, (1 - sec) * half, half, 2)
        grad_input = jnp.where(first, kept, swapped(sent).astype(F32))
        pooled_kept = lax.dynamic_slice_in_dim(pooled, sec * half, half, 2)
        pooled_sent = lax.dynamic_slice_in_dim(pooled, (1 - sec) * half, half, 2).astype(BF)
        pooled_out = jnp.where(first, swapped(pooled_sent).astype(F32), pooled_kept)
        loss_out = jnp.where(first, swapped(loss.astype(BF)).astype(F32), loss)
    return (pooled_out, loss_out, grad_input[:, None], g_qkv, gbq, gbv, g_at, gba, gg1, gb1, g_in, gbi, g_out, gbo, gg2, gb2)


def solution(mesh):
    in_specs = (
        P(None, "dp", None, None),
        P(None, "dp", None),
        P(None, "dp"),
        P("section", None, None),
        P("section", None),
        P("section", None),
        P("section", None, None),
        P("section", None),
        P("section", None),
        P("section", None),
        P("section", None, None),
        P("section", None),
        P("section", None, None),
        P("section", None),
        P("section", None),
        P("section", None),
    )
    out_specs = (
        P(None, "dp", "section"),
        P(None, "dp"),
        P(None, "dp", None, "section"),
        P("section", "dp", None),
        P("section", "dp"),
        P("section", "dp"),
        P("section", "dp", None),
        P("section", "dp"),
        P("section", "dp"),
        P("section", "dp"),
        P("section", "dp", None),
        P("section", "dp"),
        P("section", "dp", None),
        P("section", "dp"),
        P("section", "dp"),
        P("section", "dp"),
    )
    return jax.shard_map(local, mesh=mesh, in_specs=in_specs, out_specs=out_specs, check_vma=False)
```

```python
import functools
import jax, jax.numpy as jnp
from jax import lax
from jax.experimental import pallas as pl
from jax.experimental.pallas import tpu as pltpu
from jax.sharding import PartitionSpec as P

HEADS = 12
HEAD_DIM = 64
SEGS = 4
UNIT_EPS = 1e-06
TEMPER = 20.0
MASK_FILL = 1000000000.0
NORM_EPS = 1e-12
BF = jnp.bfloat16
F32 = jnp.float32
VMEM_LIMIT = 60 * 2**20
MESH = pl.DeviceIdType.MESH
ANY = pl.BlockSpec(memory_space=pl.ANY)
VM = pl.BlockSpec(memory_space=pltpu.VMEM)


def dot(a, b):
    return jnp.dot(a, b, preferred_element_type=F32)


def dot_nt(a, b):
    return lax.dot_general(a, b, (((1,), (1,)), ((), ())), preferred_element_type=F32)


def dot_tn(a, b):
    return lax.dot_general(a, b, (((0,), (0,)), ((), ())), preferred_element_type=F32)


def split3(v):
    hi = v.astype(BF)
    rest = v - hi.astype(F32)
    mid = rest.astype(BF)
    low = (rest - mid.astype(F32)).astype(BF)
    return hi, mid, low


def members(seg_row):
    rows = lax.broadcasted_iota(jnp.int32, (16, seg_row.shape[1]), 0)
    return jnp.where(rows == seg_row, 1.0, 0.0).astype(BF)


def normed_rows(rows):
    centre = rows - jnp.mean(rows, axis=-1, keepdims=True)
    scale = lax.rsqrt(jnp.mean(centre * centre, axis=-1, keepdims=True) + NORM_EPS)
    return centre * scale, scale


def gelu_pair(u):
    mag = jnp.abs(u)
    t = 1.0 / (1.0 + (0.3275911 * 0.7071067811865476) * mag)
    e = jnp.exp(-0.5 * (u * u))
    poly = t * (0.127414796 + t * (-0.142248368 + t * (0.7107068705 + t * (-0.7265760135 + t * 0.5307027145))))
    tail = poly * e
    cdf = jnp.where(u >= 0.0, 1.0 - tail, tail)
    return u * cdf, cdf + (u * 0.3989422804014327) * e


def codes(mem):
    lanes = lax.rem(lax.broadcasted_iota(jnp.int32, (16, 128), 1), HEAD_DIM)
    pick = jnp.where(lanes == lax.broadcasted_iota(jnp.int32, (16, 128), 0), 1.0, 0.0)
    pick = jnp.where(lanes < SEGS, pick, 0.0).astype(BF)
    key_code = dot_tn(mem, pick)
    active = jnp.where(lanes[:1] < SEGS, 1.0, 0.0)
    return key_code.astype(BF), ((key_code - active) * MASK_FILL).astype(BF)


def documents(mem, pool):
    counts = jnp.maximum(jnp.sum(mem.astype(F32), axis=1, keepdims=True)[:8], 1.0)
    pooled = pool[:8, :] / counts
    radius = lax.rsqrt(jnp.sum(pooled * pooled, axis=-1, keepdims=True) + UNIT_EPS)
    return pooled, radius, counts


def message(unit, pairs):
    half = unit.shape[1] // 2
    tag = [jnp.broadcast_to(pairs[:, j:j + 1].astype(F32), (1, 128)) for j in range(SEGS)]
    tag = jnp.concatenate(tag + [jnp.zeros((8 - SEGS, 128), F32)], axis=0)
    return jnp.concatenate([jnp.concatenate([unit[:, :half], tag], axis=1), jnp.concatenate([unit[:, half:], tag], axis=1)], axis=0).astype(BF)


def fwd_kernel(tb, peers,
    x_h, seg, pairs, wqkv_h, bq, bv, wat_h, bat, g1, b1, win_h, bin_, wout_h, bout, g2, b2,
    pool_o, x_o, qkv_h, lse_o, c_h, z1_h, s12_o, hb_h, gp_h, act_h, z2_h, msgs_o,
    x_s, wqkv, wat, win, wout, qkv, c_s, hb_s, z1_s, gp_s, act_s, z2_s, y_s, yf, msgs, kcode, qcode,
    insem, wsem, outsem, send_sem, recv_sem, msg_send, msg_recv):
    sec = lax.axis_index("section")
    me = lax.axis_index("dp")
    other = {"section": 1 - sec}
    M, T, D = x_s.shape
    FF = win.shape[1]
    nb = T // tb

    ws = [pltpu.make_async_copy(a, b, wsem.at[i]) for i, (a, b) in enumerate(
        ((wqkv_h, wqkv), (wat_h, wat), (win_h, win), (wout_h, wout)))]
    barrier = pltpu.get_barrier_semaphore()

    @pl.when(sec == 0)
    def _():
        pltpu.make_async_copy(x_h.at[0], x_s.at[0], insem.at[0]).start()
    ws[0].start()
    pl.semaphore_signal(barrier, inc=1, device_id=other, device_id_type=MESH)
    for d in range(1, peers):
        pl.semaphore_signal(barrier, inc=1, device_id={"dp": lax.rem(me + d, peers)}, device_id_type=MESH)

    lane = lax.broadcasted_iota(jnp.int32, (1, 128), 1)
    low_half = lane < HEAD_DIM

    def block(start):
        return pl.ds(start if isinstance(start, int) else pl.multiple_of(start, tb), tb)

    def out_copies(m, i):
        r = block(i * tb)
        return [pltpu.make_async_copy(a.at[m, r], b.at[m, r], outsem.at[m, i, j]) for j, (a, b) in enumerate(
            ((c_s, c_h), (hb_s, hb_h), (z1_s, z1_h), (z2_s, z2_h)))]

    def wide_copies(m, i, j):
        r = block(i * tb)
        cols = slice(j * D, (j + 1) * D)
        return [pltpu.make_async_copy(gp_s.at[m, r, cols], gp_h.at[m, r, cols], outsem.at[m, i, 4 + 2 * j]),
            pltpu.make_async_copy(act_s.at[m, r, cols], act_h.at[j, block(m * T + i * tb)], outsem.at[m, i, 5 + 2 * j])]

    def whole_copies(m):
        return [pltpu.make_async_copy(a.at[m], b.at[m], outsem.at[m, nb, j]) for j, (a, b) in enumerate(((x_s, x_o), (qkv, qkv_h)))]

    def handoff(m, i):
        r = block(i * tb)
        return pltpu.make_async_remote_copy(src_ref=y_s.at[m, r], dst_ref=x_s.at[m, r], send_sem=send_sem.at[m, i],
            recv_sem=recv_sem.at[m, i], device_id=other, device_id_type=MESH)

    def msg_copy(d):
        return pltpu.make_async_remote_copy(src_ref=msgs.at[me], dst_ref=msgs.at[me], send_sem=msg_send.at[d - 1], recv_sem=msg_recv.at[d - 1],
            device_id={"dp": lax.rem(me + d, peers)}, device_id_type=MESH)

    def micro_step(m, _):
        mem = members(seg[m])
        kcode[...], qcode[...] = codes(mem)

        @pl.when(sec == 0)
        def _():
            pltpu.make_async_copy(x_h.at[m], x_s.at[m], insem.at[m]).wait()

        @pl.when(m == 0)
        def _():
            ws[0].wait()
            for w in ws[1:]:
                w.start()

            @pl.when(sec == 0)
            def _():
                for n in range(1, M):
                    pltpu.make_async_copy(x_h.at[n], x_s.at[n], insem.at[n]).start()

        def qkv_step(i, _):
            r = block(i * tb)

            @pl.when(sec != 0)
            def _():
                handoff(m, i).wait_recv()
            xi = x_s[m, r, :]
            for j, b in ((0, bq), (1, None), (2, bv)):
                cols = slice(j * D, (j + 1) * D)
                v = dot(xi, wqkv[:, cols])
                if b is not None:
                    v = v + b[...].astype(F32)
                qkv[m, r, cols] = v.astype(BF)
            return 0
        lax.fori_loop(0, nb, qkv_step, 0)
        for cp in whole_copies(m):
            cp.start()
        ones = jnp.ones((T, 128), BF)
        def block_step(i, _):
            r = block(i * tb)
            key_code = kcode[...]
            qc = qcode[r, :]
            lses = jnp.zeros((tb, 128), F32)
            for p in range(HEADS // 2):
                cols = slice(p * 128, (p + 1) * 128)
                k2 = qkv[m, :, D + p * 128:D + (p + 1) * 128]
                v2 = jnp.concatenate([qkv[m, :, 2 * D + p * 128:2 * D + (p + 1) * 128], ones], axis=1)
                q2 = qkv[m, r, cols] * (HEAD_DIM ** -0.5)
                halves = []
                for h in range(2):
                    if h == 0:
                        s = dot_nt(jnp.where(low_half, q2, qc), jnp.where(low_half, k2, key_code))
                    else:
                        s = dot_nt(jnp.where(low_half, qc, q2), jnp.where(low_half, key_code, k2))
                    mx = jnp.max(s, axis=-1, keepdims=True)
                    e = jnp.exp(s - mx).astype(BF)
                    c = dot(e, v2)
                    l = c[:, 128:]
                    halves.append(c[:, :128] / l)
                    lses = jnp.where(lane == 2 * p + h, mx + jnp.log(l), lses)
                c_s[m, r, cols] = jnp.where(low_half, halves[0], halves[1]).astype(BF)
            lse_o[m, :, r] = jnp.transpose(lses)[:16, :]

            @pl.when(jnp.logical_and(m == 0, i == 0))
            def _():
                for w in ws[1:]:
                    w.wait()
                pl.semaphore_wait(barrier, max(peers, 1))
            r1 = x_s[m, r, :].astype(F32) + dot(c_s[m, r, :], wat[...]) + bat[...].astype(F32)
            z, scale = normed_rows(r1)
            acc = z * g1[...].astype(F32) + b1[...].astype(F32)
            hi = acc.astype(BF)
            hb_s[m, r, :] = hi
            z1_s[m, r, :] = z.astype(BF)
            s12_o[m, r, 0:1] = scale
            outs = out_copies(m, i)
            for cp in outs[:3]:
                cp.start()
            acc = acc + bout[...].astype(F32)
            nj = FF // D
            us = [dot(hi, win[:, :D])]
            for j in range(nj):
                cols = slice(j * D, (j + 1) * D)
                if j + 1 < nj:
                    us.append(dot(hi, win[:, (j + 1) * D:(j + 2) * D]))
                f, gp = gelu_pair(us[j] + bin_[:, cols].astype(F32))
                f = f.astype(BF)
                act_s[m, r, cols] = f
                gp_s[m, r, cols] = gp.astype(BF)
                acc = acc + dot(f, wout[cols, :])
                for cp in wide_copies(m, i, j):
                    cp.start()
            z, scale = normed_rows(acc)
            y = z * g2[...].astype(F32) + b2[...].astype(F32)
            y_s[m, r, :] = y.astype(BF)

            @pl.when(sec == 0)
            def _():
                handoff(m, i).start()
            z2_s[m, r, :] = z.astype(BF)
            s12_o[m, r, 1:2] = scale
            yf[r, :] = y
            outs[3].start()
            return 0
        lax.fori_loop(0, nb, block_step, 0)

        @pl.when(sec != 0)
        def _():
            hi, mid, low = split3(yf[...])
            pool = (dot(mem, hi) + dot(mem, mid)) + dot(mem, low)
            pool_o[m] = pool
            if peers:
                @pl.when(m == 0)
                def _():
                    pooled, radius, _ = documents(mem, pool)
                    msgs[me] = message(pooled * radius, pairs[0:1, :])
                    for d in range(1, peers):
                        msg_copy(d).start()
        return 0
    lax.fori_loop(0, M, micro_step, 0)

    @pl.when(sec == 0)
    def _():
        pool_o[...] = jnp.zeros_like(pool_o)
        msgs_o[...] = jnp.zeros_like(msgs_o)

    if peers:
        @pl.when(sec != 0)
        def _():
            for d in range(1, peers):
                msg_copy(d).wait()
            msgs_o[...] = msgs[...]
    for m in range(M):
        for cp in whole_copies(m):
            cp.wait()
        for i in range(nb):
            for cp in out_copies(m, i) + sum((wide_copies(m, i, j) for j in range(FF // D)), []):
                cp.wait()

    @pl.when(sec == 0)
    def _():
        for m in range(M):
            for i in range(nb):
                handoff(m, i).wait_send()


def stack_fwd(x, seg, pairs, weights, peers, tb=256):
    M, T, D = x.shape
    FF = weights[7].shape[1]
    sds = jax.ShapeDtypeStruct
    out_shape = (sds((M, 16, D), F32), sds((M, T, D), BF), sds((M, T, 3 * D), BF), sds((M, 16, T), F32), sds((M, T, D), BF),
        sds((M, T, D), BF), sds((M, T, 2), F32), sds((M, T, D), BF), sds((M, T, FF), BF), sds((FF // D, M * T, D), BF), sds((M, T, D), BF), sds((max(peers, 1), 16, D // 2 + 128), BF))
    out_specs = (VM, ANY, ANY, VM, ANY, ANY, VM, ANY, ANY, ANY, ANY, VM)
    V = pltpu.VMEM
    S = pltpu.SemaphoreType.DMA
    nb = T // tb
    scratch = [V((M, T, D), BF), V((D, 3 * D), BF), V((D, D), BF), V((D, FF), BF), V((FF, D), BF), V((M, T, 3 * D), BF),
        V((M, T, D), BF), V((M, T, D), BF), V((M, T, D), BF), V((M, T, FF), BF), V((M, T, FF), BF), V((M, T, D), BF), V((M, T, D), BF),
        V((T, D), F32), V((max(peers, 1), 16, D // 2 + 128), BF), V((T, 128), BF), V((T, 128), BF), S((M,)), S((4,)), S((M, nb + 1, 4 + 2 * (FF // D))), S((M, nb)), S((M, nb)),
        S((max(peers, 2) - 1,)), S((max(peers, 2) - 1,))]
    in_specs = (ANY, VM, VM, ANY, VM, VM, ANY, VM, VM, VM, ANY, VM, ANY, VM, VM, VM)
    return pl.pallas_call(functools.partial(fwd_kernel, tb, peers), out_shape=out_shape, in_specs=in_specs, out_specs=out_specs,
        scratch_shapes=scratch, compiler_params=pltpu.CompilerParams(vmem_limit_bytes=VMEM_LIMIT, collective_id=0, has_side_effects=True),
        name="stack_fwd")(x, seg, pairs, *weights)


def rowsum8(v):
    return jnp.sum(v.reshape(v.shape[0] // 8, 8, v.shape[1]), axis=0)


def bwd_kernel(tb, fc, kb,
    seg, dp, lse, s12, qkv_h, c_h, z1_h, gp_h, z2_h, wqkv_h, wat_h, g1, win_h, wout_h, g2,
    vec_o, dx_h, dxb_h, db2_h, du_h, db1_h, dqkv_h,
    dyr, wqkv, wat, win, wout, qkv, c_s, z1, gp, z2, bias, dy_s, dr1, dc, delta, du, db2, db1, dqkv, dx, dxb, vacc, bacc,
    insem, wsem, outsem, send_sem, recv_sem):
    sec = lax.axis_index("section")
    other = {"section": 1 - sec}
    M, T, D = c_s.shape
    FF = win.shape[1]
    nb = T // tb

    ws = [pltpu.make_async_copy(a, b, wsem.at[i]) for i, (a, b) in enumerate(
        ((wout_h, wout), (win_h, win), (wat_h, wat), (wqkv_h, wqkv)))]

    def in_copies(m):
        pairs = [(z2_h, z2), (gp_h, gp), (z1_h, z1), (c_h, c_s), (qkv_h, qkv)]
        return [pltpu.make_async_copy(a.at[m], b.at[m], insem.at[m, i]) for i, (a, b) in enumerate(pairs)]
    first = in_copies(0)
    first[0].start()
    ws[0].start()
    barrier = pltpu.get_barrier_semaphore()
    pl.semaphore_signal(barrier, inc=1, device_id=other, device_id_type=MESH)
    for a, b in zip(first[1:], ws[1:]):
        a.start()
        b.start()
    first[4].start()
    for m in range(1, M):
        for a in in_copies(m):
            a.start()
    vacc[...] = jnp.zeros_like(vacc)
    bacc[...] = jnp.zeros_like(bacc)
    pl.semaphore_wait(barrier, 1)

    lane = lax.broadcasted_iota(jnp.int32, (1, 128), 1)
    low_half = lane < HEAD_DIM
    indicator = jnp.where(lax.broadcasted_iota(jnp.int32, (16, D), 1) // HEAD_DIM == lax.broadcasted_iota(jnp.int32, (16, D), 0), 1.0, 0.0).astype(BF)

    def out_copies(m):
        pairs = [(db2, db2_h), (du, du_h), (db1, db1_h), (dqkv, dqkv_h), (dx, dx_h), (dxb, dxb_h)]
        return [pltpu.make_async_copy(a.at[m], b.at[m], outsem.at[m, i]) for i, (a, b) in enumerate(pairs)]

    def handoff(m, i):
        r = pl.ds(i * tb if isinstance(i, int) else pl.multiple_of(i * tb, tb), tb)
        return pltpu.make_async_remote_copy(src_ref=dxb.at[m, r], dst_ref=dyr.at[m, r], send_sem=send_sem.at[m, i],
            recv_sem=recv_sem.at[m, i], device_id=other, device_id_type=MESH)

    def norm_pull(z, scale, gain, dy):
        g = dy * gain
        return scale * (g - jnp.mean(g, axis=-1, keepdims=True) - z * jnp.mean(g * z, axis=-1, keepdims=True))

    def micro_step(m, _):
        ins = in_copies(m)
        outs = out_copies(m)
        mem = members(seg[pl.ds(m, 1), :])
        bias[...] = (dot_tn(mem, mem) - 1.0) * MASK_FILL
        dp3 = jnp.concatenate(split3(dp[m]), axis=0)

        @pl.when(sec == 0)
        def _():
            for i in range(nb):
                handoff(m, i).wait_recv()

        @pl.when(m == 0)
        def _():
            ws[0].wait()
            ws[1].wait()
            ws[2].wait()
        for a in ins[:4]:
            a.wait()

        def tok_step(i, _):
            r = pl.ds(pl.multiple_of(i * tb, tb), tb)

            @pl.when(sec == 0)
            def _():
                dy_s[...] = dyr[m, r, :].astype(F32)

            @pl.when(sec != 0)
            def _():
                blk = members(seg[pl.ds(m, 1), r])
                dy_s[...] = dot_tn(jnp.concatenate([blk, blk, blk], axis=0), dp3)
            dy = dy_s[...]
            z = z2[m, r, :].astype(F32)
            dr2 = norm_pull(z, s12[m, r, 1:2], g2[...].astype(F32), dy)
            vacc[0] += rowsum8(dy * z)
            vacc[1] += rowsum8(dy)
            d2 = dr2.astype(BF)
            db2[m, r, :] = d2
            vacc[2] += rowsum8(d2.astype(F32))
            dh = dr2
            nj = FF // fc
            dfs = [dot_nt(d2, wout[:fc, :])]
            for j in range(nj):
                cols = slice(j * fc, (j + 1) * fc)
                if j + 1 < nj:
                    dfs.append(dot_nt(d2, wout[(j + 1) * fc:(j + 2) * fc, :]))
                dub = (dfs[j] * gp[m, r, cols].astype(F32)).astype(BF)
                du[m, r, cols] = dub
                bacc[:, cols] += rowsum8(dub.astype(F32))
                dh = dh + dot_nt(dub, win[:, cols])
            z = z1[m, r, :].astype(F32)
            d1 = norm_pull(z, s12[m, r, 0:1], g1[...].astype(F32), dh)
            vacc[3] += rowsum8(dh * z)
            vacc[4] += rowsum8(dh)
            dr1[r, :] = d1
            d1 = d1.astype(BF)
            db1[m, r, :] = d1
            vacc[5] += rowsum8(d1.astype(F32))
            dcb = dot_nt(d1, wat[...]).astype(BF)
            dc[r, :] = dcb
            prod = dcb.astype(F32) * c_s[m, r, :].astype(F32)
            hi = prod.astype(BF)
            low = (prod - hi.astype(F32)).astype(BF)
            delta[:, r] = dot_nt(indicator, hi) + dot_nt(indicator, low)
            return 0
        lax.fori_loop(0, nb, tok_step, 0)
        for o in outs[:3]:
            o.start()
        ins[4].wait()

        def att_step(p, _):
            cols = pl.ds(pl.multiple_of(p * 128, 128), 128)
            kcols = pl.ds(pl.multiple_of(p * 128 + D, 128), 128)
            vcols = pl.ds(pl.multiple_of(p * 128 + 2 * D, 128), 128)
            q2 = qkv[m, :, cols] * (HEAD_DIM ** -0.5)
            dc2 = dc[:, cols]
            dqt = jnp.zeros((128, T), F32)
            for i in range(T // kb):
                rows = slice(i * kb, (i + 1) * kb)
                k2 = qkv[m, rows, kcols]
                v2 = qkv[m, rows, vcols]
                dks, dvs = [], []
                for h in range(2):
                    pick = low_half if h == 0 else jnp.logical_not(low_half)
                    kh = jnp.where(pick, k2, 0)
                    vh = jnp.where(pick, v2, 0)
                    st = dot_nt(kh, q2) + bias[rows, :]
                    pt = jnp.exp(st - lse[m, pl.ds(2 * p + h, 1), :])
                    dpt = dot_nt(vh, dc2)
                    da = (pt * (dpt - delta[pl.ds(2 * p + h, 1), :])).astype(BF)
                    dvs.append(dot(pt.astype(BF), dc2))
                    dks.append(dot(da, q2))
                    dqt = dqt + dot_tn(kh, da)
                dqkv[m, rows, kcols] = jnp.where(low_half, dks[0], dks[1]).astype(BF)
                dqkv[m, rows, vcols] = jnp.where(low_half, dvs[0], dvs[1]).astype(BF)
            dqkv[m, :, cols] = (jnp.transpose(dqt) * (HEAD_DIM ** -0.5)).astype(BF)
            return 0
        lax.fori_loop(0, HEADS // 2, att_step, 0)
        outs[3].start()

        @pl.when(m == 0)
        def _():
            ws[3].wait()

        def dx_step(i, _):
            r = pl.ds(pl.multiple_of(i * tb, tb), tb)
            v = dr1[r, :] + dot_nt(dqkv[m, r, :], wqkv[...])
            dx[m, r, :] = v
            dxb[m, r, :] = v.astype(BF)
            vacc[6] += rowsum8(dqkv[m, r, :D].astype(F32))
            vacc[7] += rowsum8(dqkv[m, r, 2 * D:].astype(F32))

            @pl.when(sec != 0)
            def _():
                handoff(m, i).start()
            return 0
        lax.fori_loop(0, nb, dx_step, 0)
        outs[4].start()
        outs[5].start()
        return 0
    lax.fori_loop(0, M, micro_step, 0)
    vec_o[...] = jnp.concatenate([jnp.sum(vacc[...], axis=1)]
        + [jnp.sum(bacc[:, j * D:(j + 1) * D], axis=0, keepdims=True) for j in range(FF // D)] + [jnp.zeros((4, D), F32)], axis=0)
    for m in range(M):
        for o in out_copies(m):
            o.wait()

    @pl.when(sec != 0)
    def _():
        for m in range(M):
            for i in range(nb):
                handoff(m, i).wait_send()


def stack_bwd(seg, dp, stash, weights, tb=256, fc=768, kb=256):
    qkv, lse, c, z1, s12, gp, z2 = stash
    wqkv, bq, bv, wat, bat, g1, b1, win, bin_, wout, bout, g2, b2 = weights
    M, T, D = c.shape
    FF = win.shape[1]
    sds = jax.ShapeDtypeStruct
    out_shape = (sds((16, D), F32), sds((M, T, D), F32), sds((M, T, D), BF), sds((M, T, D), BF), sds((M, T, FF), BF), sds((M, T, D), BF), sds((M, T, 3 * D), BF))
    out_specs = (VM, ANY, ANY, ANY, ANY, ANY, ANY)
    V = pltpu.VMEM
    S = pltpu.SemaphoreType.DMA
    nb = T // tb
    scratch = [V((M, T, D), BF), V((D, 3 * D), BF), V((D, D), BF), V((D, FF), BF), V((FF, D), BF),
        V((M, T, 3 * D), BF), V((M, T, D), BF), V((M, T, D), BF), V((M, T, FF), BF), V((M, T, D), BF),
        V((T, T), F32), V((tb, D), F32), V((T, D), F32), V((T, D), BF), V((16, T), F32),
        V((M, T, FF), BF), V((M, T, D), BF), V((M, T, D), BF), V((M, T, 3 * D), BF), V((M, T, D), F32), V((M, T, D), BF),
        V((8, 8, D), F32), V((8, FF), F32), S((M, 5)), S((4,)), S((M, 6)), S((M, nb)), S((M, nb))]
    in_specs = (VM, VM, VM, VM, ANY, ANY, ANY, ANY, ANY, ANY, ANY, VM, ANY, ANY, VM)
    return pl.pallas_call(functools.partial(bwd_kernel, tb, fc, kb), out_shape=out_shape, in_specs=in_specs, out_specs=out_specs,
        scratch_shapes=scratch, compiler_params=pltpu.CompilerParams(vmem_limit_bytes=VMEM_LIMIT, collective_id=1, has_side_effects=True),
        name="stack_bwd")(seg, dp, lse, s12, qkv, c, z1, gp, z2, wqkv, wat, g1, win, wout, g2)


AFTER_TOKENS = ("", " ".join(("a2 a3 b0",)))
AFTER_W = ("", " ".join(("a4 b1",)), " ".join(("a5",)), " ".join(("a6 b2 c0",)))
AFTER_A = " ".join(("b3",))
AFTER_PAIR = (" ".join(("a7 c1",)), "", "", " ".join(("b4",)), " ".join(("a8",)), "")
BEFORE_Q = " ".join(("c2 b5",))
AFTER_Q = ("", " ".join(("v0 a9 c3 c4", "b6",)), "")
AT_THE_END = " ".join(("v1 a10 b8 b7", "c5 a11 d4 b9", "d3 c6 c8 b10", "c7 v2 d5 b11", "c9 v3 b12 d8", "d6 c10 d7 c11", "d9 c12 d10 d11", "d12",))


def back_kernel(tb, xb, kb,
    seg, pool, pairs, msgs0, lse, s12, z2_h, gp_h, z1_h, c_h, qkv_h, hb_h, x_h, act_h, wout_h, win_h, wat_h, wqkv_h, g1, g2,
    vec_o, pooled_o, loss_o, g_qkv, g_at, g_in, g_out, dx_o, dxr_o,
    dyx, wqkv, wat, win, wout, qkv, c_s, z1, gp, z2, dr, dc, delta, db2, db1, vacc, bacc,
    msgs, dps, loss_w, dn_s, pooled_s, loss_s, pooled_r, loss_r, kcode, qcode, gathered, rhs, part, got_a, got_b, got_c, got_d, got_t, va, vb,
    insem, wsem, latesem, outsem, send_sem, recv_sem, msg_send, msg_recv, pool_sem, dx_sem,
    send_a, recv_a, send_b, recv_b, send_c, recv_c, send_d, recv_d):
    sec = lax.axis_index("section")
    me = lax.axis_index("dp")
    peers = msgs.shape[0]
    core = lax.rem(me, 2)
    y = lax.rem(lax.div(me, 2), 2)
    z = lax.div(me, 4)
    zlow = lax.rem(z, 2)
    zhigh = lax.div(z, 2)
    other = {"section": 1 - sec}
    sibling = {"dp": me + 1 - 2 * core}
    across = {"dp": me + 2 - 4 * y}
    near = {"dp": me + 4 - 8 * zlow}
    far = {"dp": me + 8 - 16 * zhigh}

    def remote(src, dst, ss, rs, target):
        return pltpu.make_async_remote_copy(src_ref=src, dst_ref=dst, send_sem=ss, recv_sem=rs, device_id=target, device_id_type=MESH)
    M, T, D = c_s.shape
    N = M * T
    FF = gp.shape[2]
    half = D // 2
    nb = T // tb
    nx = T // xb
    nj = FF // D
    chunks = got_a.shape[0]
    rows = got_a.shape[4]
    SL = 8
    zchunk = 2 * nj
    cut = rows // 48 * 32

    wcp = [pltpu.make_async_copy(a, b, wsem.at[i]) for i, (a, b) in enumerate(
        ((wout_h, wout), (win_h, win), (wat_h, wat), (wqkv_h, wqkv)))]

    def norm_copies(m):
        return [pltpu.make_async_copy(a.at[m], b, insem.at[m, i]) for i, (a, b) in enumerate(((z2_h, z2), (z1_h, z1)))]

    def in_copies(m):
        return [pltpu.make_async_copy(a.at[m], b.at[m], insem.at[m, 2 + i]) for i, (a, b) in enumerate(((gp_h, gp), (c_h, c_s), (qkv_h, qkv)))]

    def act_copy(t):
        return pltpu.make_async_copy(act_h.at[t], rhs.at[t % 2 if isinstance(t, int) else lax.rem(t, 2)], latesem.at[t])
    hb_copy = pltpu.make_async_copy(hb_h, rhs.at[0], latesem.at[nj])
    x_copy = pltpu.make_async_copy(x_h, rhs.at[1], latesem.at[nj + 1])
    norms = norm_copies(0)
    ins = in_copies(0)
    norms[0].start()
    wcp[0].start()
    barrier = pltpu.get_barrier_semaphore()
    pl.semaphore_signal(barrier, inc=1, device_id=other, device_id_type=MESH)
    for d in range(1, peers):
        pl.semaphore_signal(barrier, inc=1, device_id={"dp": lax.rem(me + d, peers)}, device_id_type=MESH)
    for a in [ins[0], wcp[1], norms[1], wcp[2], ins[1]]:
        a.start()
    vacc[...] = jnp.zeros_like(vacc)
    bacc[...] = jnp.zeros_like(bacc)

    def msg_copy(d):
        return remote(msgs.at[me], msgs.at[me], msg_send.at[d - 1], msg_recv.at[d - 1], {"dp": lax.rem(me + d, peers)})
    pool_copy = remote(pooled_s, pooled_r, pool_sem.at[0], pool_sem.at[1], other)
    loss_copy = remote(loss_s, loss_r, pool_sem.at[2], pool_sem.at[3], other)
    def head(m):
        eight = pl.ds(pl.multiple_of(m * SL, SL), SL)
        pooled, radius, counts = documents(members(seg[m]), pool[m])
        G = peers * SL
        lo = gathered[:, :SL, :half].astype(F32).reshape(G, half).astype(BF)
        hi = gathered[:, SL:, :half].astype(F32).reshape(G, half).astype(BF)
        partner = gathered[:, :SL, half:].astype(F32).reshape(G, 128)
        rid = lax.broadcasted_iota(jnp.int32, (G, G), 0)
        cid = lax.broadcasted_iota(jnp.int32, (G, G), 1)
        held = jnp.logical_and(lax.rem(rid, SL) < SEGS, lax.rem(cid, SL) < SEGS)
        logits = TEMPER * (dot_nt(lo, lo) + dot_nt(hi, hi))
        logits = jnp.where(jnp.logical_and(held, rid != cid), logits, -MASK_FILL)
        peak = jnp.max(logits, axis=-1, keepdims=True)
        exponent = jnp.exp(logits - peak)
        denom = jnp.sum(exponent, axis=-1, keepdims=True)
        doc = (lax.div(cid, SL) * SEGS + lax.rem(cid, SL)).astype(F32)
        target = jnp.where(jnp.logical_and(held, doc == partner[:, :1]), 1.0, 0.0)
        loss = peak + jnp.log(denom) - jnp.sum(target * logits, axis=-1, keepdims=True)
        dl = jnp.where(held, exponent / denom - target, 0.0).astype(BF)
        own = pl.ds(pl.multiple_of(me * SL, SL), SL)
        for side, part_of in ((0, lo), (1, hi)):
            dn_s[:, side * half:(side + 1) * half] = TEMPER * (dot(dl, part_of) + dot_tn(dl, part_of))
        dn = dn_s[own, :]
        loss_w[...] = jnp.broadcast_to(loss, (G, 128))
        loss_s[eight, :] = loss_w[own, :]
        dps[eight, :] = (radius * dn - radius * radius * radius * jnp.sum(pooled * dn, axis=-1, keepdims=True) * pooled) / counts

    lane = lax.broadcasted_iota(jnp.int32, (1, 128), 1)
    low_half = lane < HEAD_DIM
    indicator = jnp.where(lax.broadcasted_iota(jnp.int32, (16, D), 1) // HEAD_DIM == lax.broadcasted_iota(jnp.int32, (16, D), 0), 1.0, 0.0).astype(BF)

    def out_copy(m):
        return pltpu.make_async_copy(dyx.at[m], dx_o.at[m], outsem.at[m])

    def handoff(m, i):
        r = pl.ds(i * xb if isinstance(i, int) else pl.multiple_of(i * xb, xb), xb)
        return remote(dyx.at[m, r], dyx.at[m, r], send_sem.at[m, i], recv_sem.at[m, i], other)

    def dx_copy(m):
        return remote(dyx.at[m, :, half:], dxr_o.at[m], dx_sem.at[m, 0], dx_sem.at[m, 1], other)

    def norm_pull(zz, scale, gain, dy):
        g = dy * gain
        return scale * (g - jnp.mean(g, axis=-1, keepdims=True) - zz * jnp.mean(g * zz, axis=-1, keepdims=True))

    def base(k):
        return min(k, chunks - 1)

    def span(k):
        return pl.ds(0, cut) if k == chunks - 1 else pl.ds(cut, rows - cut) if k == chunks else pl.ds(0, rows)

    def slot(k):
        return k % 2 if isinstance(k, int) else lax.rem(k, 2)

    def copy_a(k):
        return remote(part.at[slot(k), :, :, :, 1 - core], got_a.at[k], send_a.at[k], recv_a.at[k], sibling)

    def copy_b(k):
        if not isinstance(k, int) or k != zchunk:
            if isinstance(k, int) and k >= nj:
                return remote(got_a.at[base(k), :, :, 1 - y, span(k)], got_b.at[base(k), :, :, span(k)], send_b.at[k], recv_b.at[k], across)
            return remote(got_a.at[k, :, :, 1 - y], got_b.at[k], send_b.at[k], recv_b.at[k], across)
        return remote(got_a.at[k, zhigh, zlow, 1 - y], got_d.at[k], send_b.at[k], recv_b.at[k], across)

    def copy_c(k):
        if k < nj:
            return remote(got_b.at[k], got_c.at[pl.ds(2 * (k // 2), 2)], send_c.at[k], recv_c.at[k], near)
        if k == zchunk:
            return remote(got_a.at[k, :, 1 - zlow], got_b.at[k], send_c.at[k], recv_c.at[k], near)
        return remote(got_b.at[base(k), :, 1 - zlow, span(k)], got_c.at[base(k), :, span(k)], send_c.at[k], recv_c.at[k], near)

    def copy_d(k):
        if not isinstance(k, int) or k < nj:
            return remote(got_b.at[k], got_t, send_d.at[k], recv_d.at[k], far)
        if k == zchunk:
            return remote(got_a.at[k, 1 - zhigh, zlow], got_c.at[k], send_d.at[k], recv_d.at[k], far)
        return remote(got_b.at[base(k), 1 - zhigh, zlow, span(k)], got_d.at[base(k), span(k)], send_d.at[k], recv_d.at[k], far)

    def e1(k):
        copy_a(k).wait_recv()

        for h in range(2):
            got_a[k, h] = got_a[k, h] + part[slot(k), h, :, :, core]
        if isinstance(k, int) and k == zchunk:
            copy_c(k).start()
        else:
            copy_b(k).start()
            if isinstance(k, int) and k == chunks - 1:
                copy_b(chunks).start()
        copy_a(k).wait_send()

    def e2(k):
        if k == zchunk:
            copy_c(k).wait_recv()
            for h in range(2):
                got_a[k, h, zlow] = got_a[k, h, zlow] + got_b[k, h]
            copy_d(k).start()
            return
        copy_b(k).wait_recv()
        for h in range(2):
            if k < nj:
                got_b[k, h] = got_b[k, h] + got_a[k, h, :, y]
            else:
                got_b[base(k), h, :, span(k)] = got_b[base(k), h, :, span(k)] + got_a[base(k), h, :, y, span(k)]
        if k < nj:
            @pl.when(zlow != k % 2)
            def _():
                copy_c(k).start()
        else:
            copy_c(k).start()

    def e3(k):
        if k < nj:
            @pl.when(zlow == k % 2)
            def _():
                copy_c(k).wait_recv()
                for h in range(2):
                    got_b[k, h] = got_b[k, h] + got_c[2 * (k // 2) + h]

                @pl.when(z != k)
                def _():
                    copy_d(k).start()
        elif k == zchunk:
            copy_d(k).wait_recv()
            got_a[k, zhigh, zlow] = got_a[k, zhigh, zlow] + got_c[k]
            copy_b(k).start()
        else:
            copy_c(k).wait_recv()
            for h in range(2):
                got_b[base(k), h, zlow, span(k)] = got_b[base(k), h, zlow, span(k)] + got_c[base(k), h, span(k)]
            copy_d(k).start()

    def e4(k):
        if k == zchunk:
            copy_b(k).wait_recv()
            return got_a[k, zhigh, zlow, y].astype(F32) + got_d[k].astype(F32)
        copy_d(k).wait_recv()
        return got_b[base(k), zhigh, zlow, span(k)].astype(F32) + got_d[base(k), span(k)].astype(F32)

    def tile_out(k, lhs, right):
        def side(i, _):
            cols = pl.ds(pl.multiple_of(i * half, half), half)
            v = dot_tn(lhs[:, cols], right)
            part[slot(k), i] = v.astype(BF).reshape(part.shape[2:])
            return 0
        lax.fori_loop(0, 2, side, 0)
        copy_a(k).start()

    def products_t():
        def one(t, _):
            act_copy(t).wait()

            def side(i, _):
                cols = pl.ds(pl.multiple_of(i * half, half), half)
                v = dot_tn(rhs[lax.rem(t, 2), :, cols], db2[...].reshape(N, D)).astype(BF)
                for c in range(2):
                    for s in range(4):
                        part[slot(t), s // 2, s % 2, i, c] = v[(c * 4 + s) * rows:(c * 4 + s + 1) * rows]
                return 0
            lax.fori_loop(0, 2, side, 0)
            copy_a(t).start()

            @pl.when(t < nj - 2)
            def _():
                act_copy(t + 2).start()

            @pl.when(t == nj - 2)
            def _():
                hb_copy.start()

            @pl.when(t == nj - 1)
            def _():
                x_copy.start()

            @pl.when(jnp.logical_and(t >= 1, t <= 2))
            def _():
                e1(t - 1)
            return 0
        lax.fori_loop(0, nj, one, 0)

    def products_w():
        hb_copy.wait()

        def one(j, _):
            tile_out(nj + j, rhs.at[0], gp[:, :, pl.ds(pl.multiple_of(j * D, D), D)].reshape(N, D))
            for n, steps in enumerate(AFTER_W):
                if steps:
                    run_when(j == n, steps)
            return 0
        lax.fori_loop(0, nj, one, 0)

        def side(i, _):
            cols = pl.ds(pl.multiple_of(i * half, half), half)
            v = dot_tn(c_s[:, :, cols].reshape(N, half), db1[...].reshape(N, D))
            part[slot(2 * nj), i] = v.astype(BF).reshape(part.shape[2:])
            return 0
        lax.fori_loop(0, 2, side, 0)
        copy_a(2 * nj).start()
        for step in AFTER_A.split():
            run(step)

    def products_q():
        x_copy.wait()

        def one(j, _):
            tile_out(2 * nj + 1 + j, rhs.at[1], qkv[:, :, pl.ds(pl.multiple_of(j * D, D), D)].reshape(N, D))
            for n, steps in enumerate(AFTER_Q):
                if steps:
                    run_when(j == n, steps)
            return 0
        lax.fori_loop(0, 3, one, 0)

    def store(k):
        v = e4(k)
        if k < 2 * nj:
            g_in[:, (k - nj) * D:(k - nj + 1) * D] = v
        elif k == 2 * nj:
            g_at[...] = v
        else:
            g_qkv[span(k), (base(k) - 2 * nj - 1) * D:(base(k) - 2 * nj) * D] = v

    def store_w_out():
        copy_d(z).wait_recv()
        for s in range(4):
            g_out[s * rows:(s + 1) * rows, :] = got_b[z, s // 2, s % 2].astype(F32) + got_t[s // 2, s % 2].astype(F32)

    def run(step):
        what, k = step[0], int(step[1:])
        if what == "v":
            vec_step(k)
        elif what == "d":
            if k >= nj:
                store(k)
            elif k == nj - 1:
                store_w_out()
        else:
            {"a": e1, "b": e2, "c": e3}[what](k)

    def run_when(where, steps):
        @pl.when(where)
        def _():
            for step in steps.split():
                run(step)

    def one_pass(step, _):
        m = jnp.minimum(step, M - 1)
        norms = norm_copies(m)
        ins = in_copies(m)
        forming = jnp.logical_or(jnp.logical_and(step == M - 1, sec == 0), jnp.logical_and(step == M, sec != 0))
        behind = jnp.logical_and(step == M, sec != 0)

        @pl.when(step < M)
        def _():
            norm_pass(m, norms)

        @pl.when(forming)
        def _():
            products_t()

        @pl.when(step < M)
        def _():
            token_pass(m, norms, ins)

        @pl.when(forming)
        def _():
            run_when(behind, " ".join(AFTER_TOKENS))
            products_w()
            run_when(behind, " ".join(AFTER_PAIR))

        @pl.when(step < M)
        def _():
            attention_pass(m)
        return 0

    def norm_pass(m, norms):
        norms = norm_copies(m)
        ins = in_copies(m)
        mem = members(seg[m])
        kcode[...], qcode[...] = codes(mem)
        norms[0].wait()

        @pl.when(sec != 0)
        def _():
            @pl.when(m == 0)
            def _():
                gathered[...] = msgs0[...]

            @pl.when(m == 1)
            def _():
                for d in range(1, peers):
                    msg_copy(d).wait()
                gathered[...] = msgs[...]
            head(m)

        def norm_rows(r):
            dy = dr[r, :]
            zz = z2[r, :].astype(F32)
            dr2 = norm_pull(zz, s12[m, r, 1:2], g2[...].astype(F32), dy)
            vacc[0] += rowsum8(dy * zz)
            vacc[1] += rowsum8(dy)
            d2 = dr2.astype(BF)
            dr[r, :] = dr2
            db2[m, r, :] = d2
            vacc[2] += rowsum8(d2.astype(F32))

        @pl.when(sec == 0)
        def _():
            def norm_step(i, _):
                r = pl.ds(pl.multiple_of(i * xb, xb), xb)
                handoff(m, i).wait_recv()
                dr[r, :] = dyx[m, r, :].astype(F32)
                norm_rows(r)
                return 0
            lax.fori_loop(0, nx, norm_step, 0)

        @pl.when(sec != 0)
        def _():
            dp3 = jnp.concatenate(split3(jnp.concatenate([dps[pl.ds(pl.multiple_of(m * SL, SL), SL), :], jnp.zeros((16 - SL, D), F32)], axis=0)), axis=0)
            dr[...] = dot_tn(jnp.concatenate([mem, mem, mem], axis=0), dp3)
            for i in range(nb):
                norm_rows(slice(i * tb, (i + 1) * tb))

        @pl.when(m == 0)
        def _():
            pl.semaphore_wait(barrier, peers)

            @pl.when(sec != 0)
            def _():
                for m in range(M):
                    pooled, radius, _ = documents(members(seg[m]), pool[m])
                    pooled_s[m * SL:(m + 1) * SL, :] = pooled
                    if m == 1:
                        msgs[me] = message(pooled * radius, pairs[m:m + 1, :])
                for d in range(1, peers):
                    msg_copy(d).start()
                pool_copy.start()

    def token_pass(m, norms, ins):
        @pl.when(jnp.logical_and(m == M - 1, sec != 0))
        def _():
            loss_copy.start()

        @pl.when(m == 0)
        def _():
            for w in wcp[:3]:
                w.wait()
            in_copies(0)[2].start()
            wcp[3].start()
            for n in range(1, M):
                for a in in_copies(n):
                    a.start()
            act_copy(0).start()
            act_copy(1).start()
        norms[1].wait()
        ins[0].wait()
        ins[1].wait()
        for i in range(nb):
            r = slice(i * tb, (i + 1) * tb)
            d2 = db2[m, r, :]
            dh = dr[r, :]
            dfs = [dot_nt(d2, wout[:D, :])]
            for j in range(nj):
                cols = slice(j * D, (j + 1) * D)
                if j + 1 < nj:
                    dfs.append(dot_nt(d2, wout[(j + 1) * D:(j + 2) * D, :]))
                dub = (dfs[j] * gp[m, r, cols].astype(F32)).astype(BF)
                gp[m, r, cols] = dub
                bacc[:, cols] += rowsum8(dub.astype(F32))
                dh = dh + dot_nt(dub, win[:, cols])
            dr[r, :] = dh
            run_when(jnp.logical_and(m == M - 1, sec == 0), AFTER_TOKENS[i])
        for i in range(nb):
            r = slice(i * tb, (i + 1) * tb)
            dh = dr[r, :]
            zz = z1[r, :].astype(F32)
            d1 = norm_pull(zz, s12[m, r, 0:1], g1[...].astype(F32), dh)
            vacc[3] += rowsum8(dh * zz)
            vacc[4] += rowsum8(dh)
            dr[r, :] = d1
            d1 = d1.astype(BF)
            db1[m, r, :] = d1
            vacc[5] += rowsum8(d1.astype(F32))
            dcb = dot_nt(d1, wat[...]).astype(BF)
            dc[r, :] = dcb
            prod = dcb.astype(F32) * c_s[m, r, :].astype(F32)
            hi = prod.astype(BF)
            low = (prod - hi.astype(F32)).astype(BF)
            delta[:, r] = dot_nt(indicator, hi) + dot_nt(indicator, low)
        @pl.when(m < M - 1)
        def _():
            for cp in norm_copies(m + 1):
                cp.start()
        ins[2].wait()

    def attention_pass(m):
        for p in range(HEADS // 2):
            cols = slice(p * 128, (p + 1) * 128)
            kcols = slice(D + p * 128, D + (p + 1) * 128)
            vcols = slice(2 * D + p * 128, 2 * D + (p + 1) * 128)
            q2 = qkv[m, :, cols] * (HEAD_DIM ** -0.5)
            qh = [jnp.where(low_half, q2, qcode[...]), jnp.where(low_half, qcode[...], q2)]
            dc2 = dc[:, cols]
            dqt = jnp.zeros((128, T), F32)
            for i in range(T // kb):
                r = slice(i * kb, (i + 1) * kb)
                k2 = qkv[m, r, kcols]
                v2 = qkv[m, r, vcols]
                kc = kcode[r, :]
                dks, dvs = [], []
                for h in range(2):
                    pick = low_half if h == 0 else jnp.logical_not(low_half)
                    kh = jnp.where(low_half, k2, kc) if h == 0 else jnp.where(low_half, kc, k2)
                    pt = jnp.exp(dot_nt(kh, qh[h]) - lse[m, 2 * p + h:2 * p + h + 1, :])
                    dpt = dot_nt(jnp.where(pick, v2, 0), dc2)
                    da = (pt * (dpt - delta[2 * p + h:2 * p + h + 1, :])).astype(BF)
                    dvs.append(dot(pt.astype(BF), dc2))
                    dks.append(dot(da, q2))
                    dqt = dqt + dot_tn(jnp.where(pick, k2, 0), da)
                qkv[m, r, kcols] = jnp.where(low_half, dks[0], dks[1]).astype(BF)
                qkv[m, r, vcols] = jnp.where(low_half, dvs[0], dvs[1]).astype(BF)
            qkv[m, :, cols] = (jnp.transpose(dqt) * (HEAD_DIM ** -0.5)).astype(BF)
            if AFTER_PAIR[p]:
                run_when(jnp.logical_and(m == M - 1, sec == 0), AFTER_PAIR[p])
        @pl.when(m == 0)
        def _():
            wcp[3].wait()

        def dx_step(i, _):
            r = pl.ds(pl.multiple_of(i * xb, xb), xb)
            dyx[m, r, :] = (dr[r, :] + dot_nt(qkv[m, r, :], wqkv[...])).astype(BF)

            @pl.when(sec != 0)
            def _():
                handoff(m, i).start()
            vacc[6] += rowsum8(qkv[m, r, :D].astype(F32))
            vacc[7] += rowsum8(qkv[m, r, 2 * D:].astype(F32))
            return 0
        lax.fori_loop(0, nx, dx_step, 0)

        @pl.when(sec == 0)
        def _():
            out_copy(m).start()
            dx_copy(m).start()

    lax.fori_loop(0, M + 1, one_pass, 0)

    vec = [remote(va.at[i], vb.at[i], s.at[chunks + 1], r.at[chunks + 1], target) for i, (s, r, target) in enumerate(
        ((send_a, recv_a, sibling), (send_b, recv_b, across), (send_c, recv_c, near), (send_d, recv_d, far)))]

    def vec_step(i):
        vec[i].wait_recv()
        total = va[i] + vb[i]
        if i < 3:
            va[i + 1] = total
            vec[i + 1].start()
        else:
            vec_o[...] = total
    va[0] = jnp.concatenate([jnp.sum(vacc[...], axis=1)]
        + [jnp.sum(bacc[:, j * D:(j + 1) * D], axis=0, keepdims=True) for j in range(nj)] + [jnp.zeros((8 - nj, D), F32)], axis=0)
    vec[0].start()
    for step in BEFORE_Q.split():
        run(step)
    products_q()
    for step in AT_THE_END.split():
        run(step)

    @pl.when(sec == 0)
    def _():
        pool_copy.wait_recv()
        loss_copy.wait_recv()
        pooled_o[...] = pooled_r[:, :half]
        loss_o[...] = loss_r[...]
        for m in range(M):
            dx_copy(m).wait_send()
            out_copy(m).wait()

    @pl.when(sec != 0)
    def _():
        pool_copy.wait_send()
        loss_copy.wait_send()
        pooled_o[...] = pooled_s[:, half:]
        loss_o[...] = loss_s[...]
        for m in range(M):
            for i in range(nx):
                handoff(m, i).wait_send()
            dx_copy(m).wait_recv()
    for v in vec:
        v.wait_send()
    for k in range(chunks + 1):
        copy_b(k).wait_send()
        if k < nj:
            @pl.when(zlow != k % 2)
            def _():
                copy_c(k).wait_send()

            @pl.when(jnp.logical_and(zlow == k % 2, z != k))
            def _():
                copy_d(k).wait_send()
        else:
            copy_c(k).wait_send()
            copy_d(k).wait_send()


def stack_back(seg, pool, pairs, msgs0, stash, weights, tb=256, xb=128, kb=256):
    x, qkv, lse, c, z1, s12, hb, gp, act, z2 = stash
    wqkv, bq, bv, wat, bat, g1, b1, win, bin_, wout, bout, g2, b2 = weights
    M, T, D = c.shape
    N = M * T
    FF = win.shape[1]
    count = lax.axis_size("dp")
    rows = D // count
    chunks = (4 * D + 2 * FF) // D
    SL = 8
    sds = jax.ShapeDtypeStruct
    out_shape = (sds((16, D), F32), sds((M * SL, D // 2), F32), sds((M * SL, 128), F32), sds((rows, 3 * D), F32), sds((rows, D), F32), sds((rows, FF), F32),
        sds((FF // count, D), F32), sds((M, T, D), BF), sds((M, T, D // 2), BF))
    out_specs = (VM,) * 7 + (ANY, ANY)
    V = pltpu.VMEM
    S = pltpu.SemaphoreType.DMA
    nx = T // xb
    nj = FF // D
    piece = (rows, D)
    scratch = [V((M, T, D), BF), V((D, 3 * D), BF), V((D, D), BF), V((D, FF), BF), V((FF, D), BF),
        V((M, T, 3 * D), BF), V((M, T, D), BF), V((T, D), BF), V((M, T, FF), BF), V((T, D), BF),
        V((T, D), F32), V((T, D), BF), V((16, T), F32), V((M, T, D), BF), V((M, T, D), BF), V((8, 8, D), F32), V((8, FF), F32),
        V((count, 16, D // 2 + 128), BF), V((M * SL, D), F32), V((count * SL, 128), F32), V((count * SL, D), F32), V((M * SL, D), F32), V((M * SL, 128), F32), V((M * SL, D), F32), V((M * SL, 128), F32),
        V((T, 128), BF), V((T, 128), BF), V((count, 16, D // 2 + 128), BF), V((2, N, D), BF), V((2, 2, 2, 2, 2) + piece, BF), V((chunks, 2, 2, 2) + piece, BF), V((chunks, 2, 2) + piece, BF),
        V((chunks, 2) + piece, BF), V((chunks,) + piece, BF), V((2, 2) + piece, BF), V((4, 16, D), F32), V((4, 16, D), F32),
        S((M, 5)), S((4,)), S((2 + nj,)), S((M,)), S((M, nx)), S((M, nx)), S((count - 1,)), S((count - 1,)), S((4,)), S((M, 2))]
    scratch += [S((chunks + 2,)) for _ in range(8)]
    in_specs = (VM,) * 6 + (ANY,) * 12 + (VM, VM)
    return pl.pallas_call(functools.partial(back_kernel, tb, xb, kb), out_shape=out_shape, in_specs=in_specs, out_specs=out_specs,
        scratch_shapes=scratch, compiler_params=pltpu.CompilerParams(vmem_limit_bytes=62 * 2**20, collective_id=3, has_side_effects=True),
        name="stack_back")(seg, pool, pairs, msgs0, lse, s12, z2, gp, z1, c, qkv, hb.reshape(N, D), x.reshape(N, D), act,
            wout, win, wat, wqkv, g1, g2)


def finish_kernel(vec, pooled, loss, g_qkv, g_at, g_in, g_out, dx_h, dxr_h,
    pooled_o, loss_o, gx_o, qkv_o, at_o, in_o, out_o, *rest):
    small, buf, wide_buf, bufs, sem = rest[:9], rest[9], rest[10], rest[11:15], rest[15]
    came = [pltpu.make_async_copy(a, b, sem.at[1 + i]) for i, (a, b) in enumerate(zip((g_qkv, g_at, g_in, g_out), bufs))]
    goes = [pltpu.make_async_copy(b, a, sem.at[5 + i]) for i, (a, b) in enumerate(zip((qkv_o, at_o, in_o, out_o), bufs))]
    goes += [pltpu.make_async_copy(wide_buf, gx_o, sem.at[9])]
    sec = lax.axis_index("section")
    me = lax.axis_index("dp")
    half = buf.shape[2]

    @pl.when(sec == 0)
    def _():
        pltpu.make_async_copy(dx_h.at[:, :, pl.ds(0, half)], buf, sem.at[0]).start()

    @pl.when(sec != 0)
    def _():
        pltpu.make_async_copy(dxr_h, buf, sem.at[0]).start()
    for cp in came:
        cp.start()
    pltpu.make_async_copy(dxr_h, buf, sem.at[0]).wait()
    wide_buf[...] = buf[...].astype(F32)
    goes[4].start()
    for a, b in zip(came, goes):
        a.wait()
        b.start()
    SL = 8
    lane = lax.broadcasted_iota(jnp.int32, (SL, 128), 1) == lax.broadcasted_iota(jnp.int32, (SL, 128), 0)
    for m in range(pooled_o.shape[0]):
        pooled_o[m] = pooled[m * SL:m * SL + SEGS, :]
        loss_o[m:m + 1, :] = jnp.sum(jnp.where(lane, loss[m * SL:(m + 1) * SL, :], 0.0), axis=0, keepdims=True)[:, :SEGS]
    D = vec.shape[1]
    width, wide = small[0].shape[1], small[8].shape[1]
    parts = split3(vec[...])

    def columns(start, size):
        pick = lax.broadcasted_iota(jnp.int32, (D, size), 0) == lax.broadcasted_iota(jnp.int32, (D, size), 1) + start
        pick = jnp.where(pick, 1.0, 0.0).astype(BF)
        return (dot(parts[0], pick) + dot(parts[1], pick)) + dot(parts[2], pick)
    v = columns(me * width, 128)
    for i in range(8):
        small[i][...] = v[i:i + 1, :width]
    per = D // wide
    v = columns(lax.rem(me, per) * wide, 256)
    row = lax.broadcasted_iota(jnp.int32, (16, 256), 0) == 8 + lax.div(me, per)
    small[8][...] = jnp.sum(jnp.where(row, v, 0.0), axis=0, keepdims=True)[:, :wide]
    for cp in goes:
        cp.wait()


def finish(vec, pooled, loss, g_qkv, g_at, g_in, g_out, dx, dxr):
    M, T, D = dx.shape
    count = lax.axis_size("dp")
    sds = jax.ShapeDtypeStruct
    f = lambda a: sds(a.shape, F32)
    out_shape = (sds((M, SEGS, D // 2), F32), sds((M, SEGS), F32), sds((M, T, D // 2), F32), f(g_qkv), f(g_at), f(g_in), f(g_out)) + tuple(
        sds((1, D // count), F32) for _ in range(8)) + (sds((1, g_in.shape[1] // count), F32),)
    return pl.pallas_call(finish_kernel, out_shape=out_shape, in_specs=(VM,) * 3 + (ANY,) * 6, out_specs=(VM,) * 2 + (ANY,) * 5 + (VM,) * 9,
        scratch_shapes=[pltpu.VMEM((M, T, D // 2), BF), pltpu.VMEM((M, T, D // 2), F32)] + [pltpu.VMEM(g.shape, F32) for g in (g_qkv, g_at, g_in, g_out)]
        + [pltpu.SemaphoreType.DMA((10,))],
        compiler_params=pltpu.CompilerParams(vmem_limit_bytes=VMEM_LIMIT), name="finish")(vec, pooled, loss, g_qkv, g_at, g_in, g_out, dx, dxr)


def contrast_head(pool, seg, pairs, all_pairs):
    M, S = pairs.shape
    D = pool.shape[-1]
    counts = jnp.sum((seg[:, :, None] == jnp.arange(SEGS)).astype(F32), axis=1)[:, :, None]
    pooled = pool[:, :SEGS] / counts
    radius = lax.rsqrt(jnp.sum(pooled * pooled, axis=-1, keepdims=True) + UNIT_EPS)
    unit = (pooled * radius).astype(BF)
    every = lax.all_gather(unit, "dp", axis=1, tiled=True)
    total = every.shape[1]
    start = lax.axis_index("dp") * S
    logits = TEMPER * jnp.einsum("mgd,mkd->mgk", every, every, preferred_element_type=F32)
    cols = jnp.arange(total)
    logits = jnp.where(cols[:, None] == cols[None, :], -MASK_FILL, logits)
    peak = jnp.max(logits, axis=-1, keepdims=True)
    exponent = jnp.exp(logits - peak)
    denom = jnp.sum(exponent, axis=-1, keepdims=True)
    target = cols[None, None, :] == all_pairs[:, :, None]
    loss = peak[..., 0] + jnp.log(denom[..., 0]) - jnp.sum(jnp.where(target, logits, 0.0), axis=-1)
    dl = (exponent / denom - target.astype(F32)).astype(BF)
    rows = lax.dynamic_slice_in_dim(dl, start, S, 1)
    columns = lax.dynamic_slice_in_dim(dl, start, S, 2)
    dn = TEMPER * (jnp.einsum("mgk,mkd->mgd", rows, every, preferred_element_type=F32)
        + jnp.einsum("mkg,mkd->mgd", columns, every, preferred_element_type=F32))
    dp = radius * dn - radius * radius * radius * jnp.sum(pooled * dn, axis=-1, keepdims=True) * pooled
    loss = lax.dynamic_slice_in_dim(loss, start, S, 1)
    return pooled, loss, jnp.pad(dp / counts, ((0, 0), (0, 16 - SEGS), (0, 0)))


def scattered(grads):
    count = lax.axis_size("dp")
    packed = jnp.concatenate([g.reshape(count, -1) for g in grads], axis=1)
    part = lax.psum_scatter(packed, "dp", scatter_dimension=0, tiled=True)[0].astype(F32)
    outs, at = [], 0
    for g in grads:
        size = g.size // count
        outs.append(part[at:at + size].reshape((1, g.shape[0] // count) + g.shape[1:]))
        at += size
    return outs


def swapped(value):
    return lax.ppermute(value, "section", [(0, 1), (1, 0)])


def local(hidden_in, seg_ids, pair_ids, w_qkv, b_query, b_value, w_attn_out, b_attn_out, ln1_gain, ln1_bias, w_in, b_in, w_out, b_out, ln2_gain, ln2_bias):
    M, _, T, D = hidden_in.shape
    sec = lax.axis_index("section")
    first = sec == 0
    weights = (w_qkv[0], b_query, b_value, w_attn_out[0], b_attn_out, ln1_gain, ln1_bias, w_in[0], b_in, w_out[0], b_out, ln2_gain, ln2_bias)
    half = D // 2
    count = lax.axis_size("dp")
    pool, x, qkv, lse, c, z1, s12, hb, gp, act, z2, msgs = stack_fwd(hidden_in[:, 0], seg_ids, pair_ids, weights, count if count == 16 else 0)
    if count == 16:
        parts = stack_back(seg_ids, pool, pair_ids, msgs, (x, qkv, lse, c, z1, s12, hb, gp, act, z2), weights)
        pooled, loss, grad_input, g_qkv, g_at, g_in, g_out, gg2, gb2, gbo, gg1, gb1, gba, gbq, gbv, gbi = finish(*parts)
        pooled_out, loss_out = pooled, loss
        g_qkv, g_at, g_in, g_out = (g[None] for g in (g_qkv, g_at, g_in, g_out))
    else:
        seg = seg_ids[:, 0]
        all_pairs = lax.all_gather(pair_ids, "dp", axis=1, tiled=True)
        pooled, loss, dp = contrast_head(pool, seg, pair_ids, all_pairs)
        vec, dx, dxb, db2, du, db1, dqkv = stack_bwd(seg, dp, (qkv, lse, c, z1, s12, gp, z2), weights)
        act = jnp.moveaxis(act, 0, 1).reshape(M, T, -1)
        big = [jnp.einsum("mta,mtb->ab", a, b, preferred_element_type=F32).astype(BF) for a, b in ((x, dqkv), (c, db1), (hb, du), (act, db2))]
        g_qkv, g_at, g_in, g_out = scattered(big)
        small = scattered([vec[i] for i in range(8)] + [vec[8:8 + w_in.shape[2] // D].reshape(-1)])
        gg2, gb2, gbo, gg1, gb1, gba, gbq, gbv, gbi = small
        kept = lax.dynamic_slice_in_dim(dx, sec * half, half, 2)
        sent = lax.dynamic_slice_in_dim(dxb, (1 - sec) * half, half, 2)
        grad_input = jnp.where(first, kept, swapped(sent).astype(F32))
        pooled_kept = lax.dynamic_slice_in_dim(pooled, sec * half, half, 2)
        pooled_sent = lax.dynamic_slice_in_dim(pooled, (1 - sec) * half, half, 2).astype(BF)
        pooled_out = jnp.where(first, swapped(pooled_sent).astype(F32), pooled_kept)
        loss_out = jnp.where(first, swapped(loss.astype(BF)).astype(F32), loss)
    return (pooled_out, loss_out, grad_input[:, None], g_qkv, gbq, gbv, g_at, gba, gg1, gb1, g_in, gbi, g_out, gbo, gg2, gb2)


def solution(mesh):
    in_specs = (
        P(None, "dp", None, None),
        P(None, "dp", None),
        P(None, "dp"),
        P("section", None, None),
        P("section", None),
        P("section", None),
        P("section", None, None),
        P("section", None),
        P("section", None),
        P("section", None),
        P("section", None, None),
        P("section", None),
        P("section", None, None),
        P("section", None),
        P("section", None),
        P("section", None),
    )
    out_specs = (
        P(None, "dp", "section"),
        P(None, "dp"),
        P(None, "dp", None, "section"),
        P("section", "dp", None),
        P("section", "dp"),
        P("section", "dp"),
        P("section", "dp", None),
        P("section", "dp"),
        P("section", "dp"),
        P("section", "dp"),
        P("section", "dp", None),
        P("section", "dp"),
        P("section", "dp", None),
        P("section", "dp"),
        P("section", "dp"),
        P("section", "dp"),
    )
    return jax.shard_map(local, mesh=mesh, in_specs=in_specs, out_specs=out_specs, check_vma=False)
```

```python
import functools
import jax, jax.numpy as jnp
from jax import lax
from jax.experimental import pallas as pl
from jax.experimental.pallas import tpu as pltpu
from jax.sharding import PartitionSpec as P

HEADS = 12
HEAD_DIM = 64
SEGS = 4
UNIT_EPS = 1e-06
TEMPER = 20.0
MASK_FILL = 1000000000.0
NORM_EPS = 1e-12
BF = jnp.bfloat16
F32 = jnp.float32
VMEM_LIMIT = 60 * 2**20
MESH = pl.DeviceIdType.MESH
ANY = pl.BlockSpec(memory_space=pl.ANY)
VM = pl.BlockSpec(memory_space=pltpu.VMEM)


def dot(a, b):
    return jnp.dot(a, b, preferred_element_type=F32)


def dot_nt(a, b):
    return lax.dot_general(a, b, (((1,), (1,)), ((), ())), preferred_element_type=F32)


def dot_tn(a, b):
    return lax.dot_general(a, b, (((0,), (0,)), ((), ())), preferred_element_type=F32)


def split3(v):
    hi = v.astype(BF)
    rest = v - hi.astype(F32)
    mid = rest.astype(BF)
    low = (rest - mid.astype(F32)).astype(BF)
    return hi, mid, low


def members(seg_row):
    rows = lax.broadcasted_iota(jnp.int32, (16, seg_row.shape[1]), 0)
    return jnp.where(rows == seg_row, 1.0, 0.0).astype(BF)


def normed_rows(rows):
    centre = rows - jnp.mean(rows, axis=-1, keepdims=True)
    scale = lax.rsqrt(jnp.mean(centre * centre, axis=-1, keepdims=True) + NORM_EPS)
    return centre * scale, scale


def gelu_pair(u):
    mag = jnp.abs(u)
    t = 1.0 / (1.0 + (0.3275911 * 0.7071067811865476) * mag)
    e = jnp.exp(-0.5 * (u * u))
    poly = t * (0.127414796 + t * (-0.142248368 + t * (0.7107068705 + t * (-0.7265760135 + t * 0.5307027145))))
    tail = poly * e
    cdf = jnp.where(u >= 0.0, 1.0 - tail, tail)
    return u * cdf, cdf + (u * 0.3989422804014327) * e


def codes(mem):
    lanes = lax.rem(lax.broadcasted_iota(jnp.int32, (16, 128), 1), HEAD_DIM)
    pick = jnp.where(lanes == lax.broadcasted_iota(jnp.int32, (16, 128), 0), 1.0, 0.0)
    pick = jnp.where(lanes < SEGS, pick, 0.0).astype(BF)
    key_code = dot_tn(mem, pick)
    active = jnp.where(lanes[:1] < SEGS, 1.0, 0.0)
    return key_code.astype(BF), ((key_code - active) * MASK_FILL).astype(BF)


def documents(mem, pool):
    counts = jnp.maximum(jnp.sum(mem.astype(F32), axis=1, keepdims=True)[:8], 1.0)
    pooled = pool[:8, :] / counts
    radius = lax.rsqrt(jnp.sum(pooled * pooled, axis=-1, keepdims=True) + UNIT_EPS)
    return pooled, radius, counts


def message(unit, pairs):
    half = unit.shape[1] // 2
    tag = [jnp.broadcast_to(pairs[:, j:j + 1].astype(F32), (1, 128)) for j in range(SEGS)]
    tag = jnp.concatenate(tag + [jnp.zeros((8 - SEGS, 128), F32)], axis=0)
    return jnp.concatenate([jnp.concatenate([unit[:, :half], tag], axis=1), jnp.concatenate([unit[:, half:], tag], axis=1)], axis=0).astype(BF)


def fwd_kernel(tb, peers,
    x_h, seg, pairs, wqkv_h, bq, bv, wat_h, bat, g1, b1, win_h, bin_, wout_h, bout, g2, b2,
    pool_o, x_o, qkv_h, lse_o, c_h, z1_h, s12_o, hb_h, gp_h, act_h, z2_h, msgs_o,
    x_s, wqkv, wat, win, wout, qkv, c_s, hb_s, z1_s, gp_s, act_s, z2_s, y_s, yf, msgs, kcode, qcode,
    insem, wsem, outsem, send_sem, recv_sem, msg_send, msg_recv):
    sec = lax.axis_index("section")
    me = lax.axis_index("dp")
    other = {"section": 1 - sec}
    M, T, D = x_s.shape
    FF = win.shape[1]
    nb = T // tb

    ws = [pltpu.make_async_copy(a, b, wsem.at[i]) for i, (a, b) in enumerate(
        ((wqkv_h, wqkv), (wat_h, wat), (win_h, win), (wout_h, wout)))]
    barrier = pltpu.get_barrier_semaphore()

    @pl.when(sec == 0)
    def _():
        pltpu.make_async_copy(x_h.at[0], x_s.at[0], insem.at[0]).start()
    ws[0].start()
    pl.semaphore_signal(barrier, inc=1, device_id=other, device_id_type=MESH)
    for d in range(1, peers):
        pl.semaphore_signal(barrier, inc=1, device_id={"dp": lax.rem(me + d, peers)}, device_id_type=MESH)

    lane = lax.broadcasted_iota(jnp.int32, (1, 128), 1)
    low_half = lane < HEAD_DIM

    def block(start):
        return pl.ds(start if isinstance(start, int) else pl.multiple_of(start, tb), tb)

    def out_copies(m, i):
        r = block(i * tb)
        return [pltpu.make_async_copy(a.at[m, r], b.at[m, r], outsem.at[m, i, j]) for j, (a, b) in enumerate(
            ((c_s, c_h), (hb_s, hb_h), (z1_s, z1_h), (z2_s, z2_h)))]

    def wide_copies(m, i, j):
        r = block(i * tb)
        cols = slice(j * D, (j + 1) * D)
        return [pltpu.make_async_copy(gp_s.at[m, r, cols], gp_h.at[m, r, cols], outsem.at[m, i, 4 + 2 * j]),
            pltpu.make_async_copy(act_s.at[m, r, cols], act_h.at[j, block(m * T + i * tb)], outsem.at[m, i, 5 + 2 * j])]

    def whole_copies(m):
        return [pltpu.make_async_copy(a.at[m], b.at[m], outsem.at[m, nb, j]) for j, (a, b) in enumerate(((x_s, x_o), (qkv, qkv_h)))]

    def handoff(m, i):
        r = block(i * tb)
        return pltpu.make_async_remote_copy(src_ref=y_s.at[m, r], dst_ref=x_s.at[m, r], send_sem=send_sem.at[m, i],
            recv_sem=recv_sem.at[m, i], device_id=other, device_id_type=MESH)

    def msg_copy(d):
        return pltpu.make_async_remote_copy(src_ref=msgs.at[me], dst_ref=msgs.at[me], send_sem=msg_send.at[d - 1], recv_sem=msg_recv.at[d - 1],
            device_id={"dp": lax.rem(me + d, peers)}, device_id_type=MESH)

    def micro_step(m, _):
        mem = members(seg[m])
        kcode[...], qcode[...] = codes(mem)

        @pl.when(sec == 0)
        def _():
            pltpu.make_async_copy(x_h.at[m], x_s.at[m], insem.at[m]).wait()

        @pl.when(m == 0)
        def _():
            ws[0].wait()
            for w in ws[1:]:
                w.start()

            @pl.when(sec == 0)
            def _():
                for n in range(1, M):
                    pltpu.make_async_copy(x_h.at[n], x_s.at[n], insem.at[n]).start()

        def qkv_step(i, _):
            r = block(i * tb)

            @pl.when(sec != 0)
            def _():
                handoff(m, i).wait_recv()
            xi = x_s[m, r, :]
            for j, b in ((0, bq), (1, None), (2, bv)):
                cols = slice(j * D, (j + 1) * D)
                v = dot(xi, wqkv[:, cols])
                if b is not None:
                    v = v + b[...].astype(F32)
                qkv[m, r, cols] = v.astype(BF)
            return 0
        lax.fori_loop(0, nb, qkv_step, 0)
        for cp in whole_copies(m):
            cp.start()
        ones = jnp.ones((T, 128), BF)
        def block_step(i, _):
            r = block(i * tb)
            key_code = kcode[...]
            qc = qcode[r, :]
            lses = jnp.zeros((tb, 128), F32)
            for p in range(HEADS // 2):
                cols = slice(p * 128, (p + 1) * 128)
                k2 = qkv[m, :, D + p * 128:D + (p + 1) * 128]
                v2 = jnp.concatenate([qkv[m, :, 2 * D + p * 128:2 * D + (p + 1) * 128], ones], axis=1)
                q2 = qkv[m, r, cols] * (HEAD_DIM ** -0.5)
                halves = []
                for h in range(2):
                    if h == 0:
                        s = dot_nt(jnp.where(low_half, q2, qc), jnp.where(low_half, k2, key_code))
                    else:
                        s = dot_nt(jnp.where(low_half, qc, q2), jnp.where(low_half, key_code, k2))
                    mx = jnp.max(s, axis=-1, keepdims=True)
                    e = jnp.exp(s - mx).astype(BF)
                    c = dot(e, v2)
                    l = c[:, 128:]
                    halves.append(c[:, :128] / l)
                    lses = jnp.where(lane == 2 * p + h, mx + jnp.log(l), lses)
                c_s[m, r, cols] = jnp.where(low_half, halves[0], halves[1]).astype(BF)
            lse_o[m, :, r] = jnp.transpose(lses)[:16, :]

            @pl.when(jnp.logical_and(m == 0, i == 0))
            def _():
                for w in ws[1:]:
                    w.wait()
                pl.semaphore_wait(barrier, max(peers, 1))
            r1 = x_s[m, r, :].astype(F32) + dot(c_s[m, r, :], wat[...]) + bat[...].astype(F32)
            z, scale = normed_rows(r1)
            acc = z * g1[...].astype(F32) + b1[...].astype(F32)
            hi = acc.astype(BF)
            hb_s[m, r, :] = hi
            z1_s[m, r, :] = z.astype(BF)
            s12_o[m, r, 0:1] = scale
            outs = out_copies(m, i)
            for cp in outs[:3]:
                cp.start()
            acc = acc + bout[...].astype(F32)
            nj = FF // D
            us = [dot(hi, win[:, :D])]
            for j in range(nj):
                cols = slice(j * D, (j + 1) * D)
                if j + 1 < nj:
                    us.append(dot(hi, win[:, (j + 1) * D:(j + 2) * D]))
                f, gp = gelu_pair(us[j] + bin_[:, cols].astype(F32))
                f = f.astype(BF)
                act_s[m, r, cols] = f
                gp_s[m, r, cols] = gp.astype(BF)
                acc = acc + dot(f, wout[cols, :])
                for cp in wide_copies(m, i, j):
                    cp.start()
            z, scale = normed_rows(acc)
            y = z * g2[...].astype(F32) + b2[...].astype(F32)
            y_s[m, r, :] = y.astype(BF)

            @pl.when(sec == 0)
            def _():
                handoff(m, i).start()
            z2_s[m, r, :] = z.astype(BF)
            s12_o[m, r, 1:2] = scale
            yf[r, :] = y
            outs[3].start()
            return 0
        lax.fori_loop(0, nb, block_step, 0)

        @pl.when(sec != 0)
        def _():
            hi, mid, low = split3(yf[...])
            pool = (dot(mem, hi) + dot(mem, mid)) + dot(mem, low)
            pool_o[m] = pool
            if peers:
                @pl.when(m == 0)
                def _():
                    pooled, radius, _ = documents(mem, pool)
                    msgs[me] = message(pooled * radius, pairs[0:1, :])
                    for d in range(1, peers):
                        msg_copy(d).start()
        return 0
    lax.fori_loop(0, M, micro_step, 0)

    @pl.when(sec == 0)
    def _():
        pool_o[...] = jnp.zeros_like(pool_o)
        msgs_o[...] = jnp.zeros_like(msgs_o)

    if peers:
        @pl.when(sec != 0)
        def _():
            for d in range(1, peers):
                msg_copy(d).wait()
            msgs_o[...] = msgs[...]
    for m in range(M):
        for cp in whole_copies(m):
            cp.wait()
        for i in range(nb):
            for cp in out_copies(m, i) + sum((wide_copies(m, i, j) for j in range(FF // D)), []):
                cp.wait()

    @pl.when(sec == 0)
    def _():
        for m in range(M):
            for i in range(nb):
                handoff(m, i).wait_send()


def stack_fwd(x, seg, pairs, weights, peers, tb=256):
    M, T, D = x.shape
    FF = weights[7].shape[1]
    sds = jax.ShapeDtypeStruct
    out_shape = (sds((M, 16, D), F32), sds((M, T, D), BF), sds((M, T, 3 * D), BF), sds((M, 16, T), F32), sds((M, T, D), BF),
        sds((M, T, D), BF), sds((M, T, 2), F32), sds((M, T, D), BF), sds((M, T, FF), BF), sds((FF // D, M * T, D), BF), sds((M, T, D), BF), sds((max(peers, 1), 16, D // 2 + 128), BF))
    out_specs = (VM, ANY, ANY, VM, ANY, ANY, VM, ANY, ANY, ANY, ANY, VM)
    V = pltpu.VMEM
    S = pltpu.SemaphoreType.DMA
    nb = T // tb
    scratch = [V((M, T, D), BF), V((D, 3 * D), BF), V((D, D), BF), V((D, FF), BF), V((FF, D), BF), V((M, T, 3 * D), BF),
        V((M, T, D), BF), V((M, T, D), BF), V((M, T, D), BF), V((M, T, FF), BF), V((M, T, FF), BF), V((M, T, D), BF), V((M, T, D), BF),
        V((T, D), F32), V((max(peers, 1), 16, D // 2 + 128), BF), V((T, 128), BF), V((T, 128), BF), S((M,)), S((4,)), S((M, nb + 1, 4 + 2 * (FF // D))), S((M, nb)), S((M, nb)),
        S((max(peers, 2) - 1,)), S((max(peers, 2) - 1,))]
    in_specs = (ANY, VM, VM, ANY, VM, VM, ANY, VM, VM, VM, ANY, VM, ANY, VM, VM, VM)
    return pl.pallas_call(functools.partial(fwd_kernel, tb, peers), out_shape=out_shape, in_specs=in_specs, out_specs=out_specs,
        scratch_shapes=scratch, compiler_params=pltpu.CompilerParams(vmem_limit_bytes=VMEM_LIMIT, collective_id=0, has_side_effects=True),
        name="stack_fwd")(x, seg, pairs, *weights)


def rowsum8(v):
    return jnp.sum(v.reshape(v.shape[0] // 8, 8, v.shape[1]), axis=0)


def bwd_kernel(tb, fc, kb,
    seg, dp, lse, s12, qkv_h, c_h, z1_h, gp_h, z2_h, wqkv_h, wat_h, g1, win_h, wout_h, g2,
    vec_o, dx_h, dxb_h, db2_h, du_h, db1_h, dqkv_h,
    dyr, wqkv, wat, win, wout, qkv, c_s, z1, gp, z2, bias, dy_s, dr1, dc, delta, du, db2, db1, dqkv, dx, dxb, vacc, bacc,
    insem, wsem, outsem, send_sem, recv_sem):
    sec = lax.axis_index("section")
    other = {"section": 1 - sec}
    M, T, D = c_s.shape
    FF = win.shape[1]
    nb = T // tb

    ws = [pltpu.make_async_copy(a, b, wsem.at[i]) for i, (a, b) in enumerate(
        ((wout_h, wout), (win_h, win), (wat_h, wat), (wqkv_h, wqkv)))]

    def in_copies(m):
        pairs = [(z2_h, z2), (gp_h, gp), (z1_h, z1), (c_h, c_s), (qkv_h, qkv)]
        return [pltpu.make_async_copy(a.at[m], b.at[m], insem.at[m, i]) for i, (a, b) in enumerate(pairs)]
    first = in_copies(0)
    first[0].start()
    ws[0].start()
    barrier = pltpu.get_barrier_semaphore()
    pl.semaphore_signal(barrier, inc=1, device_id=other, device_id_type=MESH)
    for a, b in zip(first[1:], ws[1:]):
        a.start()
        b.start()
    first[4].start()
    for m in range(1, M):
        for a in in_copies(m):
            a.start()
    vacc[...] = jnp.zeros_like(vacc)
    bacc[...] = jnp.zeros_like(bacc)
    pl.semaphore_wait(barrier, 1)

    lane = lax.broadcasted_iota(jnp.int32, (1, 128), 1)
    low_half = lane < HEAD_DIM
    indicator = jnp.where(lax.broadcasted_iota(jnp.int32, (16, D), 1) // HEAD_DIM == lax.broadcasted_iota(jnp.int32, (16, D), 0), 1.0, 0.0).astype(BF)

    def out_copies(m):
        pairs = [(db2, db2_h), (du, du_h), (db1, db1_h), (dqkv, dqkv_h), (dx, dx_h), (dxb, dxb_h)]
        return [pltpu.make_async_copy(a.at[m], b.at[m], outsem.at[m, i]) for i, (a, b) in enumerate(pairs)]

    def handoff(m, i):
        r = pl.ds(i * tb if isinstance(i, int) else pl.multiple_of(i * tb, tb), tb)
        return pltpu.make_async_remote_copy(src_ref=dxb.at[m, r], dst_ref=dyr.at[m, r], send_sem=send_sem.at[m, i],
            recv_sem=recv_sem.at[m, i], device_id=other, device_id_type=MESH)

    def norm_pull(z, scale, gain, dy):
        g = dy * gain
        return scale * (g - jnp.mean(g, axis=-1, keepdims=True) - z * jnp.mean(g * z, axis=-1, keepdims=True))

    def micro_step(m, _):
        ins = in_copies(m)
        outs = out_copies(m)
        mem = members(seg[pl.ds(m, 1), :])
        bias[...] = (dot_tn(mem, mem) - 1.0) * MASK_FILL
        dp3 = jnp.concatenate(split3(dp[m]), axis=0)

        @pl.when(sec == 0)
        def _():
            for i in range(nb):
                handoff(m, i).wait_recv()

        @pl.when(m == 0)
        def _():
            ws[0].wait()
            ws[1].wait()
            ws[2].wait()
        for a in ins[:4]:
            a.wait()

        def tok_step(i, _):
            r = pl.ds(pl.multiple_of(i * tb, tb), tb)

            @pl.when(sec == 0)
            def _():
                dy_s[...] = dyr[m, r, :].astype(F32)

            @pl.when(sec != 0)
            def _():
                blk = members(seg[pl.ds(m, 1), r])
                dy_s[...] = dot_tn(jnp.concatenate([blk, blk, blk], axis=0), dp3)
            dy = dy_s[...]
            z = z2[m, r, :].astype(F32)
            dr2 = norm_pull(z, s12[m, r, 1:2], g2[...].astype(F32), dy)
            vacc[0] += rowsum8(dy * z)
            vacc[1] += rowsum8(dy)
            d2 = dr2.astype(BF)
            db2[m, r, :] = d2
            vacc[2] += rowsum8(d2.astype(F32))
            dh = dr2
            nj = FF // fc
            dfs = [dot_nt(d2, wout[:fc, :])]
            for j in range(nj):
                cols = slice(j * fc, (j + 1) * fc)
                if j + 1 < nj:
                    dfs.append(dot_nt(d2, wout[(j + 1) * fc:(j + 2) * fc, :]))
                dub = (dfs[j] * gp[m, r, cols].astype(F32)).astype(BF)
                du[m, r, cols] = dub
                bacc[:, cols] += rowsum8(dub.astype(F32))
                dh = dh + dot_nt(dub, win[:, cols])
            z = z1[m, r, :].astype(F32)
            d1 = norm_pull(z, s12[m, r, 0:1], g1[...].astype(F32), dh)
            vacc[3] += rowsum8(dh * z)
            vacc[4] += rowsum8(dh)
            dr1[r, :] = d1
            d1 = d1.astype(BF)
            db1[m, r, :] = d1
            vacc[5] += rowsum8(d1.astype(F32))
            dcb = dot_nt(d1, wat[...]).astype(BF)
            dc[r, :] = dcb
            prod = dcb.astype(F32) * c_s[m, r, :].astype(F32)
            hi = prod.astype(BF)
            low = (prod - hi.astype(F32)).astype(BF)
            delta[:, r] = dot_nt(indicator, hi) + dot_nt(indicator, low)
            return 0
        lax.fori_loop(0, nb, tok_step, 0)
        for o in outs[:3]:
            o.start()
        ins[4].wait()

        def att_step(p, _):
            cols = pl.ds(pl.multiple_of(p * 128, 128), 128)
            kcols = pl.ds(pl.multiple_of(p * 128 + D, 128), 128)
            vcols = pl.ds(pl.multiple_of(p * 128 + 2 * D, 128), 128)
            q2 = qkv[m, :, cols] * (HEAD_DIM ** -0.5)
            dc2 = dc[:, cols]
            dqt = jnp.zeros((128, T), F32)
            for i in range(T // kb):
                rows = slice(i * kb, (i + 1) * kb)
                k2 = qkv[m, rows, kcols]
                v2 = qkv[m, rows, vcols]
                dks, dvs = [], []
                for h in range(2):
                    pick = low_half if h == 0 else jnp.logical_not(low_half)
                    kh = jnp.where(pick, k2, 0)
                    vh = jnp.where(pick, v2, 0)
                    st = dot_nt(kh, q2) + bias[rows, :]
                    pt = jnp.exp(st - lse[m, pl.ds(2 * p + h, 1), :])
                    dpt = dot_nt(vh, dc2)
                    da = (pt * (dpt - delta[pl.ds(2 * p + h, 1), :])).astype(BF)
                    dvs.append(dot(pt.astype(BF), dc2))
                    dks.append(dot(da, q2))
                    dqt = dqt + dot_tn(kh, da)
                dqkv[m, rows, kcols] = jnp.where(low_half, dks[0], dks[1]).astype(BF)
                dqkv[m, rows, vcols] = jnp.where(low_half, dvs[0], dvs[1]).astype(BF)
            dqkv[m, :, cols] = (jnp.transpose(dqt) * (HEAD_DIM ** -0.5)).astype(BF)
            return 0
        lax.fori_loop(0, HEADS // 2, att_step, 0)
        outs[3].start()

        @pl.when(m == 0)
        def _():
            ws[3].wait()

        def dx_step(i, _):
            r = pl.ds(pl.multiple_of(i * tb, tb), tb)
            v = dr1[r, :] + dot_nt(dqkv[m, r, :], wqkv[...])
            dx[m, r, :] = v
            dxb[m, r, :] = v.astype(BF)
            vacc[6] += rowsum8(dqkv[m, r, :D].astype(F32))
            vacc[7] += rowsum8(dqkv[m, r, 2 * D:].astype(F32))

            @pl.when(sec != 0)
            def _():
                handoff(m, i).start()
            return 0
        lax.fori_loop(0, nb, dx_step, 0)
        outs[4].start()
        outs[5].start()
        return 0
    lax.fori_loop(0, M, micro_step, 0)
    vec_o[...] = jnp.concatenate([jnp.sum(vacc[...], axis=1)]
        + [jnp.sum(bacc[:, j * D:(j + 1) * D], axis=0, keepdims=True) for j in range(FF // D)] + [jnp.zeros((4, D), F32)], axis=0)
    for m in range(M):
        for o in out_copies(m):
            o.wait()

    @pl.when(sec != 0)
    def _():
        for m in range(M):
            for i in range(nb):
                handoff(m, i).wait_send()


def stack_bwd(seg, dp, stash, weights, tb=256, fc=768, kb=256):
    qkv, lse, c, z1, s12, gp, z2 = stash
    wqkv, bq, bv, wat, bat, g1, b1, win, bin_, wout, bout, g2, b2 = weights
    M, T, D = c.shape
    FF = win.shape[1]
    sds = jax.ShapeDtypeStruct
    out_shape = (sds((16, D), F32), sds((M, T, D), F32), sds((M, T, D), BF), sds((M, T, D), BF), sds((M, T, FF), BF), sds((M, T, D), BF), sds((M, T, 3 * D), BF))
    out_specs = (VM, ANY, ANY, ANY, ANY, ANY, ANY)
    V = pltpu.VMEM
    S = pltpu.SemaphoreType.DMA
    nb = T // tb
    scratch = [V((M, T, D), BF), V((D, 3 * D), BF), V((D, D), BF), V((D, FF), BF), V((FF, D), BF),
        V((M, T, 3 * D), BF), V((M, T, D), BF), V((M, T, D), BF), V((M, T, FF), BF), V((M, T, D), BF),
        V((T, T), F32), V((tb, D), F32), V((T, D), F32), V((T, D), BF), V((16, T), F32),
        V((M, T, FF), BF), V((M, T, D), BF), V((M, T, D), BF), V((M, T, 3 * D), BF), V((M, T, D), F32), V((M, T, D), BF),
        V((8, 8, D), F32), V((8, FF), F32), S((M, 5)), S((4,)), S((M, 6)), S((M, nb)), S((M, nb))]
    in_specs = (VM, VM, VM, VM, ANY, ANY, ANY, ANY, ANY, ANY, ANY, VM, ANY, ANY, VM)
    return pl.pallas_call(functools.partial(bwd_kernel, tb, fc, kb), out_shape=out_shape, in_specs=in_specs, out_specs=out_specs,
        scratch_shapes=scratch, compiler_params=pltpu.CompilerParams(vmem_limit_bytes=VMEM_LIMIT, collective_id=1, has_side_effects=True),
        name="stack_bwd")(seg, dp, lse, s12, qkv, c, z1, gp, z2, wqkv, wat, g1, win, wout, g2)


AFTER_TOKENS = ("", " ".join(("a2 a3 b0",)))
AFTER_W = ("", " ".join(("a4 b1",)), " ".join(("a5",)), " ".join(("a6 b2 c0",)))
AFTER_A = " ".join(("b3",))
AFTER_PAIR = (" ".join(("a7 c1",)), "", "", " ".join(("b4",)), " ".join(("a8",)), "")
BEFORE_Q = " ".join(("c2 b5",))
AFTER_Q = ("", " ".join(("v0 a9 c3 c4", "b6",)), "")
AT_THE_END = " ".join(("v1 a10 b8 b7", "c5 a11 d4 b9", "d3 c6 c8 b10", "c7 v2 d5 b11", "c9 v3 b12 d8", "d6 c10 d7 c11", "d9 c12 d10 d11", "d12",))


def back_kernel(tb, xb, kb,
    seg, pool, pairs, msgs0, lse, s12, z2_h, gp_h, z1_h, c_h, qkv_h, hb_h, x_h, act_h, wout_h, win_h, wat_h, wqkv_h, g1, g2,
    vec_o, pooled_o, loss_o, g_qkv, g_at, g_in, g_out, dx_o, dxr_o,
    dyx, wqkv, wat, win, wout, qkv, c_s, z1, gp, z2, dr, dc, delta, db2, db1, vacc, bacc,
    msgs, dps, loss_w, dn_s, pooled_s, loss_s, pooled_r, loss_r, kcode, qcode, gathered, rhs, part, got_a, got_b, got_c, got_d, got_t, va, vb,
    insem, wsem, latesem, outsem, send_sem, recv_sem, msg_send, msg_recv, pool_sem, dx_sem,
    send_a, recv_a, send_b, recv_b, send_c, recv_c, send_d, recv_d):
    sec = lax.axis_index("section")
    me = lax.axis_index("dp")
    peers = msgs.shape[0]
    core = lax.rem(me, 2)
    y = lax.rem(lax.div(me, 2), 2)
    z = lax.div(me, 4)
    zlow = lax.rem(z, 2)
    zhigh = lax.div(z, 2)
    other = {"section": 1 - sec}
    sibling = {"dp": me + 1 - 2 * core}
    across = {"dp": me + 2 - 4 * y}
    near = {"dp": me + 4 - 8 * zlow}
    far = {"dp": me + 8 - 16 * zhigh}

    def remote(src, dst, ss, rs, target):
        return pltpu.make_async_remote_copy(src_ref=src, dst_ref=dst, send_sem=ss, recv_sem=rs, device_id=target, device_id_type=MESH)
    M, T, D = c_s.shape
    N = M * T
    FF = gp.shape[2]
    half = D // 2
    nb = T // tb
    nx = T // xb
    nj = FF // D
    chunks = got_a.shape[0]
    rows = got_a.shape[4]
    SL = 8
    zchunk = 2 * nj
    cut = rows // 48 * 32

    wcp = [pltpu.make_async_copy(a, b, wsem.at[i]) for i, (a, b) in enumerate(
        ((wout_h, wout), (win_h, win), (wat_h, wat), (wqkv_h, wqkv)))]

    def norm_copies(m):
        return [pltpu.make_async_copy(a.at[m], b, insem.at[m, i]) for i, (a, b) in enumerate(((z2_h, z2), (z1_h, z1)))]

    def in_copies(m):
        return [pltpu.make_async_copy(a.at[m], b.at[m], insem.at[m, 2 + i]) for i, (a, b) in enumerate(((gp_h, gp), (c_h, c_s), (qkv_h, qkv)))]

    def act_copy(t):
        return pltpu.make_async_copy(act_h.at[t], rhs.at[t % 2 if isinstance(t, int) else lax.rem(t, 2)], latesem.at[t])
    hb_copy = pltpu.make_async_copy(hb_h, rhs.at[0], latesem.at[nj])
    x_copy = pltpu.make_async_copy(x_h, rhs.at[1], latesem.at[nj + 1])
    norms = norm_copies(0)
    ins = in_copies(0)
    norms[0].start()
    wcp[0].start()
    barrier = pltpu.get_barrier_semaphore()
    pl.semaphore_signal(barrier, inc=1, device_id=other, device_id_type=MESH)
    for d in range(1, peers):
        pl.semaphore_signal(barrier, inc=1, device_id={"dp": lax.rem(me + d, peers)}, device_id_type=MESH)
    for a in [ins[0], wcp[1], norms[1], wcp[2], ins[1]]:
        a.start()
    vacc[...] = jnp.zeros_like(vacc)
    bacc[...] = jnp.zeros_like(bacc)

    def msg_copy(d):
        return remote(msgs.at[me], msgs.at[me], msg_send.at[d - 1], msg_recv.at[d - 1], {"dp": lax.rem(me + d, peers)})
    pool_copy = remote(pooled_s, pooled_r, pool_sem.at[0], pool_sem.at[1], other)
    loss_copy = remote(loss_s, loss_r, pool_sem.at[2], pool_sem.at[3], other)
    def head(m):
        eight = pl.ds(pl.multiple_of(m * SL, SL), SL)
        pooled, radius, counts = documents(members(seg[m]), pool[m])
        G = peers * SL
        lo = gathered[:, :SL, :half].astype(F32).reshape(G, half).astype(BF)
        hi = gathered[:, SL:, :half].astype(F32).reshape(G, half).astype(BF)
        partner = gathered[:, :SL, half:].astype(F32).reshape(G, 128)
        rid = lax.broadcasted_iota(jnp.int32, (G, G), 0)
        cid = lax.broadcasted_iota(jnp.int32, (G, G), 1)
        held = jnp.logical_and(lax.rem(rid, SL) < SEGS, lax.rem(cid, SL) < SEGS)
        logits = TEMPER * (dot_nt(lo, lo) + dot_nt(hi, hi))
        logits = jnp.where(jnp.logical_and(held, rid != cid), logits, -MASK_FILL)
        peak = jnp.max(logits, axis=-1, keepdims=True)
        exponent = jnp.exp(logits - peak)
        denom = jnp.sum(exponent, axis=-1, keepdims=True)
        doc = (lax.div(cid, SL) * SEGS + lax.rem(cid, SL)).astype(F32)
        target = jnp.where(jnp.logical_and(held, doc == partner[:, :1]), 1.0, 0.0)
        loss = peak + jnp.log(denom) - jnp.sum(target * logits, axis=-1, keepdims=True)
        dl = jnp.where(held, exponent / denom - target, 0.0).astype(BF)
        own = pl.ds(pl.multiple_of(me * SL, SL), SL)
        for side, part_of in ((0, lo), (1, hi)):
            dn_s[:, side * half:(side + 1) * half] = TEMPER * (dot(dl, part_of) + dot_tn(dl, part_of))
        dn = dn_s[own, :]
        loss_w[...] = jnp.broadcast_to(loss, (G, 128))
        loss_s[eight, :] = loss_w[own, :]
        dps[eight, :] = (radius * dn - radius * radius * radius * jnp.sum(pooled * dn, axis=-1, keepdims=True) * pooled) / counts

    lane = lax.broadcasted_iota(jnp.int32, (1, 128), 1)
    low_half = lane < HEAD_DIM
    indicator = jnp.where(lax.broadcasted_iota(jnp.int32, (16, D), 1) // HEAD_DIM == lax.broadcasted_iota(jnp.int32, (16, D), 0), 1.0, 0.0).astype(BF)

    def out_copy(m):
        return pltpu.make_async_copy(dyx.at[m], dx_o.at[m], outsem.at[m])

    def handoff(m, i):
        r = pl.ds(i * xb if isinstance(i, int) else pl.multiple_of(i * xb, xb), xb)
        return remote(dyx.at[m, r], dyx.at[m, r], send_sem.at[m, i], recv_sem.at[m, i], other)

    def dx_copy(m):
        return remote(dyx.at[m, :, half:], dxr_o.at[m], dx_sem.at[m, 0], dx_sem.at[m, 1], other)

    def norm_pull(zz, scale, gain, dy):
        g = dy * gain
        return scale * (g - jnp.mean(g, axis=-1, keepdims=True) - zz * jnp.mean(g * zz, axis=-1, keepdims=True))

    def base(k):
        return min(k, chunks - 1)

    def span(k):
        return pl.ds(0, cut) if k == chunks - 1 else pl.ds(cut, rows - cut) if k == chunks else pl.ds(0, rows)

    def slot(k):
        return k % 2 if isinstance(k, int) else lax.rem(k, 2)

    def copy_a(k):
        return remote(part.at[slot(k), :, :, :, 1 - core], got_a.at[k], send_a.at[k], recv_a.at[k], sibling)

    def copy_b(k):
        if not isinstance(k, int) or k != zchunk:
            if isinstance(k, int) and k >= nj:
                return remote(got_a.at[base(k), :, :, 1 - y, span(k)], got_b.at[base(k), :, :, span(k)], send_b.at[k], recv_b.at[k], across)
            return remote(got_a.at[k, :, :, 1 - y], got_b.at[k], send_b.at[k], recv_b.at[k], across)
        return remote(got_a.at[k, zhigh, zlow, 1 - y], got_d.at[k], send_b.at[k], recv_b.at[k], across)

    def copy_c(k):
        if k < nj:
            return remote(got_b.at[k], got_c.at[pl.ds(2 * (k // 2), 2)], send_c.at[k], recv_c.at[k], near)
        if k == zchunk:
            return remote(got_a.at[k, :, 1 - zlow], got_b.at[k], send_c.at[k], recv_c.at[k], near)
        return remote(got_b.at[base(k), :, 1 - zlow, span(k)], got_c.at[base(k), :, span(k)], send_c.at[k], recv_c.at[k], near)

    def copy_d(k):
        if not isinstance(k, int) or k < nj:
            return remote(got_b.at[k], got_t, send_d.at[k], recv_d.at[k], far)
        if k == zchunk:
            return remote(got_a.at[k, 1 - zhigh, zlow], got_c.at[k], send_d.at[k], recv_d.at[k], far)
        return remote(got_b.at[base(k), 1 - zhigh, zlow, span(k)], got_d.at[base(k), span(k)], send_d.at[k], recv_d.at[k], far)

    def e1(k):
        copy_a(k).wait_recv()

        for h in range(2):
            got_a[k, h] = got_a[k, h] + part[slot(k), h, :, :, core]
        if isinstance(k, int) and k == zchunk:
            copy_c(k).start()
        else:
            copy_b(k).start()
            if isinstance(k, int) and k == chunks - 1:
                copy_b(chunks).start()
        copy_a(k).wait_send()

    def e2(k):
        if k == zchunk:
            copy_c(k).wait_recv()
            for h in range(2):
                got_a[k, h, zlow] = got_a[k, h, zlow] + got_b[k, h]
            copy_d(k).start()
            return
        copy_b(k).wait_recv()
        for h in range(2):
            if k < nj:
                got_b[k, h] = got_b[k, h] + got_a[k, h, :, y]
            else:
                got_b[base(k), h, :, span(k)] = got_b[base(k), h, :, span(k)] + got_a[base(k), h, :, y, span(k)]
        if k < nj:
            @pl.when(zlow != k % 2)
            def _():
                copy_c(k).start()
        else:
            copy_c(k).start()

    def e3(k):
        if k < nj:
            @pl.when(zlow == k % 2)
            def _():
                copy_c(k).wait_recv()
                for h in range(2):
                    got_b[k, h] = got_b[k, h] + got_c[2 * (k // 2) + h]

                @pl.when(z != k)
                def _():
                    copy_d(k).start()
        elif k == zchunk:
            copy_d(k).wait_recv()
            got_a[k, zhigh, zlow] = got_a[k, zhigh, zlow] + got_c[k]
            copy_b(k).start()
        else:
            copy_c(k).wait_recv()
            for h in range(2):
                got_b[base(k), h, zlow, span(k)] = got_b[base(k), h, zlow, span(k)] + got_c[base(k), h, span(k)]
            copy_d(k).start()

    def e4(k):
        if k == zchunk:
            copy_b(k).wait_recv()
            return got_a[k, zhigh, zlow, y].astype(F32) + got_d[k].astype(F32)
        copy_d(k).wait_recv()
        return got_b[base(k), zhigh, zlow, span(k)].astype(F32) + got_d[base(k), span(k)].astype(F32)

    def tile_out(k, lhs, right):
        def side(i, _):
            cols = pl.ds(pl.multiple_of(i * half, half), half)
            v = dot_tn(lhs[:, cols], right)
            part[slot(k), i] = v.astype(BF).reshape(part.shape[2:])
            return 0
        lax.fori_loop(0, 2, side, 0)
        copy_a(k).start()

    def products_t():
        def one(t, _):
            act_copy(t).wait()

            def side(i, _):
                cols = pl.ds(pl.multiple_of(i * half, half), half)
                v = dot_tn(rhs[lax.rem(t, 2), :, cols], db2[...].reshape(N, D)).astype(BF)
                for c in range(2):
                    for s in range(4):
                        part[slot(t), s // 2, s % 2, i, c] = v[(c * 4 + s) * rows:(c * 4 + s + 1) * rows]
                return 0
            lax.fori_loop(0, 2, side, 0)
            copy_a(t).start()

            @pl.when(t < nj - 2)
            def _():
                act_copy(t + 2).start()

            @pl.when(t == nj - 2)
            def _():
                hb_copy.start()

            @pl.when(t == nj - 1)
            def _():
                x_copy.start()

            @pl.when(jnp.logical_and(t >= 1, t <= 2))
            def _():
                e1(t - 1)
            return 0
        lax.fori_loop(0, nj, one, 0)

    def products_w():
        hb_copy.wait()

        def one(j, _):
            tile_out(nj + j, rhs.at[0], gp[:, :, pl.ds(pl.multiple_of(j * D, D), D)].reshape(N, D))
            for n, steps in enumerate(AFTER_W):
                if steps:
                    run_when(j == n, steps)
            return 0
        lax.fori_loop(0, nj, one, 0)

        def side(i, _):
            cols = pl.ds(pl.multiple_of(i * half, half), half)
            v = dot_tn(c_s[:, :, cols].reshape(N, half), db1[...].reshape(N, D))
            part[slot(2 * nj), i] = v.astype(BF).reshape(part.shape[2:])
            return 0
        lax.fori_loop(0, 2, side, 0)
        copy_a(2 * nj).start()
        for step in AFTER_A.split():
            run(step)

    def products_q():
        x_copy.wait()

        def one(j, _):
            tile_out(2 * nj + 1 + j, rhs.at[1], qkv[:, :, pl.ds(pl.multiple_of(j * D, D), D)].reshape(N, D))
            for n, steps in enumerate(AFTER_Q):
                if steps:
                    run_when(j == n, steps)
            return 0
        lax.fori_loop(0, 3, one, 0)

    def store(k):
        v = e4(k)
        if k < 2 * nj:
            g_in[:, (k - nj) * D:(k - nj + 1) * D] = v
        elif k == 2 * nj:
            g_at[...] = v
        else:
            g_qkv[span(k), (base(k) - 2 * nj - 1) * D:(base(k) - 2 * nj) * D] = v

    def store_w_out():
        copy_d(z).wait_recv()
        for s in range(4):
            g_out[s * rows:(s + 1) * rows, :] = got_b[z, s // 2, s % 2].astype(F32) + got_t[s // 2, s % 2].astype(F32)

    def run(step):
        what, k = step[0], int(step[1:])
        if what == "v":
            vec_step(k)
        elif what == "d":
            if k >= nj:
                store(k)
            elif k == nj - 1:
                store_w_out()
        else:
            {"a": e1, "b": e2, "c": e3}[what](k)

    def run_when(where, steps):
        @pl.when(where)
        def _():
            for step in steps.split():
                run(step)

    def one_pass(step, _):
        m = jnp.minimum(step, M - 1)
        norms = norm_copies(m)
        ins = in_copies(m)
        forming = jnp.logical_or(jnp.logical_and(step == M - 1, sec == 0), jnp.logical_and(step == M, sec != 0))
        behind = jnp.logical_and(step == M, sec != 0)

        @pl.when(step < M)
        def _():
            norm_pass(m, norms)

        @pl.when(forming)
        def _():
            products_t()

        @pl.when(step < M)
        def _():
            token_pass(m, norms, ins)

        @pl.when(forming)
        def _():
            run_when(behind, " ".join(AFTER_TOKENS))
            products_w()
            run_when(behind, " ".join(AFTER_PAIR))

        @pl.when(step < M)
        def _():
            attention_pass(m)
        return 0

    def norm_pass(m, norms):
        norms = norm_copies(m)
        ins = in_copies(m)
        mem = members(seg[m])
        kcode[...], qcode[...] = codes(mem)
        norms[0].wait()

        @pl.when(sec != 0)
        def _():
            @pl.when(m == 0)
            def _():
                gathered[...] = msgs0[...]

            @pl.when(m == 1)
            def _():
                for d in range(1, peers):
                    msg_copy(d).wait()
                gathered[...] = msgs[...]
            head(m)

        def norm_rows(r):
            dy = dr[r, :]
            zz = z2[r, :].astype(F32)
            dr2 = norm_pull(zz, s12[m, r, 1:2], g2[...].astype(F32), dy)
            vacc[0] += rowsum8(dy * zz)
            vacc[1] += rowsum8(dy)
            d2 = dr2.astype(BF)
            dr[r, :] = dr2
            db2[m, r, :] = d2
            vacc[2] += rowsum8(d2.astype(F32))

        @pl.when(sec == 0)
        def _():
            def norm_step(i, _):
                r = pl.ds(pl.multiple_of(i * xb, xb), xb)
                handoff(m, i).wait_recv()
                dr[r, :] = dyx[m, r, :].astype(F32)
                norm_rows(r)
                return 0
            lax.fori_loop(0, nx, norm_step, 0)

        @pl.when(sec != 0)
        def _():
            dp3 = jnp.concatenate(split3(jnp.concatenate([dps[pl.ds(pl.multiple_of(m * SL, SL), SL), :], jnp.zeros((16 - SL, D), F32)], axis=0)), axis=0)
            dr[...] = dot_tn(jnp.concatenate([mem, mem, mem], axis=0), dp3)
            for i in range(nb):
                norm_rows(slice(i * tb, (i + 1) * tb))

        @pl.when(m == 0)
        def _():
            pl.semaphore_wait(barrier, peers)

            @pl.when(sec != 0)
            def _():
                for m in range(M):
                    pooled, radius, _ = documents(members(seg[m]), pool[m])
                    pooled_s[m * SL:(m + 1) * SL, :] = pooled
                    if m == 1:
                        msgs[me] = message(pooled * radius, pairs[m:m + 1, :])
                for d in range(1, peers):
                    msg_copy(d).start()
                pool_copy.start()

    def token_pass(m, norms, ins):
        @pl.when(jnp.logical_and(m == M - 1, sec != 0))
        def _():
            loss_copy.start()

        @pl.when(m == 0)
        def _():
            for w in wcp[:3]:
                w.wait()
            in_copies(0)[2].start()
            wcp[3].start()
            for n in range(1, M):
                for a in in_copies(n):
                    a.start()
            act_copy(0).start()
            act_copy(1).start()
        norms[1].wait()
        ins[0].wait()
        ins[1].wait()
        for i in range(nb):
            r = slice(i * tb, (i + 1) * tb)
            d2 = db2[m, r, :]
            dh = dr[r, :]
            dfs = [dot_nt(d2, wout[:D, :])]
            for j in range(nj):
                cols = slice(j * D, (j + 1) * D)
                if j + 1 < nj:
                    dfs.append(dot_nt(d2, wout[(j + 1) * D:(j + 2) * D, :]))
                dub = (dfs[j] * gp[m, r, cols].astype(F32)).astype(BF)
                gp[m, r, cols] = dub
                bacc[:, cols] += rowsum8(dub.astype(F32))
                dh = dh + dot_nt(dub, win[:, cols])
            dr[r, :] = dh
            run_when(jnp.logical_and(m == M - 1, sec == 0), AFTER_TOKENS[i])
        for i in range(nb):
            r = slice(i * tb, (i + 1) * tb)
            dh = dr[r, :]
            zz = z1[r, :].astype(F32)
            d1 = norm_pull(zz, s12[m, r, 0:1], g1[...].astype(F32), dh)
            vacc[3] += rowsum8(dh * zz)
            vacc[4] += rowsum8(dh)
            dr[r, :] = d1
            d1 = d1.astype(BF)
            db1[m, r, :] = d1
            vacc[5] += rowsum8(d1.astype(F32))
            dcb = dot_nt(d1, wat[...]).astype(BF)
            dc[r, :] = dcb
            prod = dcb.astype(F32) * c_s[m, r, :].astype(F32)
            hi = prod.astype(BF)
            low = (prod - hi.astype(F32)).astype(BF)
            delta[:, r] = dot_nt(indicator, hi) + dot_nt(indicator, low)
        @pl.when(m < M - 1)
        def _():
            for cp in norm_copies(m + 1):
                cp.start()
        ins[2].wait()

    def attention_pass(m):
        for p in range(HEADS // 2):
            cols = slice(p * 128, (p + 1) * 128)
            kcols = slice(D + p * 128, D + (p + 1) * 128)
            vcols = slice(2 * D + p * 128, 2 * D + (p + 1) * 128)
            q2 = qkv[m, :, cols] * (HEAD_DIM ** -0.5)
            qh = [jnp.where(low_half, q2, qcode[...]), jnp.where(low_half, qcode[...], q2)]
            dc2 = dc[:, cols]
            dqt = jnp.zeros((128, T), F32)
            for i in range(T // kb):
                r = slice(i * kb, (i + 1) * kb)
                k2 = qkv[m, r, kcols]
                v2 = qkv[m, r, vcols]
                kc = kcode[r, :]
                dks, dvs = [], []
                for h in range(2):
                    pick = low_half if h == 0 else jnp.logical_not(low_half)
                    kh = jnp.where(low_half, k2, kc) if h == 0 else jnp.where(low_half, kc, k2)
                    pt = jnp.exp(dot_nt(kh, qh[h]) - lse[m, 2 * p + h:2 * p + h + 1, :])
                    dpt = dot_nt(jnp.where(pick, v2, 0), dc2)
                    da = (pt * (dpt - delta[2 * p + h:2 * p + h + 1, :])).astype(BF)
                    dvs.append(dot(pt.astype(BF), dc2))
                    dks.append(dot(da, q2))
                    dqt = dqt + dot_tn(jnp.where(pick, k2, 0), da)
                qkv[m, r, kcols] = jnp.where(low_half, dks[0], dks[1]).astype(BF)
                qkv[m, r, vcols] = jnp.where(low_half, dvs[0], dvs[1]).astype(BF)
            qkv[m, :, cols] = (jnp.transpose(dqt) * (HEAD_DIM ** -0.5)).astype(BF)
            if AFTER_PAIR[p]:
                run_when(jnp.logical_and(m == M - 1, sec == 0), AFTER_PAIR[p])
        @pl.when(m == 0)
        def _():
            wcp[3].wait()

        def dx_step(i, _):
            r = pl.ds(pl.multiple_of(i * xb, xb), xb)
            dyx[m, r, :] = (dr[r, :] + dot_nt(qkv[m, r, :], wqkv[...])).astype(BF)

            @pl.when(sec != 0)
            def _():
                handoff(m, i).start()
            vacc[6] += rowsum8(qkv[m, r, :D].astype(F32))
            vacc[7] += rowsum8(qkv[m, r, 2 * D:].astype(F32))
            return 0
        lax.fori_loop(0, nx, dx_step, 0)

        @pl.when(sec == 0)
        def _():
            out_copy(m).start()
            dx_copy(m).start()

    lax.fori_loop(0, M + 1, one_pass, 0)

    vec = [remote(va.at[i], vb.at[i], s.at[chunks + 1], r.at[chunks + 1], target) for i, (s, r, target) in enumerate(
        ((send_a, recv_a, sibling), (send_b, recv_b, across), (send_c, recv_c, near), (send_d, recv_d, far)))]

    def vec_step(i):
        vec[i].wait_recv()
        total = va[i] + vb[i]
        if i < 3:
            va[i + 1] = total
            vec[i + 1].start()
        else:
            vec_o[...] = total
    va[0] = jnp.concatenate([jnp.sum(vacc[...], axis=1)]
        + [jnp.sum(bacc[:, j * D:(j + 1) * D], axis=0, keepdims=True) for j in range(nj)] + [jnp.zeros((8 - nj, D), F32)], axis=0)
    vec[0].start()
    for step in BEFORE_Q.split():
        run(step)
    products_q()
    for step in AT_THE_END.split():
        run(step)

    @pl.when(sec == 0)
    def _():
        pool_copy.wait_recv()
        loss_copy.wait_recv()
        pooled_o[...] = pooled_r[:, :half]
        loss_o[...] = loss_r[...]
        for m in range(M):
            dx_copy(m).wait_send()
            out_copy(m).wait()

    @pl.when(sec != 0)
    def _():
        pool_copy.wait_send()
        loss_copy.wait_send()
        pooled_o[...] = pooled_s[:, half:]
        loss_o[...] = loss_s[...]
        for m in range(M):
            for i in range(nx):
                handoff(m, i).wait_send()
            dx_copy(m).wait_recv()
    for v in vec:
        v.wait_send()
    for k in range(chunks + 1):
        copy_b(k).wait_send()
        if k < nj:
            @pl.when(zlow != k % 2)
            def _():
                copy_c(k).wait_send()

            @pl.when(jnp.logical_and(zlow == k % 2, z != k))
            def _():
                copy_d(k).wait_send()
        else:
            copy_c(k).wait_send()
            copy_d(k).wait_send()


def stack_back(seg, pool, pairs, msgs0, stash, weights, tb=256, xb=256, kb=256):
    x, qkv, lse, c, z1, s12, hb, gp, act, z2 = stash
    wqkv, bq, bv, wat, bat, g1, b1, win, bin_, wout, bout, g2, b2 = weights
    M, T, D = c.shape
    N = M * T
    FF = win.shape[1]
    count = lax.axis_size("dp")
    rows = D // count
    chunks = (4 * D + 2 * FF) // D
    SL = 8
    sds = jax.ShapeDtypeStruct
    out_shape = (sds((16, D), F32), sds((M * SL, D // 2), F32), sds((M * SL, 128), F32), sds((rows, 3 * D), F32), sds((rows, D), F32), sds((rows, FF), F32),
        sds((FF // count, D), F32), sds((M, T, D), BF), sds((M, T, D // 2), BF))
    out_specs = (VM,) * 7 + (ANY, ANY)
    V = pltpu.VMEM
    S = pltpu.SemaphoreType.DMA
    nx = T // xb
    nj = FF // D
    piece = (rows, D)
    scratch = [V((M, T, D), BF), V((D, 3 * D), BF), V((D, D), BF), V((D, FF), BF), V((FF, D), BF),
        V((M, T, 3 * D), BF), V((M, T, D), BF), V((T, D), BF), V((M, T, FF), BF), V((T, D), BF),
        V((T, D), F32), V((T, D), BF), V((16, T), F32), V((M, T, D), BF), V((M, T, D), BF), V((8, 8, D), F32), V((8, FF), F32),
        V((count, 16, D // 2 + 128), BF), V((M * SL, D), F32), V((count * SL, 128), F32), V((count * SL, D), F32), V((M * SL, D), F32), V((M * SL, 128), F32), V((M * SL, D), F32), V((M * SL, 128), F32),
        V((T, 128), BF), V((T, 128), BF), V((count, 16, D // 2 + 128), BF), V((2, N, D), BF), V((2, 2, 2, 2, 2) + piece, BF), V((chunks, 2, 2, 2) + piece, BF), V((chunks, 2, 2) + piece, BF),
        V((chunks, 2) + piece, BF), V((chunks,) + piece, BF), V((2, 2) + piece, BF), V((4, 16, D), F32), V((4, 16, D), F32),
        S((M, 5)), S((4,)), S((2 + nj,)), S((M,)), S((M, nx)), S((M, nx)), S((count - 1,)), S((count - 1,)), S((4,)), S((M, 2))]
    scratch += [S((chunks + 2,)) for _ in range(8)]
    in_specs = (VM,) * 6 + (ANY,) * 12 + (VM, VM)
    return pl.pallas_call(functools.partial(back_kernel, tb, xb, kb), out_shape=out_shape, in_specs=in_specs, out_specs=out_specs,
        scratch_shapes=scratch, compiler_params=pltpu.CompilerParams(vmem_limit_bytes=62 * 2**20, collective_id=3, has_side_effects=True),
        name="stack_back")(seg, pool, pairs, msgs0, lse, s12, z2, gp, z1, c, qkv, hb.reshape(N, D), x.reshape(N, D), act,
            wout, win, wat, wqkv, g1, g2)


def finish_kernel(vec, pooled, loss, g_qkv, g_at, g_in, g_out, dx_h, dxr_h,
    pooled_o, loss_o, gx_o, qkv_o, at_o, in_o, out_o, *rest):
    small, buf, wide_buf, bufs, sem = rest[:9], rest[9], rest[10], rest[11:15], rest[15]
    came = [pltpu.make_async_copy(a, b, sem.at[1 + i]) for i, (a, b) in enumerate(zip((g_qkv, g_at, g_in, g_out), bufs))]
    goes = [pltpu.make_async_copy(b, a, sem.at[5 + i]) for i, (a, b) in enumerate(zip((qkv_o, at_o, in_o, out_o), bufs))]
    goes += [pltpu.make_async_copy(wide_buf, gx_o, sem.at[9])]
    sec = lax.axis_index("section")
    me = lax.axis_index("dp")
    half = buf.shape[2]

    @pl.when(sec == 0)
    def _():
        pltpu.make_async_copy(dx_h.at[:, :, pl.ds(0, half)], buf, sem.at[0]).start()

    @pl.when(sec != 0)
    def _():
        pltpu.make_async_copy(dxr_h, buf, sem.at[0]).start()
    for cp in came:
        cp.start()
    pltpu.make_async_copy(dxr_h, buf, sem.at[0]).wait()
    wide_buf[...] = buf[...].astype(F32)
    goes[4].start()
    for a, b in zip(came, goes):
        a.wait()
        b.start()
    SL = 8
    lane = lax.broadcasted_iota(jnp.int32, (SL, 128), 1) == lax.broadcasted_iota(jnp.int32, (SL, 128), 0)
    for m in range(pooled_o.shape[0]):
        pooled_o[m] = pooled[m * SL:m * SL + SEGS, :]
        loss_o[m:m + 1, :] = jnp.sum(jnp.where(lane, loss[m * SL:(m + 1) * SL, :], 0.0), axis=0, keepdims=True)[:, :SEGS]
    D = vec.shape[1]
    width, wide = small[0].shape[1], small[8].shape[1]
    parts = split3(vec[...])

    def columns(start, size):
        pick = lax.broadcasted_iota(jnp.int32, (D, size), 0) == lax.broadcasted_iota(jnp.int32, (D, size), 1) + start
        pick = jnp.where(pick, 1.0, 0.0).astype(BF)
        return (dot(parts[0], pick) + dot(parts[1], pick)) + dot(parts[2], pick)
    v = columns(me * width, 128)
    for i in range(8):
        small[i][...] = v[i:i + 1, :width]
    per = D // wide
    v = columns(lax.rem(me, per) * wide, 256)
    row = lax.broadcasted_iota(jnp.int32, (16, 256), 0) == 8 + lax.div(me, per)
    small[8][...] = jnp.sum(jnp.where(row, v, 0.0), axis=0, keepdims=True)[:, :wide]
    for cp in goes:
        cp.wait()


def finish(vec, pooled, loss, g_qkv, g_at, g_in, g_out, dx, dxr):
    M, T, D = dx.shape
    count = lax.axis_size("dp")
    sds = jax.ShapeDtypeStruct
    f = lambda a: sds(a.shape, F32)
    out_shape = (sds((M, SEGS, D // 2), F32), sds((M, SEGS), F32), sds((M, T, D // 2), F32), f(g_qkv), f(g_at), f(g_in), f(g_out)) + tuple(
        sds((1, D // count), F32) for _ in range(8)) + (sds((1, g_in.shape[1] // count), F32),)
    return pl.pallas_call(finish_kernel, out_shape=out_shape, in_specs=(VM,) * 3 + (ANY,) * 6, out_specs=(VM,) * 2 + (ANY,) * 5 + (VM,) * 9,
        scratch_shapes=[pltpu.VMEM((M, T, D // 2), BF), pltpu.VMEM((M, T, D // 2), F32)] + [pltpu.VMEM(g.shape, F32) for g in (g_qkv, g_at, g_in, g_out)]
        + [pltpu.SemaphoreType.DMA((10,))],
        compiler_params=pltpu.CompilerParams(vmem_limit_bytes=VMEM_LIMIT), name="finish")(vec, pooled, loss, g_qkv, g_at, g_in, g_out, dx, dxr)


def contrast_head(pool, seg, pairs, all_pairs):
    M, S = pairs.shape
    D = pool.shape[-1]
    counts = jnp.sum((seg[:, :, None] == jnp.arange(SEGS)).astype(F32), axis=1)[:, :, None]
    pooled = pool[:, :SEGS] / counts
    radius = lax.rsqrt(jnp.sum(pooled * pooled, axis=-1, keepdims=True) + UNIT_EPS)
    unit = (pooled * radius).astype(BF)
    every = lax.all_gather(unit, "dp", axis=1, tiled=True)
    total = every.shape[1]
    start = lax.axis_index("dp") * S
    logits = TEMPER * jnp.einsum("mgd,mkd->mgk", every, every, preferred_element_type=F32)
    cols = jnp.arange(total)
    logits = jnp.where(cols[:, None] == cols[None, :], -MASK_FILL, logits)
    peak = jnp.max(logits, axis=-1, keepdims=True)
    exponent = jnp.exp(logits - peak)
    denom = jnp.sum(exponent, axis=-1, keepdims=True)
    target = cols[None, None, :] == all_pairs[:, :, None]
    loss = peak[..., 0] + jnp.log(denom[..., 0]) - jnp.sum(jnp.where(target, logits, 0.0), axis=-1)
    dl = (exponent / denom - target.astype(F32)).astype(BF)
    rows = lax.dynamic_slice_in_dim(dl, start, S, 1)
    columns = lax.dynamic_slice_in_dim(dl, start, S, 2)
    dn = TEMPER * (jnp.einsum("mgk,mkd->mgd", rows, every, preferred_element_type=F32)
        + jnp.einsum("mkg,mkd->mgd", columns, every, preferred_element_type=F32))
    dp = radius * dn - radius * radius * radius * jnp.sum(pooled * dn, axis=-1, keepdims=True) * pooled
    loss = lax.dynamic_slice_in_dim(loss, start, S, 1)
    return pooled, loss, jnp.pad(dp / counts, ((0, 0), (0, 16 - SEGS), (0, 0)))


def scattered(grads):
    count = lax.axis_size("dp")
    packed = jnp.concatenate([g.reshape(count, -1) for g in grads], axis=1)
    part = lax.psum_scatter(packed, "dp", scatter_dimension=0, tiled=True)[0].astype(F32)
    outs, at = [], 0
    for g in grads:
        size = g.size // count
        outs.append(part[at:at + size].reshape((1, g.shape[0] // count) + g.shape[1:]))
        at += size
    return outs


def swapped(value):
    return lax.ppermute(value, "section", [(0, 1), (1, 0)])


def local(hidden_in, seg_ids, pair_ids, w_qkv, b_query, b_value, w_attn_out, b_attn_out, ln1_gain, ln1_bias, w_in, b_in, w_out, b_out, ln2_gain, ln2_bias):
    M, _, T, D = hidden_in.shape
    sec = lax.axis_index("section")
    first = sec == 0
    weights = (w_qkv[0], b_query, b_value, w_attn_out[0], b_attn_out, ln1_gain, ln1_bias, w_in[0], b_in, w_out[0], b_out, ln2_gain, ln2_bias)
    half = D // 2
    count = lax.axis_size("dp")
    pool, x, qkv, lse, c, z1, s12, hb, gp, act, z2, msgs = stack_fwd(hidden_in[:, 0], seg_ids, pair_ids, weights, count if count == 16 else 0)
    if count == 16:
        parts = stack_back(seg_ids, pool, pair_ids, msgs, (x, qkv, lse, c, z1, s12, hb, gp, act, z2), weights)
        pooled, loss, grad_input, g_qkv, g_at, g_in, g_out, gg2, gb2, gbo, gg1, gb1, gba, gbq, gbv, gbi = finish(*parts)
        pooled_out, loss_out = pooled, loss
        g_qkv, g_at, g_in, g_out = (g[None] for g in (g_qkv, g_at, g_in, g_out))
    else:
        seg = seg_ids[:, 0]
        all_pairs = lax.all_gather(pair_ids, "dp", axis=1, tiled=True)
        pooled, loss, dp = contrast_head(pool, seg, pair_ids, all_pairs)
        vec, dx, dxb, db2, du, db1, dqkv = stack_bwd(seg, dp, (qkv, lse, c, z1, s12, gp, z2), weights)
        act = jnp.moveaxis(act, 0, 1).reshape(M, T, -1)
        big = [jnp.einsum("mta,mtb->ab", a, b, preferred_element_type=F32).astype(BF) for a, b in ((x, dqkv), (c, db1), (hb, du), (act, db2))]
        g_qkv, g_at, g_in, g_out = scattered(big)
        small = scattered([vec[i] for i in range(8)] + [vec[8:8 + w_in.shape[2] // D].reshape(-1)])
        gg2, gb2, gbo, gg1, gb1, gba, gbq, gbv, gbi = small
        kept = lax.dynamic_slice_in_dim(dx, sec * half, half, 2)
        sent = lax.dynamic_slice_in_dim(dxb, (1 - sec) * half, half, 2)
        grad_input = jnp.where(first, kept, swapped(sent).astype(F32))
        pooled_kept = lax.dynamic_slice_in_dim(pooled, sec * half, half, 2)
        pooled_sent = lax.dynamic_slice_in_dim(pooled, (1 - sec) * half, half, 2).astype(BF)
        pooled_out = jnp.where(first, swapped(pooled_sent).astype(F32), pooled_kept)
        loss_out = jnp.where(first, swapped(loss.astype(BF)).astype(F32), loss)
    return (pooled_out, loss_out, grad_input[:, None], g_qkv, gbq, gbv, g_at, gba, gg1, gb1, g_in, gbi, g_out, gbo, gg2, gb2)


def solution(mesh):
    in_specs = (
        P(None, "dp", None, None),
        P(None, "dp", None),
        P(None, "dp"),
        P("section", None, None),
        P("section", None),
        P("section", None),
        P("section", None, None),
        P("section", None),
        P("section", None),
        P("section", None),
        P("section", None, None),
        P("section", None),
        P("section", None, None),
        P("section", None),
        P("section", None),
        P("section", None),
    )
    out_specs = (
        P(None, "dp", "section"),
        P(None, "dp"),
        P(None, "dp", None, "section"),
        P("section", "dp", None),
        P("section", "dp"),
        P("section", "dp"),
        P("section", "dp", None),
        P("section", "dp"),
        P("section", "dp"),
        P("section", "dp"),
        P("section", "dp", None),
        P("section", "dp"),
        P("section", "dp", None),
        P("section", "dp"),
        P("section", "dp"),
        P("section", "dp"),
    )
    return jax.shard_map(local, mesh=mesh, in_specs=in_specs, out_specs=out_specs, check_vma=False)
```
